32 devices in a mesh: shard: 2 (over y), ctx: 4 (over z), tensor: 4 (over x, core).
Axes of the slice: x: 2, y: 2, z: 4, core: 2. Of those that a mesh axis runs over, the one named last changes fastest.
Arguments:
- tokens: bfloat16 [4, 4096, 960], P('shard', 'ctx'), may hold values from -6 to 6
- gains: bfloat16 [2, 960], P(None, ('shard', 'ctx')), may hold values from 0.5 to 1.5
- qkv_weight: bfloat16 [960, 1600], P('tensor', ('shard', 'ctx')), may hold values from -0.1875 to 0.1875
- out_weight: bfloat16 [960, 960], P('tensor', ('shard', 'ctx')), may hold values from -6 to 6
- gate_weight: bfloat16 [960, 2560], P(('shard', 'ctx'), 'tensor'), may hold values from -0.1875 to 0.1875
- up_weight: bfloat16 [960, 2560], P(('shard', 'ctx'), 'tensor'), may hold values from -0.1875 to 0.1875
- down_weight: bfloat16 [2560, 960], P('tensor', ('shard', 'ctx')), may hold values from -0.125 to 0.125
- cotangent: float32 [4, 4096, 960], P('shard', 'ctx'), may hold values from -6 to 6
Outputs:
- block_out: bfloat16 [4, 4096, 960], P('shard', 'ctx')
- input_grad: float32 [4, 4096, 960], P('shard', 'ctx')
- gains_grad: float32 [2, 960], P(None, ('shard', 'ctx'))
- qkv_weight_grad: float32 [960, 1600], P('tensor', ('shard', 'ctx'))
- out_weight_grad: float32 [960, 960], P('tensor', ('shard', 'ctx'))
- gate_weight_grad: float32 [960, 2560], P(('shard', 'ctx'), 'tensor')
- up_weight_grad: float32 [960, 2560], P(('shard', 'ctx'), 'tensor')
- down_weight_grad: float32 [2560, 960], P('tensor', ('shard', 'ctx'))
The draws below stay inside these ranges and needn't reach their ends.
All inputs are finite; a program needn't handle non-finite values.
Results may differ from the reference program's by a relative error of at most 0.03.
Values may be sent and summed in bfloat16 or wider, within the bound.
No kernel may reach another device: no remote copies, remote signals or barrier semaphores. Data moves between devices by JAX's collectives and lax.ppermute only.
A program may use at most 192 MiB of HBM per device.

```python
import jax
import jax.numpy as jnp
from jax import lax

D = 960
HEADS = 15
KV_HEADS = 5
HEAD_DIM = 64
FF = 2560
LEN = 4096
QKV = 1600
GROUP = 3
SEQS = 4


def level_of(stream_key, dims, split, smallest, high):
    gain = 1.0
    for axis_at, shards_of in split:
        draws = jax.random.uniform(jax.random.fold_in(jax.random.fold_in(stream_key, 6), axis_at), (shards_of,), jnp.float32, smallest / len(split), high / len(split))
        gain = gain * jnp.repeat(jnp.exp(draws), dims[axis_at] // shards_of).reshape((-1,) + (1,) * (len(dims) - 1 - axis_at))
    return gain


def noise(key, extent, spread, most, cuts=(), kind=jnp.bfloat16):
    drawn = spread * jax.random.normal(key, extent, jnp.float32)
    if cuts:
        drawn = drawn * level_of(key, extent, cuts, -0.22, 0.18)
    return jnp.clip(drawn, -most, most).astype(kind)


def setup_inputs(seed: int = 0) -> dict:
    arg_keys = jax.random.split(jax.random.key(seed), 9)
    return {
        "tokens": noise(arg_keys[0], (SEQS, LEN, D), 1.0, 6.0, ((0, 2), (1, 4))),
        "gains": jnp.clip(1.0 + 0.1 * jax.random.normal(arg_keys[1], (2, D), jnp.float32), 0.5, 1.5).astype(jnp.bfloat16),
        "qkv_weight": noise(arg_keys[2], (D, QKV), D ** -0.5, 0.1875, ((0, 4), (1, 8))),
        "out_weight": noise(arg_keys[3], (D, D), (max(D // LEN, 1)) ** -0.5, 6.0, ((0, 4), (1, 8))),
        "gate_weight": noise(arg_keys[4], (D, FF), D ** -0.5, 0.1875, ((0, 8), (1, 4))),
        "up_weight": noise(arg_keys[5], (D, FF), D ** -0.5, 0.1875, ((0, 8), (1, 4))),
        "down_weight": noise(arg_keys[6], (FF, D), FF ** -0.5, 0.125, ((0, 4), (1, 8))),
        "cotangent": noise(arg_keys[7], (SEQS, LEN, D), 1.0, 6.0, ((0, 2), (1, 4)), jnp.float32),
    }


@jax.custom_vjp
def low(v):
    return lax.optimization_barrier(v.astype(jnp.bfloat16)).astype(jnp.float32)

@jax.custom_vjp
def low_back(v):
    return v

def low_keep(v):
    return (low(v), None)

def low_pass(kept, grad):
    return (grad,)

def back_keep(v):
    return (v, None)

def back_low(kept, grad):
    return (low(grad),)
low.defvjp(low_keep, low_pass)
low_back.defvjp(back_keep, back_low)
epsilon = 1e-05
rope_base = 100000.0
masked_score = -1e+30
highest = lax.Precision.HIGHEST

def rope_tables(positions):
    half_dim = HEAD_DIM // 2
    frequency = rope_base ** (-2.0 * jnp.arange(half_dim, dtype=jnp.float32) / HEAD_DIM)
    angles = positions.astype(jnp.float32)[:, None] * frequency[None, :]
    return (jnp.cos(angles)[:, None, :], jnp.sin(angles)[:, None, :])

def rotate(values, cosine_table, sine_table):
    half_dim = HEAD_DIM // 2
    first_half = values[..., :half_dim]
    second_half = values[..., half_dim:]
    return jnp.concatenate([first_half * cosine_table - second_half * sine_table, second_half * cosine_table + first_half * sine_table], axis=-1)

def rms_norm(values, gain_row):
    inv_rms = lax.rsqrt(lax.optimization_barrier(jnp.mean(values * values, axis=-1, keepdims=True)) + epsilon)
    return values * inv_rms * gain_row

def attend_block(queries, row_start, keys, values):
    scores = jnp.einsum('qhgd,khd->hgqk', queries, keys, precision=highest) * HEAD_DIM ** (-0.5)
    scores = low_back(scores)
    query_pos = row_start + jnp.arange(queries.shape[0], dtype=jnp.int32)
    key_pos = jnp.arange(keys.shape[0], dtype=jnp.int32)
    scores = jnp.where(key_pos[None, :] <= query_pos[:, None], scores, masked_score)
    row_max = lax.optimization_barrier(jnp.max(scores, axis=-1, keepdims=True))
    powers = jnp.exp(scores - row_max)
    weights_low = low(powers / lax.optimization_barrier(jnp.sum(powers, axis=-1, keepdims=True)))
    return jnp.einsum('hgqk,khd->qhgd', weights_low, values, precision=highest)

def block_forward(inputs, gains, w_qkv, w_out, w_gate, w_up, w_down):
    length = inputs.shape[0]
    kv_width = KV_HEADS * HEAD_DIM
    normed = low(rms_norm(inputs, gains[0]))
    projected = low_back(jnp.dot(normed, w_qkv, precision=highest))
    cosine_table, sine_table = rope_tables(jnp.arange(length, dtype=jnp.int32))
    query_raw = projected[:, :D].reshape(length, HEADS, HEAD_DIM)
    key_raw = projected[:, D:D + kv_width].reshape(length, KV_HEADS, HEAD_DIM)
    value_raw = projected[:, D + kv_width:].reshape(length, KV_HEADS, HEAD_DIM)
    queries = low(rotate(query_raw, cosine_table, sine_table)).reshape(length, KV_HEADS, GROUP, HEAD_DIM)
    keys = low(rotate(key_raw, cosine_table, sine_table))
    values = low(value_raw)
    q_block = min(512, length)
    query_blocks = queries.reshape(length // q_block, q_block, KV_HEADS, GROUP, HEAD_DIM)
    row_starts = jnp.arange(length // q_block, dtype=jnp.int32) * q_block
    attend = jax.checkpoint(attend_block)
    outputs = lax.map(lambda seq_pair: attend(seq_pair[0], seq_pair[1], keys, values), (query_blocks, row_starts))
    attn_out = low_back(low(outputs.reshape(length, D)))
    hidden = inputs + low_back(jnp.dot(attn_out, w_out, precision=highest))
    normed_two = low(rms_norm(hidden, gains[1]))
    gate_value = low_back(jnp.dot(normed_two, w_gate, precision=highest))
    up_value = low_back(jnp.dot(normed_two, w_up, precision=highest))
    inner_act = low(gate_value * jax.nn.sigmoid(gate_value) * up_value)
    return hidden + low_back(jnp.dot(inner_act, w_down, precision=highest))

def reference(tokens, gains, qkv_weight, out_weight, gate_weight, up_weight, down_weight, cotangent):
    weights = (gains.astype(jnp.float32), qkv_weight.astype(jnp.float32), out_weight.astype(jnp.float32), gate_weight.astype(jnp.float32), up_weight.astype(jnp.float32), down_weight.astype(jnp.float32))

    def one_sequence(totals, seq_pair):
        inputs, upstream = seq_pair
        result, pullback = jax.vjp(block_forward, inputs, *weights)
        gradients = pullback(upstream)
        totals = tuple((running + extra for running, extra in zip(totals, gradients[1:])))
        return (totals, (result.astype(jnp.bfloat16), gradients[0]))
    start_totals = tuple((jnp.zeros(weight.shape, jnp.float32) for weight in weights))
    totals, (block_out, input_grad) = lax.scan(one_sequence, start_totals, (tokens.astype(jnp.float32), cotangent))
    return (block_out, input_grad, totals[0], totals[1], totals[2], totals[3], totals[4], totals[5])
```

```python
import functools

import jax
import jax.numpy as jnp
from jax import lax
from jax.experimental import pallas as pl
from jax.experimental.pallas import tpu as pltpu
from jax.sharding import Mesh
from jax.sharding import PartitionSpec as P

HEADS = 15
KV_HEADS = 5
HEAD_DIM = 64
GROUP = 3
LANES = 128
HALF = HEAD_DIM


epsilon = 1e-05
rope_base = 100000.0
masked_score = -1e30


def pair_place(pair, ctx_count, sub):
    turn = pair // (2 * sub)
    spot = pair % (2 * sub)
    low = spot < sub
    return jnp.where(low, turn * sub + spot, (ctx_count - 1 - turn) * sub + 2 * sub - 1 - spot)


def dot_nt(a, b):
    return lax.dot_general(a, b, (((1,), (1,)), ((), ())), preferred_element_type=jnp.float32)


def dot_nn(a, b):
    return lax.dot_general(a, b, (((1,), (0,)), ((), ())), preferred_element_type=jnp.float32)


def dot_tn(a, b):
    return lax.dot_general(a, b, (((0,), (0,)), ((), ())), preferred_element_type=jnp.float32)


def causal(rows, cols, chunk, key_axis):
    shape = (rows, cols)
    query_axis = 1 - key_axis
    query = lax.broadcasted_iota(jnp.int32, shape, query_axis)
    key = lax.broadcasted_iota(jnp.int32, shape, key_axis)
    return key <= lax.rem(query, chunk)


def forward_kernel(ctx_count, sub, chunk, group, pair_ref, q_ref, kv_ref, out_ref, top, total):
    pairs = ctx_count * sub
    own = pair_ref[0]
    part = group * chunk
    lanes = lambda rows: lax.broadcasted_iota(jnp.int32, (rows, LANES), 1)

    def load(place, slot, count):
        return kv_ref[0, pl.ds(pl.multiple_of(place * 2 * chunk + slot * chunk, chunk), count * chunk), :]

    def weighted(powers, kv):
        ones = jnp.where(lanes(kv.shape[0]) < HALF, jnp.ones_like(kv), kv)
        return dot_nn(powers, ones)

    def update(start, rows, kv, first, mask):
        scores = dot_nt(q_ref[0, start : start + rows, :], kv)
        if mask is not None:
            scores = jnp.where(mask, scores, masked_score)
        best = jnp.max(scores, axis=1, keepdims=True)
        spot = slice(start, start + rows)
        if first:
            top[spot, :] = jnp.broadcast_to(best, (rows, LANES))
            powers = jnp.exp(scores - best).astype(jnp.bfloat16)
            total[spot, :] = weighted(powers, kv)
        else:
            old = top[spot, :]
            new = jnp.maximum(old, best)
            powers = jnp.exp(scores - new[:, :1]).astype(jnp.bfloat16)
            total[spot, :] = total[spot, :] * jnp.exp(old - new) + weighted(powers, kv)
            top[spot, :] = new

    place = pair_place(own, ctx_count, sub)
    near = load(place, 0, 1)
    both = load(place, 0, 2)
    near_mask = causal(chunk, chunk, chunk, 1)
    columns = lax.broadcasted_iota(jnp.int32, (chunk, 2 * chunk), 1)
    queries = lax.broadcasted_iota(jnp.int32, (chunk, 2 * chunk), 0)
    both_mask = columns <= queries + chunk
    for head in range(group):
        update(head * chunk, chunk, near, True, near_mask)
        update(part + head * chunk, chunk, both, True, both_mask)

    @pl.loop(0, own)
    def _(pair):
        kv = load(pair_place(pair, ctx_count, sub), 0, 1)
        for head in range(2 * group):
            update(head * chunk, chunk, kv, False, None)

    @pl.loop(own + 1, pairs)
    def _(pair):
        kv = load(pair_place(pair, ctx_count, sub), 0, 2)
        for head in range(group):
            update(part + head * chunk, chunk, kv, False, None)

    for head in range(2 * group):
        spot = slice(head * chunk, (head + 1) * chunk)
        sums = total[spot, :]
        count = sums[:, :1]
        out_ref[0, spot, :] = jnp.where(
            lanes(chunk) < HALF, top[spot, :] + jnp.log(count), sums / count
        )


def attention_forward(own_pair, queries, pairs_all, ctx_count, sub, chunk, group):
    heads, rows, _ = queries.shape
    length = pairs_all.shape[1]
    grid_spec = pltpu.PrefetchScalarGridSpec(
        num_scalar_prefetch=1,
        grid=(heads,),
        in_specs=[
            pl.BlockSpec((1, rows, LANES), lambda h, p: (h, 0, 0)),
            pl.BlockSpec((1, length, LANES), lambda h, p: (h, 0, 0)),
        ],
        out_specs=pl.BlockSpec((1, rows, LANES), lambda h, p: (h, 0, 0)),
        scratch_shapes=[
            pltpu.VMEM((rows, LANES), jnp.float32),
            pltpu.VMEM((rows, LANES), jnp.float32),
        ],
    )
    cost = heads * rows * length // 2
    return pl.pallas_call(
        functools.partial(forward_kernel, ctx_count, sub, chunk, group),
        out_shape=jax.ShapeDtypeStruct((heads, rows, LANES), jnp.float32),
        grid_spec=grid_spec,
        compiler_params=pltpu.CompilerParams(vmem_limit_bytes=48 * 2**20),
        cost_estimate=pl.CostEstimate(
            flops=cost * 4 * HALF, bytes_accessed=heads * LANES * (rows * 6 + length * 2), transcendentals=cost
        ),
        name="attention_forward",
    )(own_pair, queries, pairs_all)


def backward_kernel(
    ctx_count, sub, chunk, group, pair_ref, q_ref, cot_ref, extra_ref, kv_ref, dq_ref, dkv_ref
):
    pairs = ctx_count * sub
    own = pair_ref[0]
    part = group * chunk

    def minus(rows, low, high):
        lane = lax.broadcasted_iota(jnp.int32, (rows, LANES), 1)
        return jnp.where((lane >= low) & (lane < high), -1.0, 0.0).astype(jnp.bfloat16)

    def step(start, rows, place, slot, count, first, mask):
        keys = count * chunk
        base = pl.multiple_of(place * 2 * chunk + slot * chunk, chunk)
        kv = kv_ref[0, pl.ds(base, keys), :]
        key_side = jnp.concatenate([kv, minus(keys, 0, 3)], axis=1)
        value_side = jnp.concatenate([kv, minus(keys, 3, 6)], axis=1)
        pair_sum = None
        for at in range(start, start + rows, chunk):
            spot = slice(at, at + chunk)
            query = q_ref[0, spot, :]
            cot = cot_ref[0, spot, :]
            extra = extra_ref[0, spot, :]
            powers = jnp.exp(dot_nt(key_side, jnp.concatenate([query, extra], axis=1)))
            if mask is not None:
                powers = jnp.where(mask, powers, 0.0)
            slope = dot_nt(value_side, jnp.concatenate([cot, extra], axis=1))
            grads = (powers * slope).astype(jnp.bfloat16)
            powers = powers.astype(jnp.bfloat16)
            term = dot_nn(powers, cot) + dot_nn(grads, query)
            pair_sum = term if pair_sum is None else pair_sum + term
            moved = dot_tn(grads, kv)
            if first:
                dq_ref[0, spot, :] = moved
            else:
                dq_ref[0, spot, :] += moved
        return pair_sum

    def store(place, slot, count, value):
        base = pl.multiple_of(place * 2 * chunk + slot * chunk, chunk)
        dkv_ref[0, pl.ds(base, count * chunk), :] = value.astype(jnp.bfloat16)

    place = pair_place(own, ctx_count, sub)
    near_mask = causal(chunk, chunk, chunk, 0)
    keys = lax.broadcasted_iota(jnp.int32, (2 * chunk, chunk), 0)
    queries = lax.broadcasted_iota(jnp.int32, (2 * chunk, chunk), 1)
    far = step(part, part, place, 0, 2, True, keys <= queries + chunk)
    near = step(0, part, place, 0, 1, True, near_mask)
    store(place, 0, 1, far[:chunk] + near)
    store(place, 1, 1, far[chunk:])

    @pl.loop(0, own)
    def _(pair):
        at = pair_place(pair, ctx_count, sub)
        store(at, 0, 1, step(0, 2 * part, at, 0, 1, False, None))
        store(at, 1, 1, jnp.zeros((chunk, LANES), jnp.float32))

    @pl.loop(own + 1, pairs)
    def _(pair):
        at = pair_place(pair, ctx_count, sub)
        store(at, 0, 2, step(part, part, at, 0, 2, False, None))


def attention_backward(own_pair, queries, cots, extra, pairs_all, ctx_count, sub, chunk, group):
    heads, rows, _ = queries.shape
    length = pairs_all.shape[1]
    row_spec = pl.BlockSpec((1, rows, LANES), lambda h, p: (h, 0, 0))
    long_spec = pl.BlockSpec((1, length, LANES), lambda h, p: (h, 0, 0))
    cost = heads * rows * length // 2
    return pl.pallas_call(
        functools.partial(backward_kernel, ctx_count, sub, chunk, group),
        out_shape=(
            jax.ShapeDtypeStruct((heads, rows, LANES), jnp.float32),
            jax.ShapeDtypeStruct((heads, length, LANES), jnp.bfloat16),
        ),
        grid_spec=pltpu.PrefetchScalarGridSpec(
            num_scalar_prefetch=1,
            grid=(heads,),
            in_specs=[row_spec, row_spec, row_spec, long_spec],
            out_specs=(row_spec, long_spec),
        ),
        compiler_params=pltpu.CompilerParams(vmem_limit_bytes=48 * 2**20),
        cost_estimate=pl.CostEstimate(
            flops=cost * 10 * HALF, bytes_accessed=heads * LANES * (rows * 10 + length * 4), transcendentals=cost
        ),
        name="attention_backward",
    )(own_pair, queries, cots, extra, pairs_all)


def three_parts(values):
    high = values.astype(jnp.bfloat16)
    rest = values - high.astype(jnp.float32)
    middle = rest.astype(jnp.bfloat16)
    low = (rest - middle.astype(jnp.float32)).astype(jnp.bfloat16)
    return [high, middle, low]


def rope_tables(positions):
    half_dim = HEAD_DIM // 2
    frequency = rope_base ** (-2.0 * jnp.arange(half_dim, dtype=jnp.float32) / HEAD_DIM)
    angles = positions.astype(jnp.float32)[:, None] * frequency[None, :]
    return (jnp.cos(angles)[:, None, :], jnp.sin(angles)[:, None, :])


def rotate(values, cosine_table, sine_table):
    half_dim = HEAD_DIM // 2
    first_half = values[..., :half_dim]
    second_half = values[..., half_dim:]
    return jnp.concatenate(
        [
            first_half * cosine_table - second_half * sine_table,
            second_half * cosine_table + first_half * sine_table,
        ],
        axis=-1,
    )


def norm_parts(values, gain_row):
    inv_rms = lax.rsqrt(jnp.mean(values * values, axis=-1, keepdims=True) + epsilon)
    unit_rows = values * inv_rms
    return (unit_rows, inv_rms, unit_rows * gain_row)


def norm_back(upstream, unit_rows, inv_rms, gain_row):
    shaped = upstream * gain_row
    inner_mean = jnp.mean(shaped * unit_rows, axis=-1, keepdims=True)
    return (inv_rms * (shaped - unit_rows * inner_mean), jnp.sum(upstream * unit_rows, axis=0))


def matmul(spec, left, right):
    return jnp.einsum(spec, left, right, preferred_element_type=jnp.float32)


def swap_ends(values):
    count = lax.axis_size("ctx")
    return lax.ppermute(values, "ctx", [(i, count - 1 - i) for i in range(count)])


def spread(values):
    count = lax.axis_size("sub")
    parts = [values]
    for shift in range(1, count):
        parts.append(lax.ppermute(values, "sub", [(i, (i + shift) % count) for i in range(count)]))
    return jnp.concatenate(parts, axis=0)


def collect(values):
    count = lax.axis_size("sub")
    parts = jnp.split(values, count, axis=0)
    total = parts[0].astype(jnp.float32)
    for shift in range(1, count):
        total = total + lax.ppermute(
            parts[shift].astype(jnp.bfloat16), "sub", [((i + shift) % count, i) for i in range(count)]
        ).astype(jnp.float32)
    return total


def shards(tokens, gains, qkv_weight, out_weight, gate_weight, up_weight, down_weight, cotangent):
    seq_count, span_len, width = tokens.shape
    ctx_count, sub_count = lax.axis_size("ctx"), lax.axis_size("sub")
    pair_count = ctx_count * sub_count
    chunk = span_len // (2 * sub_count)
    row_count = 2 * chunk
    kv_width = KV_HEADS * HEAD_DIM
    owners = lax.axis_size(("shard", "ctx"))
    tensor_count = lax.axis_size(("seq", "sub"))
    everyone = ("seq", "sub", "shard", "ctx")
    own_seq, own_sub, own_ctx = lax.axis_index("seq"), lax.axis_index("sub"), lax.axis_index("ctx")
    is_low = own_ctx < ctx_count // 2
    own_pair = jnp.where(
        is_low,
        2 * sub_count * own_ctx + own_sub,
        2 * pair_count - 1 - 2 * sub_count * own_ctx - own_sub,
    ).astype(jnp.int32)
    scale_factor = HEAD_DIM ** (-0.5)

    def take_rows(values):
        span = lax.dynamic_index_in_dim(values, own_seq, 0, keepdims=False)
        kept = lax.dynamic_slice_in_dim(span, own_sub * chunk, chunk, 0)
        moved = lax.dynamic_slice_in_dim(span, (2 * sub_count - 1 - own_sub) * chunk, chunk, 0)
        return kept, moved

    def in_order(kept, moved):
        return jnp.where(is_low, jnp.concatenate([kept, moved]), jnp.concatenate([moved, kept]))

    def give_rows(values):
        low, high = values[:chunk], values[chunk:]
        kept = jnp.where(is_low, low, high)
        moved = swap_ends(jnp.where(is_low, high, low))
        both = lax.all_gather(jnp.stack([kept, moved]), ("seq", "sub"), axis=0, tiled=False)
        both = both.reshape(seq_count, sub_count, 2, chunk, width)
        return jnp.concatenate([both[:, :, 0], both[:, ::-1, 1]], axis=1).reshape(
            seq_count, span_len, width
        )

    tile_rows, tile_cols = qkv_weight.shape
    gain_part = gains.shape[1]
    first_tile = jnp.concatenate(
        [qkv_weight, jnp.pad(gains, ((0, 0), (0, tile_cols - gain_part)))], axis=0
    )
    first_all = lax.all_gather(first_tile, everyone, axis=0, tiled=False).reshape(
        tensor_count, owners, tile_rows + 2, tile_cols
    )
    qkv_all = jnp.transpose(first_all[:, :, :tile_rows], (0, 2, 1, 3)).reshape(
        tensor_count * tile_rows, owners * tile_cols
    )
    gain_all = (
        jnp.transpose(first_all[0, :, tile_rows:, :gain_part], (1, 0, 2))
        .reshape(2, width)
        .astype(jnp.float32)
    )
    gain_one, gain_two = gain_all[0], gain_all[1]
    out_rows, out_cols = out_weight.shape
    out_all = jnp.transpose(
        lax.all_gather(out_weight, everyone, axis=0, tiled=False).reshape(
            tensor_count, owners, out_rows, out_cols
        ),
        (0, 2, 1, 3),
    ).reshape(width, width)
    hidden_part = gate_weight.shape[1]
    ffn_tile = jnp.concatenate([gate_weight, up_weight, down_weight.T], axis=1)
    ffn_all = lax.all_gather(ffn_tile, ("seq", "shard", "ctx"), axis=0, tiled=True).reshape(
        seq_count, width, 3 * hidden_part
    )

    kept_tokens, moved_tokens = take_rows(tokens)
    kept_cot, moved_cot = take_rows(cotangent)
    rows_low = in_order(kept_tokens, swap_ends(moved_tokens))
    cot = in_order(kept_cot, swap_ends(moved_cot.astype(jnp.bfloat16)).astype(jnp.float32))
    inputs = rows_low.astype(jnp.float32)
    unit_one, rms_one, normed_full = norm_parts(inputs, gain_one)
    normed = normed_full.astype(jnp.bfloat16)
    projected = matmul("rd,de->re", normed, qkv_all)
    step = jnp.arange(chunk, dtype=jnp.int32)
    positions = jnp.concatenate([own_pair * chunk + step, (2 * pair_count - 1 - own_pair) * chunk + step])
    cosine_table, sine_table = rope_tables(positions)
    queries = rotate(
        projected[:, :width].reshape(row_count, HEADS, HEAD_DIM), cosine_table, sine_table
    )
    keys = rotate(
        projected[:, width : width + kv_width].reshape(row_count, KV_HEADS, HEAD_DIM),
        cosine_table,
        sine_table,
    )
    values = projected[:, width + kv_width :].reshape(row_count, KV_HEADS, HEAD_DIM)

    def by_head(rows, before, after):
        rows = rows.reshape(2, chunk, KV_HEADS, GROUP, HEAD_DIM)
        rows = jnp.transpose(rows, (2, 0, 3, 1, 4)).reshape(KV_HEADS, GROUP * row_count, HEAD_DIM)
        return jnp.pad(rows, ((0, 0), (0, 0), (before, after)))

    def by_row(rows):
        rows = rows.reshape(KV_HEADS, 2, GROUP, chunk, HEAD_DIM)
        return jnp.transpose(rows, (1, 3, 0, 2, 4)).reshape(row_count, HEADS, HEAD_DIM)

    query_heads = by_head(queries.astype(jnp.bfloat16) * jnp.bfloat16(scale_factor), 0, HEAD_DIM)
    pair_own = jnp.transpose(
        jnp.concatenate([keys, values], axis=-1).astype(jnp.bfloat16), (1, 0, 2)
    )
    pair_all = lax.all_gather(pair_own, ("ctx", "sub"), axis=1, tiled=True)
    place = own_pair[None]
    attended = attention_forward(place, query_heads, pair_all, ctx_count, sub_count, chunk, GROUP)
    attn_sum = attended[..., HEAD_DIM:]
    log_total = attended[..., 0]
    attn_low = by_row(attn_sum.astype(jnp.bfloat16)).reshape(row_count, width)
    hidden = inputs + matmul("rf,fe->re", attn_low, out_all)
    unit_two, rms_two, normed_two_full = norm_parts(hidden, gain_two)
    normed_two = spread(normed_two_full.astype(jnp.bfloat16))
    cot_low = spread(cot.astype(jnp.bfloat16))
    feed_sum, normed_sum, ffn_grads = 0.0, 0.0, []
    for part in range(seq_count):
        gate_up = ffn_all[part, :, : 2 * hidden_part]
        down = ffn_all[part, :, 2 * hidden_part :]
        both = matmul("rd,df->rf", normed_two, gate_up)
        gate_value, up_value = both[:, :hidden_part], both[:, hidden_part:]
        gate_sigmoid = jax.nn.sigmoid(gate_value)
        inner_act = (gate_value * gate_sigmoid * up_value).astype(jnp.bfloat16)
        feed_sum = feed_sum + matmul("rf,ef->re", inner_act, down)
        inner_grad = matmul("re,ef->rf", cot_low, down)
        gate_grad = (
            inner_grad * up_value * gate_sigmoid * (1.0 + gate_value * (1.0 - gate_sigmoid))
        ).astype(jnp.bfloat16)
        up_grad = (inner_grad * gate_value * gate_sigmoid).astype(jnp.bfloat16)
        both_grad = jnp.concatenate([gate_grad, up_grad], axis=1)
        normed_sum = normed_sum + matmul("rf,df->rd", both_grad, gate_up)
        ffn_grads.append(
            jnp.concatenate(
                [
                    matmul("rd,rf->df", normed_two, both_grad).astype(jnp.bfloat16),
                    matmul("re,rf->ef", cot_low, inner_act).astype(jnp.bfloat16),
                ],
                axis=1,
            )
        )
    normed_two_grad = collect(normed_sum)
    block_out = give_rows((hidden + collect(feed_sum)).astype(jnp.bfloat16))
    hidden_part_grad, gain_two_grad = norm_back(normed_two_grad, unit_two, rms_two, gain_two)
    hidden_grad = cot + hidden_part_grad
    hidden_low = hidden_grad.astype(jnp.bfloat16)
    attn_grad = matmul("re,fe->rf", hidden_low, out_all).astype(jnp.bfloat16)
    grad_heads = by_head(attn_grad, HEAD_DIM, 0)
    row_delta = jnp.sum(grad_heads[..., HEAD_DIM:].astype(jnp.float32) * attn_sum, axis=-1)
    extra = jnp.stack(three_parts(log_total) + three_parts(row_delta), axis=-1)
    extra = jnp.pad(extra, ((0, 0), (0, 0), (0, LANES - extra.shape[-1])))
    query_grad, pair_grad = attention_backward(
        place, query_heads, grad_heads, extra, pair_all, ctx_count, sub_count, chunk, GROUP
    )
    pair_own_grad = jnp.transpose(
        lax.psum_scatter(pair_grad, ("ctx", "sub"), scatter_dimension=1, tiled=True).astype(jnp.float32),
        (1, 0, 2),
    )
    query_back = rotate(by_row(query_grad[..., :HEAD_DIM] * scale_factor), cosine_table, -sine_table)
    key_back = rotate(pair_own_grad[..., :HEAD_DIM], cosine_table, -sine_table)
    proj_grad = jnp.concatenate(
        [
            query_back.reshape(row_count, width),
            key_back.reshape(row_count, kv_width),
            pair_own_grad[..., HEAD_DIM:].reshape(row_count, kv_width),
        ],
        axis=-1,
    ).astype(jnp.bfloat16)
    normed_grad = matmul("re,de->rd", proj_grad, qkv_all)
    input_part_grad, gain_one_grad = norm_back(normed_grad, unit_one, rms_one, gain_one)
    input_grad = give_rows((hidden_grad + input_part_grad).astype(jnp.bfloat16)).astype(jnp.float32)

    def tiles(grad, rows, cols):
        grad = grad.reshape(tensor_count, rows, owners, cols)
        return jnp.transpose(grad, (0, 2, 1, 3))

    qkv_grad = tiles(matmul("rd,re->de", normed, proj_grad).astype(jnp.bfloat16), tile_rows, tile_cols)
    gains_grad = jnp.transpose(
        jnp.stack([gain_one_grad, gain_two_grad]).reshape(2, owners, gain_part), (1, 0, 2)
    ).astype(jnp.bfloat16)
    gains_tile = jnp.pad(gains_grad, ((0, 0), (0, 0), (0, tile_cols - gain_part)))
    last = jnp.concatenate(
        [qkv_grad, jnp.broadcast_to(gains_tile, (tensor_count,) + gains_tile.shape)], axis=2
    ).reshape(tensor_count * owners, tile_rows + 2, tile_cols)
    last = lax.psum_scatter(last, everyone, scatter_dimension=0, tiled=False).astype(jnp.float32)
    out_grad = tiles(
        matmul("rf,re->fe", attn_low, hidden_low).astype(jnp.bfloat16), out_rows, out_cols
    ).reshape(tensor_count * owners, out_rows, out_cols)
    out_out = lax.psum_scatter(out_grad, everyone, scatter_dimension=0, tiled=False).astype(jnp.float32)
    ffn_out = lax.psum_scatter(
        jnp.concatenate(ffn_grads, axis=0), ("seq", "shard", "ctx"), scatter_dimension=0, tiled=True
    ).astype(jnp.float32)
    return (
        block_out,
        input_grad,
        last[tile_rows:, :gain_part],
        last[:tile_rows],
        out_out,
        ffn_out[:, :hidden_part],
        ffn_out[:, hidden_part : 2 * hidden_part],
        ffn_out[:, 2 * hidden_part :].T,
    )


def solution(mesh):
    shard_count, ctx_count, tensor_count = (mesh.shape[axis] for axis in ("shard", "ctx", "tensor"))

    def run(tokens, *rest):
        seq_count = tokens.shape[0] // shard_count
        split = Mesh(
            mesh.devices.reshape(shard_count, ctx_count, seq_count, tensor_count // seq_count),
            ("shard", "ctx", "seq", "sub"),
        )
        rows = P("shard", "ctx", None)
        pool = ("shard", "ctx")
        team = ("seq", "sub")
        weights = (P(None, pool), P(team, pool), P(team, pool), P(pool, team), P(pool, team), P(team, pool))
        return jax.shard_map(
            shards,
            mesh=split,
            in_specs=(rows,) + weights + (rows,),
            out_specs=(rows, rows) + weights,
            check_vma=False,
        )(tokens, *rest)

    return run
```

```python
import functools

import jax
import jax.numpy as jnp
from jax import lax
from jax.experimental import pallas as pl
from jax.experimental.pallas import tpu as pltpu
from jax.sharding import Mesh
from jax.sharding import PartitionSpec as P

HEADS = 15
KV_HEADS = 5
HEAD_DIM = 64
GROUP = 3
LANES = 128
HALF = HEAD_DIM


epsilon = 1e-05
rope_base = 100000.0
masked_score = -1e30


def pair_place(pair, ctx_count, sub):
    turn = pair // (2 * sub)
    spot = pair % (2 * sub)
    low = spot < sub
    return jnp.where(low, turn * sub + spot, (ctx_count - 1 - turn) * sub + 2 * sub - 1 - spot)


def dot_nt(a, b):
    return lax.dot_general(a, b, (((1,), (1,)), ((), ())), preferred_element_type=jnp.float32)


def dot_nn(a, b):
    return lax.dot_general(a, b, (((1,), (0,)), ((), ())), preferred_element_type=jnp.float32)


def dot_tn(a, b):
    return lax.dot_general(a, b, (((0,), (0,)), ((), ())), preferred_element_type=jnp.float32)


def causal(rows, cols, chunk, key_axis):
    shape = (rows, cols)
    query_axis = 1 - key_axis
    query = lax.broadcasted_iota(jnp.int32, shape, query_axis)
    key = lax.broadcasted_iota(jnp.int32, shape, key_axis)
    return key <= lax.rem(query, chunk)


def forward_kernel(ctx_count, sub, chunk, group, pair_ref, q_ref, kv_ref, out_ref, top, total):
    pairs = ctx_count * sub
    own = pair_ref[0]
    part = group * chunk
    lanes = lambda rows: lax.broadcasted_iota(jnp.int32, (rows, LANES), 1)

    def load(place, slot, count):
        return kv_ref[0, pl.ds(pl.multiple_of(place * 2 * chunk + slot * chunk, chunk), count * chunk), :]

    def weighted(powers, kv):
        ones = jnp.where(lanes(kv.shape[0]) < HALF, jnp.ones_like(kv), kv)
        return dot_nn(powers, ones)

    def update(start, rows, kv, first, mask):
        scores = dot_nt(q_ref[0, start : start + rows, :], kv)
        if mask is not None:
            scores = jnp.where(mask, scores, masked_score)
        best = jnp.max(scores, axis=1, keepdims=True)
        spot = slice(start, start + rows)
        if first:
            top[spot, :] = jnp.broadcast_to(best, (rows, LANES))
            powers = jnp.exp(scores - best).astype(jnp.bfloat16)
            total[spot, :] = weighted(powers, kv)
        else:
            old = top[spot, :]
            new = jnp.maximum(old, best)
            powers = jnp.exp(scores - new[:, :1]).astype(jnp.bfloat16)
            total[spot, :] = total[spot, :] * jnp.exp(old - new) + weighted(powers, kv)
            top[spot, :] = new

    place = pair_place(own, ctx_count, sub)
    near = load(place, 0, 1)
    both = load(place, 0, 2)
    near_mask = causal(chunk, chunk, chunk, 1)
    columns = lax.broadcasted_iota(jnp.int32, (chunk, 2 * chunk), 1)
    queries = lax.broadcasted_iota(jnp.int32, (chunk, 2 * chunk), 0)
    both_mask = columns <= queries + chunk
    for head in range(group):
        update(head * chunk, chunk, near, True, near_mask)
        update(part + head * chunk, chunk, both, True, both_mask)

    def sweep(first, last, count, start, heads):
        def load_at(pair):
            return load(pair_place(pair, ctx_count, sub), 0, count)

        def absorb(kv):
            for head in range(heads):
                update(start + head * chunk, chunk, kv, False, None)

        twos = (last - first) // 2

        @pl.loop(0, twos)
        def _(step):
            pair = first + 2 * step
            absorb(jnp.concatenate([load_at(pair), load_at(pair + 1)], axis=0))

        @pl.when(first + 2 * twos < last)
        def _():
            absorb(load_at(last - 1))

    sweep(0, own, 1, 0, 2 * group)
    sweep(own + 1, pairs, 2, part, group)

    for head in range(2 * group):
        spot = slice(head * chunk, (head + 1) * chunk)
        sums = total[spot, :]
        count = sums[:, :1]
        out_ref[0, spot, :] = jnp.where(
            lanes(chunk) < HALF, top[spot, :] + jnp.log(count), sums / count
        )


def attention_forward(own_pair, queries, pairs_all, base, ctx_count, sub, chunk, group):
    rows = queries.shape[1]
    heads, length, _ = pairs_all.shape
    grid_spec = pltpu.PrefetchScalarGridSpec(
        num_scalar_prefetch=1,
        grid=(heads,),
        in_specs=[
            pl.BlockSpec((1, rows, LANES), lambda h, p: (base + h, 0, 0)),
            pl.BlockSpec((1, length, LANES), lambda h, p: (h, 0, 0)),
        ],
        out_specs=pl.BlockSpec((1, rows, LANES), lambda h, p: (h, 0, 0)),
        scratch_shapes=[
            pltpu.VMEM((rows, LANES), jnp.float32),
            pltpu.VMEM((rows, LANES), jnp.float32),
        ],
    )
    cost = heads * rows * length // 2
    return pl.pallas_call(
        functools.partial(forward_kernel, ctx_count, sub, chunk, group),
        out_shape=jax.ShapeDtypeStruct((heads, rows, LANES), jnp.float32),
        grid_spec=grid_spec,
        compiler_params=pltpu.CompilerParams(vmem_limit_bytes=48 * 2**20),
        cost_estimate=pl.CostEstimate(
            flops=cost * 4 * HALF, bytes_accessed=heads * LANES * (rows * 6 + length * 2), transcendentals=cost
        ),
        name="attention_forward",
    )(own_pair, queries, pairs_all)


def backward_kernel(
    ctx_count, sub, chunk, group, pair_ref, q_ref, cot_ref, extra_ref, kv_ref, dq_ref, dkv_ref
):
    pairs = ctx_count * sub
    own = pair_ref[0]
    part = group * chunk

    def minus(rows, low, high):
        lane = lax.broadcasted_iota(jnp.int32, (rows, LANES), 1)
        return jnp.where((lane >= low) & (lane < high), -1.0, 0.0).astype(jnp.bfloat16)

    def load(place, slot, count):
        base = pl.multiple_of(place * 2 * chunk + slot * chunk, chunk)
        return kv_ref[0, pl.ds(base, count * chunk), :]

    def step(start, rows, kv, first, mask):
        keys = kv.shape[0]
        key_side = jnp.concatenate([kv, minus(keys, 0, 3)], axis=1)
        value_side = jnp.concatenate([kv, minus(keys, 3, 6)], axis=1)
        pair_sum = None
        for at in range(start, start + rows, chunk):
            spot = slice(at, at + chunk)
            query = q_ref[0, spot, :]
            cot = cot_ref[0, spot, :]
            extra = extra_ref[0, spot, :]
            powers = jnp.exp(dot_nt(key_side, jnp.concatenate([query, extra], axis=1)))
            if mask is not None:
                powers = jnp.where(mask, powers, 0.0)
            slope = dot_nt(value_side, jnp.concatenate([cot, extra], axis=1))
            grads = (powers * slope).astype(jnp.bfloat16)
            powers = powers.astype(jnp.bfloat16)
            term = dot_nn(powers, cot) + dot_nn(grads, query)
            pair_sum = term if pair_sum is None else pair_sum + term
            moved = dot_tn(grads, kv)
            if first:
                dq_ref[0, spot, :] = moved
            else:
                dq_ref[0, spot, :] += moved
        return pair_sum

    def store(place, slot, count, value):
        base = pl.multiple_of(place * 2 * chunk + slot * chunk, chunk)
        dkv_ref[0, pl.ds(base, count * chunk), :] = value.astype(jnp.bfloat16)

    place = pair_place(own, ctx_count, sub)
    near_mask = causal(chunk, chunk, chunk, 0)
    keys = lax.broadcasted_iota(jnp.int32, (2 * chunk, chunk), 0)
    queries = lax.broadcasted_iota(jnp.int32, (2 * chunk, chunk), 1)
    far = step(part, part, load(place, 0, 2), True, keys <= queries + chunk)
    near = step(0, part, load(place, 0, 1), True, near_mask)
    store(place, 0, 1, far[:chunk] + near)
    store(place, 1, 1, far[chunk:])

    def sweep(first, last, count, start, rows):
        twos = (last - first) // 2

        def put(at, value):
            store(at, 0, count, value)
            if count == 1:
                store(at, 1, 1, jnp.zeros((chunk, LANES), jnp.float32))

        @pl.loop(0, twos)
        def _(turn):
            one = pair_place(first + 2 * turn, ctx_count, sub)
            two = pair_place(first + 2 * turn + 1, ctx_count, sub)
            kv = jnp.concatenate([load(one, 0, count), load(two, 0, count)], axis=0)
            sums = step(start, rows, kv, False, None)
            put(one, sums[: count * chunk])
            put(two, sums[count * chunk :])

        @pl.when(first + 2 * twos < last)
        def _():
            at = pair_place(last - 1, ctx_count, sub)
            put(at, step(start, rows, load(at, 0, count), False, None))

    sweep(0, own, 1, 0, 2 * part)
    sweep(own + 1, pairs, 2, part, part)


def attention_backward(own_pair, queries, cots, extra, pairs_all, base, filled, ctx_count, sub, chunk, group):
    total_heads, rows, _ = queries.shape
    heads, length, _ = pairs_all.shape
    row_spec = pl.BlockSpec((1, rows, LANES), lambda h, p: (base + h, 0, 0))
    long_spec = pl.BlockSpec((1, length, LANES), lambda h, p: (base + h, 0, 0))
    part_spec = pl.BlockSpec((1, length, LANES), lambda h, p: (h, 0, 0))
    cost = heads * rows * length // 2
    kernel = functools.partial(backward_kernel, ctx_count, sub, chunk, group)

    def filling(pair_ref, q_ref, cot_ref, extra_ref, kv_ref, old_dq_ref, old_dkv_ref, dq_ref, dkv_ref):
        kernel(pair_ref, q_ref, cot_ref, extra_ref, kv_ref, dq_ref, dkv_ref)

    return pl.pallas_call(
        filling if filled else kernel,
        out_shape=(
            jax.ShapeDtypeStruct((total_heads, rows, LANES), jnp.float32),
            jax.ShapeDtypeStruct((total_heads, length, LANES), jnp.bfloat16),
        ),
        grid_spec=pltpu.PrefetchScalarGridSpec(
            num_scalar_prefetch=1,
            grid=(heads,),
            in_specs=[row_spec, row_spec, row_spec, part_spec]
            + [pl.BlockSpec(memory_space=pl.ANY)] * len(filled),
            out_specs=(row_spec, long_spec),
        ),
        input_output_aliases={5 + at: at for at in range(len(filled))},
        compiler_params=pltpu.CompilerParams(vmem_limit_bytes=48 * 2**20),
        cost_estimate=pl.CostEstimate(
            flops=cost * 10 * HALF, bytes_accessed=heads * LANES * (rows * 10 + length * 4), transcendentals=cost
        ),
        name="attention_backward",
    )(own_pair, queries, cots, extra, pairs_all, *filled)


def three_parts(values):
    high = values.astype(jnp.bfloat16)
    rest = values - high.astype(jnp.float32)
    middle = rest.astype(jnp.bfloat16)
    low = (rest - middle.astype(jnp.float32)).astype(jnp.bfloat16)
    return [high, middle, low]


def lane_index(rows):
    return lax.broadcasted_iota(jnp.int32, (rows, LANES), 1)


def swap_halves(tile):
    lane = lane_index(tile.shape[0])
    quarter = HALF // 2
    return jnp.where(
        lax.rem(lane, HALF) < quarter,
        pltpu.roll(tile, LANES - quarter, 1),
        pltpu.roll(tile, quarter, 1),
    )


def normalise(values):
    inv_rms = lax.rsqrt(jnp.mean(values * values, axis=-1, keepdims=True) + epsilon)
    return values * inv_rms, inv_rms


def norm_back(upstream, values, gain_row):
    unit_rows, inv_rms = normalise(values)
    shaped = upstream * gain_row
    inner_mean = jnp.mean(shaped * unit_rows, axis=-1, keepdims=True)
    return inv_rms * (shaped - unit_rows * inner_mean), upstream * unit_rows


def assemble_kernel(rows, in_ref, out_ref):
    tiles = [in_ref[at, :rows, :] for at in range(in_ref.shape[0])]
    used = len(tiles) * tiles[0].shape[1]
    if used < out_ref.shape[1]:
        tiles.append(jnp.zeros((rows, out_ref.shape[1] - used), tiles[0].dtype))
    out_ref[...] = jnp.concatenate(tiles, axis=1)


def assemble(gathered, teams, rows, cols):
    count = gathered.shape[0] // teams
    return pl.pallas_call(
        functools.partial(assemble_kernel, rows),
        grid=(teams,),
        in_specs=[pl.BlockSpec((count,) + gathered.shape[1:], lambda t: (t, 0, 0))],
        out_specs=pl.BlockSpec((rows, cols), lambda t: (t, 0)),
        out_shape=jax.ShapeDtypeStruct((teams * rows, cols), gathered.dtype),
        compiler_params=pltpu.CompilerParams(vmem_limit_bytes=48 * 2**20),
        name="assemble",
    )(gathered)


def project_kernel(token_ref, gain_ref, weight_ref, cos_ref, sin_ref, q_ref, kv_ref, normed_ref):
    rows = token_ref.shape[0]
    unit_rows, _ = normalise(token_ref[...].astype(jnp.float32))
    normed = (unit_rows * gain_ref[...]).astype(jnp.bfloat16)
    normed_ref[...] = normed
    projected = dot_nn(normed, weight_ref[...])
    cos, sin = cos_ref[...], sin_ref[...]
    low = lane_index(rows) < HALF

    def tile(column):
        return projected[:, column // 2 * LANES : (column // 2 + 1) * LANES]

    def turned(column):
        raw = tile(column)
        out = raw * cos + swap_halves(raw) * sin
        return pltpu.roll(out, HALF, 1) if column % 2 else out

    for head in range(HEADS):
        query = jnp.where(low, turned(head) * HEAD_DIM ** (-0.5), 0.0)
        q_ref[head // GROUP, 0, head % GROUP] = query.astype(jnp.bfloat16)
    for head in range(KV_HEADS):
        key = turned(HEADS + head)
        column = HEADS + KV_HEADS + head
        value = tile(column) if column % 2 else pltpu.roll(tile(column), HALF, 1)
        kv_ref[head] = jnp.where(low, key, value).astype(jnp.bfloat16)


def whole(shape):
    return pl.BlockSpec(shape, lambda c: (0,) * len(shape))


def row_call(kernel, chunk, ins, outs, name, flops):
    def spec(array):
        shape = array.shape
        if len(shape) == 5:
            return pl.BlockSpec((shape[0], 1) + shape[2:], lambda c: (0, c, 0, 0, 0))
        if len(shape) == 3:
            return pl.BlockSpec((shape[0], chunk, shape[2]), lambda c: (0, c, 0))
        if shape[0] != 2 * chunk:
            return pl.BlockSpec((shape[0], chunk), lambda c: (0, c))
        return pl.BlockSpec((chunk, shape[1]), lambda c: (c, 0))

    moved = sum(a.size * a.dtype.itemsize for a, _ in ins) + sum(o.size * o.dtype.itemsize for o, _ in outs)
    return pl.pallas_call(
        kernel,
        grid=(2,),
        in_specs=[whole(a.shape) if fixed else spec(a) for a, fixed in ins],
        out_specs=[whole(o.shape) if fixed else spec(o) for o, fixed in outs],
        out_shape=[o for o, _ in outs],
        compiler_params=pltpu.CompilerParams(vmem_limit_bytes=56 * 2**20),
        cost_estimate=pl.CostEstimate(flops=flops, bytes_accessed=moved, transcendentals=0),
        name=name,
    )(*[a for a, _ in ins])


def pick(refs, head):
    group, at = head // GROUP, 0
    for ref in refs:
        if group < at + ref.shape[0]:
            return ref[group - at, 0, head % GROUP]
        at += ref.shape[0]


def pick_pair(refs, group):
    at = 0
    for ref in refs:
        if group < at + ref.shape[0]:
            return ref[group - at]
        at += ref.shape[0]


def mix_kernel(count, *refs):
    attended_refs = refs[:count]
    weight_ref, token_ref, gain_ref, hidden_ref, normed_ref, attn_ref = refs[count:]
    total = token_ref[...].astype(jnp.float32)
    first = lane_index(token_ref.shape[0]) < HALF
    for head in range(HEADS):
        rows = pick(attended_refs, head)
        total = total + dot_nn(rows.astype(jnp.bfloat16), weight_ref[head])
        base = head // 2 * LANES
        if head % 2:
            both = jnp.where(first, pltpu.roll(before, HALF, 1), rows)
            attn_ref[:, base : base + LANES] = both.astype(jnp.bfloat16)
        elif head == HEADS - 1:
            alone = pltpu.roll(rows, HALF, 1)[:, :HALF]
            attn_ref[:, base : base + HALF] = alone.astype(jnp.bfloat16)
        before = rows
    hidden_ref[...] = total
    unit_rows, _ = normalise(total)
    normed_ref[:, : total.shape[1]] = (unit_rows * gain_ref[...]).astype(jnp.bfloat16)


def accumulate(ref, rows):
    summed = jnp.broadcast_to(jnp.sum(rows, axis=0, keepdims=True), ref.shape)

    @pl.when(pl.program_id(0) == 0)
    def _():
        ref[...] = summed

    @pl.when(pl.program_id(0) != 0)
    def _():
        ref[...] += summed


def unmix_kernel(count, parts, *refs):
    ups = refs[:count]
    attended_refs, refs = refs[count : count + parts], refs[count + parts :]
    (hidden_ref, cot_ref, gain_ref, weight_ref, grad_ref, low_ref, heads_ref, extra_ref, gain_grad_ref) = refs
    width = hidden_ref.shape[1]
    upstream = ups[0][:, :width].astype(jnp.float32)
    for ref in ups[1:]:
        upstream = upstream + ref[:, :width].astype(jnp.float32)
    back, gain_rows = norm_back(upstream, hidden_ref[...], gain_ref[...])
    accumulate(gain_grad_ref, gain_rows)
    hidden_grad = cot_ref[...] + back
    grad_ref[...] = hidden_grad
    hidden_low = hidden_grad.astype(jnp.bfloat16)
    low_ref[...] = hidden_low
    lane = lane_index(hidden_low.shape[0])
    for head in range(HEADS):
        spot = (head // GROUP, 0, head % GROUP)
        cots = dot_nt(hidden_low, weight_ref[head]).astype(jnp.bfloat16)
        heads_ref[spot] = cots
        attended = pick(attended_refs, head)
        delta = jnp.sum(cots.astype(jnp.float32) * attended, axis=1, keepdims=True)
        base = jnp.where(lane < 3, attended[:, :1], jnp.where(lane < 6, delta, 0.0))
        high, middle, low = three_parts(base)
        part = lax.rem(lane, 3)
        extra_ref[spot] = jnp.where(
            part == 0,
            high.astype(jnp.float32),
            jnp.where(part == 1, middle.astype(jnp.float32), low.astype(jnp.float32)),
        ).astype(jnp.bfloat16)


def turn_back(dq_ref, dkv_ref, cos_ref, sin_ref, proj_ref):
    rows = cos_ref.shape[0]
    cos, sin = cos_ref[...], sin_ref[...]
    low = lane_index(rows) < HALF

    def half(column):
        if column < HEADS:
            return dq_ref[column // GROUP, 0, column % GROUP] * HEAD_DIM ** (-0.5), 0
        if column < HEADS + KV_HEADS:
            return dkv_ref[column - HEADS].astype(jnp.float32), 0
        if column < HEADS + 2 * KV_HEADS:
            return dkv_ref[column - HEADS - KV_HEADS].astype(jnp.float32), 1
        return jnp.zeros((rows, LANES), jnp.float32), 0

    def placed(column):
        value, side = half(column)
        return value if side == column % 2 else pltpu.roll(value, HALF, 1)

    for at in range(proj_ref.shape[1] // LANES):
        raw = jnp.where(low, placed(2 * at), placed(2 * at + 1))
        if 2 * at < HEADS + KV_HEADS:
            raw = raw * cos - swap_halves(raw) * sin
        proj_ref[:, at * LANES : (at + 1) * LANES] = raw.astype(jnp.bfloat16)


def early_kernel(dq_ref, cos_ref, sin_ref, proj_ref):
    turn_back(dq_ref, None, cos_ref, sin_ref, proj_ref)


def block_kernel(count, *refs):
    hidden_ref, out_ref = refs[count], refs[count + 1]
    rows = hidden_ref[...]
    for ref in refs[:count]:
        rows = rows + ref[:, : rows.shape[1]].astype(jnp.float32)
    out_ref[...] = jnp.transpose(rows).astype(jnp.bfloat16)


def finish_kernel(
    dq_ref, dkv_ref, cos_ref, sin_ref, weight_ref, token_ref, grad_ref, gain_ref,
    proj_ref, input_ref, gain_grad_ref,
):
    turn_back(dq_ref, dkv_ref, cos_ref, sin_ref, proj_ref)
    upstream = dot_nt(proj_ref[...], weight_ref[...])
    back, gain_rows = norm_back(upstream, token_ref[...].astype(jnp.float32), gain_ref[...])
    accumulate(gain_grad_ref, gain_rows)
    input_ref[...] = jnp.transpose(grad_ref[...] + back).astype(jnp.bfloat16)


def feed_kernel(rows_ref, cot_ref, weight_ref, back_ref, feed_ref, inner_ref, grad_ref):
    part = inner_ref.shape[1]
    width = weight_ref.shape[0]
    rows, cots = rows_ref[:, :width], cot_ref[:, :width]
    gate_up, down = weight_ref[:, : 2 * part], weight_ref[:, 2 * part :]
    both = dot_nn(rows, gate_up)
    inner_grad = dot_nn(cots, down)
    gate_value, up_value = both[:, :part], both[:, part:]
    gate_sigmoid = jax.nn.sigmoid(gate_value)
    swish = gate_value * gate_sigmoid
    inner = (swish * up_value).astype(jnp.bfloat16)
    inner_ref[...] = inner
    gate_grad = inner_grad * up_value * (gate_sigmoid * (1.0 + gate_value * (1.0 - gate_sigmoid)))
    grad_ref[:, :part] = gate_grad.astype(jnp.bfloat16)
    grad_ref[:, part:] = (inner_grad * swish).astype(jnp.bfloat16)
    back_ref[:, :width] = dot_nt(grad_ref[...], gate_up).astype(back_ref.dtype)
    feed_ref[:, :width] = dot_nt(inner, down).astype(feed_ref.dtype)


def weight_grad_kernel(count, *refs):
    rows, cots = refs[:count], refs[count : 2 * count]
    inners, grads = refs[2 * count : 3 * count], refs[3 * count : 4 * count]
    out_ref = refs[4 * count]
    width = out_ref.shape[0]
    step = pl.program_id(0)

    @pl.when(step < 2)
    def _():
        out_ref[...] = sum(dot_tn(a[:, :width], b[...]) for a, b in zip(rows, grads)).astype(jnp.bfloat16)

    @pl.when(step == 2)
    def _():
        out_ref[...] = sum(dot_tn(a[:, :width], b[...]) for a, b in zip(cots, inners)).astype(jnp.bfloat16)


def weight_grads(width, rows, cots, inners, grads):
    count, size, part = len(rows), rows[0].shape[0], inners[0].shape[1]
    once = [pl.BlockSpec((size, rows[0].shape[1]), lambda j: (0, 0))] * (2 * count)
    once += [pl.BlockSpec((size, part), lambda j: (0, 0))] * count
    turns = [pl.BlockSpec((size, part), lambda j: (0, jnp.minimum(j, 1)))] * count
    return pl.pallas_call(
        functools.partial(weight_grad_kernel, count),
        grid=(3,),
        in_specs=once + turns,
        out_specs=pl.BlockSpec((width, part), lambda j: (0, j)),
        out_shape=jax.ShapeDtypeStruct((width, 3 * part), jnp.bfloat16),
        compiler_params=pltpu.CompilerParams(vmem_limit_bytes=56 * 2**20),
        cost_estimate=pl.CostEstimate(
            flops=6 * count * size * width * part,
            bytes_accessed=count * size * (4 * width + 6 * part) + 6 * width * part,
            transcendentals=0,
        ),
        name="weight_grads",
    )(*rows, *cots, *inners, *grads)


def matmul(spec, left, right):
    return jnp.einsum(spec, left, right, preferred_element_type=jnp.float32)


def pull(values, axis, ahead):
    count = lax.axis_size(axis)
    return lax.ppermute(values, axis, [((i + ahead) % count, i) for i in range(count)])


def swap_ends(values):
    count = lax.axis_size("ctx")
    return lax.ppermute(values, "ctx", [(i, count - 1 - i) for i in range(count)])


def spread(values, axis):
    return [values] + [pull(values, axis, ahead) for ahead in range(1, lax.axis_size(axis))]


def gather(values, axis):
    count = lax.axis_size(axis)
    ahead = jnp.stack(spread(values, axis))
    return lax.dynamic_slice_in_dim(
        jnp.concatenate([ahead, ahead]), count - lax.axis_index(axis), count, 0
    )


def collect(parts, axis):
    received = [parts[0]]
    for ahead in range(1, len(parts)):
        received.append(pull(parts[ahead].astype(jnp.bfloat16), axis, len(parts) - ahead))
    return received


def total(parts):
    return sum(part.astype(jnp.float32) for part in parts)


def reduce_blocks(values, axis, dim):
    count = lax.axis_size(axis)
    at = lax.axis_index(axis)
    blocks = [
        lax.dynamic_index_in_dim(values, (at + ahead) % count, dim, keepdims=False)
        for ahead in range(count)
    ]
    return total(collect(blocks, axis)).astype(jnp.bfloat16)


def reduce_to(values, axis, base):
    count, at = lax.axis_size(axis), lax.axis_index(axis)
    size = values.shape[0]
    summed = 0.0
    for ahead in range(count):
        target = jnp.clip((at + ahead) % count - base, 0, size - 1)
        block = lax.dynamic_index_in_dim(values, target, 0, keepdims=False)
        if ahead:
            ways = [(i, (i + ahead) % count) for i in range(count)]
            block = lax.ppermute(block, axis, [w for w in ways if base <= w[1] < base + size])
        summed = summed + block.astype(jnp.float32)
    return summed.astype(jnp.bfloat16)


def place_kernel(seq_ref, chunk_ref, in_ref, out_ref):
    out_ref[...] = in_ref[...].astype(out_ref.dtype)


def place_rows(stacked, seqs, chunks, seq_count, chunk_count, kind):
    pieces, width, chunk = stacked.shape
    return pl.pallas_call(
        place_kernel,
        out_shape=jax.ShapeDtypeStruct((seq_count, width, chunk_count * chunk), kind),
        grid_spec=pltpu.PrefetchScalarGridSpec(
            num_scalar_prefetch=2,
            grid=(pieces,),
            in_specs=[pl.BlockSpec((1, width, chunk), lambda i, s, c: (i, 0, 0))],
            out_specs=pl.BlockSpec((1, width, chunk), lambda i, s, c: (s[i], 0, c[i])),
        ),
        name="place_rows",
    )(seqs, chunks, stacked)


def shards(tokens, gains, qkv_weight, out_weight, gate_weight, up_weight, down_weight, cotangent):
    seq_count, span_len, width = tokens.shape
    ctx_count, sub_count = lax.axis_size("ctx"), lax.axis_size("sub")
    pair_count = ctx_count * sub_count
    chunk = span_len // (2 * sub_count)
    row_count = 2 * chunk
    owners = lax.axis_size(("shard", "ctx"))
    tensor_count = lax.axis_size(("seq", "sub"))
    everyone = ("seq", "sub", "shard", "ctx")
    own_seq, own_sub, own_ctx = lax.axis_index("seq"), lax.axis_index("sub"), lax.axis_index("ctx")
    is_low = own_ctx < ctx_count // 2
    own_pair = jnp.where(
        is_low,
        2 * sub_count * own_ctx + own_sub,
        2 * pair_count - 1 - 2 * sub_count * own_ctx - own_sub,
    ).astype(jnp.int32)

    def take_rows(values):
        span = lax.dynamic_index_in_dim(values, own_seq, 0, keepdims=False)
        kept = lax.dynamic_slice_in_dim(span, own_sub * chunk, chunk, 0)
        moved = lax.dynamic_slice_in_dim(span, (2 * sub_count - 1 - own_sub) * chunk, chunk, 0)
        return kept, moved

    def in_order(kept, moved):
        return jnp.where(is_low, jnp.concatenate([kept, moved]), jnp.concatenate([moved, kept]))

    def owner_sums(grad, cols, base):
        count = grad.shape[1] // cols
        grad = jnp.transpose(grad.reshape(grad.shape[0], count, cols), (1, 0, 2))
        grad = grad.reshape(count // ctx_count, ctx_count, -1, cols)
        here = reduce_blocks(grad, "shard", 0) if base is None else reduce_to(grad, "shard", base)
        return reduce_blocks(here, "ctx", 0)

    def deliver(home, kind):
        stacked = jnp.concatenate(
            [part for seq_rows in spread(home, "seq") for part in spread(seq_rows, "sub")]
        )
        seqs, chunks = [], []
        for seq_ahead in range(seq_count):
            for sub_ahead in range(sub_count):
                sub = (own_sub + sub_ahead) % sub_count
                seqs += [(own_seq + seq_ahead) % seq_count] * 2
                chunks += [sub, 2 * sub_count - 1 - sub]
        placed = place_rows(
            stacked,
            jnp.stack(seqs).astype(jnp.int32),
            jnp.stack(chunks).astype(jnp.int32),
            seq_count,
            2 * sub_count,
            kind,
        )
        return jnp.transpose(placed, (0, 2, 1))

    def back_home(columns):
        low, high = columns[:, :chunk], columns[:, chunk:]
        kept = jnp.where(is_low, low, high)
        moved = swap_ends(jnp.where(is_low, high, low))
        return jnp.stack([kept, moved])

    tile_rows, tile_cols = qkv_weight.shape
    gain_part = gains.shape[1]
    first_tile = jnp.concatenate(
        [qkv_weight, jnp.pad(gains, ((0, 0), (0, tile_cols - gain_part)))], axis=0
    )
    first_all = lax.all_gather(first_tile, everyone, axis=0, tiled=False)
    qkv_cols = owners * tile_cols
    padded_cols = -(-qkv_cols // LANES) * LANES
    qkv_all = assemble(first_all, tensor_count, tile_rows, padded_cols)
    gain_all = (
        jnp.transpose(first_all[:owners, tile_rows:, :gain_part], (1, 0, 2))
        .reshape(2, 1, width)
        .astype(jnp.float32)
    )
    gain_one, gain_two = gain_all[0], gain_all[1]
    out_rows, out_cols = out_weight.shape
    out_tiles = gather(gather(gather(gather(out_weight, "ctx"), "shard"), "seq"), "sub")
    out_heads = jnp.pad(
        jnp.transpose(out_tiles, (1, 0, 4, 2, 3, 5)).reshape(HEADS, HEAD_DIM, width),
        ((0, 0), (HEAD_DIM, 0), (0, 0)),
    )

    qkv_all, out_heads = lax.optimization_barrier((qkv_all, out_heads))

    kept_tokens, moved_tokens = take_rows(tokens)
    kept_cot, moved_cot = take_rows(cotangent)
    rows_low = in_order(kept_tokens, swap_ends(moved_tokens))
    wide = -(-width // LANES) * LANES
    step = jnp.arange(chunk, dtype=jnp.int32)
    positions = jnp.concatenate([own_pair * chunk + step, (2 * pair_count - 1 - own_pair) * chunk + step])
    half_dim = HEAD_DIM // 2
    frequency = rope_base ** (-2.0 * jnp.arange(half_dim, dtype=jnp.float32) / HEAD_DIM)
    angles = positions.astype(jnp.float32)[:, None] * frequency[None, :]
    cosine, sine = jnp.cos(angles), jnp.sin(angles)
    cosine_table = jnp.concatenate([cosine] * 4, axis=1)
    sine_table = jnp.concatenate([-sine, sine] * 2, axis=1)

    def shape(*dims, kind=jnp.bfloat16):
        return jax.ShapeDtypeStruct(dims, kind)

    head_rows = (KV_HEADS, 2, GROUP, chunk, LANES)
    qkv_flops = 2 * row_count * width * padded_cols
    query_heads, pair_own, normed = row_call(
        project_kernel,
        chunk,
        [(rows_low, 0), (gain_one, 1), (qkv_all, 1), (cosine_table, 0), (sine_table, 0)],
        [(shape(*head_rows), 0), (shape(KV_HEADS, row_count, LANES), 0), (shape(row_count, width), 0)],
        "project",
        qkv_flops,
    )
    query_heads = query_heads.reshape(KV_HEADS, GROUP * row_count, LANES)
    cuts = [slice(0, 3), slice(3, KV_HEADS)]
    pairs = []
    for cut in cuts:
        own_part = pair_own[cut]
        if pairs:
            own_part, pairs[-1] = lax.optimization_barrier((own_part, pairs[-1]))
        pairs.append(lax.all_gather(own_part, ("ctx", "sub"), axis=1, tiled=True))
    hidden_part = gate_weight.shape[1]
    place = own_pair[None]
    first = attention_forward(place, query_heads, pairs[0], 0, ctx_count, sub_count, chunk, GROUP)
    ffn_tile = jnp.concatenate([gate_weight, up_weight, down_weight.T], axis=1)
    first, pairs[1], ffn_tile, moved_low = lax.optimization_barrier(
        (first, pairs[1], ffn_tile, moved_cot.astype(jnp.bfloat16))
    )
    swapped_cot = swap_ends(moved_low)
    ffn_all = lax.all_gather(ffn_tile, ("shard", "ctx"), axis=0, tiled=True)
    second = attention_forward(
        place, query_heads, pairs[1], cuts[1].start, ctx_count, sub_count, chunk, GROUP
    )
    second, swapped_cot = lax.optimization_barrier((second, swapped_cot))
    attended = [rows.reshape((-1,) + head_rows[1:]) for rows in (first, second)]
    cot = in_order(kept_cot, swapped_cot.astype(jnp.float32))
    far_cots = spread(jnp.pad(cot.astype(jnp.bfloat16), ((0, 0), (0, wide - width))), "seq")
    cot_low = [spread(seq_rows, "sub") for seq_rows in far_cots]
    mix_flops = 4 * row_count * width * width
    hidden, normed_own, attn_low = row_call(
        functools.partial(mix_kernel, len(attended)),
        chunk,
        [(rows, 0) for rows in attended]
        + [(out_heads, 1), (rows_low, 0), (gain_two, 1)],
        [
            (shape(row_count, width, kind=jnp.float32), 0),
            (shape(row_count, wide), 0),
            (shape(row_count, width), 0),
        ],
        "mix",
        mix_flops,
    )
    far_rows = spread(normed_own, "seq")
    feeds, backs, pieces = [], [], []
    for seq_ahead, near_rows in enumerate(far_rows):
        if seq_ahead:
            near_rows, backs[-1] = lax.optimization_barrier((near_rows, backs[-1]))
        seq_feeds, seq_backs = [], []
        for sub_ahead, rows in enumerate(spread(near_rows, "sub")):
            kind = jnp.bfloat16 if sub_ahead else jnp.float32
            cots = cot_low[seq_ahead][sub_ahead]
            back, feed, inner, grad = row_call(
                feed_kernel,
                chunk,
                [(rows, 0), (cots, 0), (ffn_all, 1)],
                [
                    (shape(row_count, wide, kind=kind), 0),
                    (shape(row_count, wide, kind=kind), 0),
                    (shape(row_count, hidden_part), 0),
                    (shape(row_count, 2 * hidden_part), 0),
                ],
                "feed",
                8 * row_count * width * 2 * hidden_part,
            )
            seq_feeds.append(feed)
            seq_backs.append(back)
            pieces.append((rows, cots, inner, grad))
        backs.append(collect(seq_backs, "sub"))
        feeds.append(collect(seq_feeds, "sub"))
    backs = backs[0] + collect([backs[0]] + [total(parts) for parts in backs[1:]], "seq")[1:]
    feed_sent = [total(parts).astype(jnp.bfloat16) for parts in feeds[1:]]
    ffn_grad = weight_grads(width, *zip(*pieces))
    backs, ffn_grad = lax.optimization_barrier((backs, ffn_grad))
    ffn_out = lax.psum_scatter(ffn_grad, ("shard", "ctx"), scatter_dimension=0, tiled=True)
    hidden_grad, hidden_low, grad_heads, extra, gain_two_grad = row_call(
        functools.partial(unmix_kernel, len(backs), len(attended)),
        chunk,
        [(part, 0) for part in backs + attended]
        + [(hidden, 0), (cot, 0), (gain_two, 1), (out_heads, 1)],
        [
            (shape(row_count, width, kind=jnp.float32), 0),
            (shape(row_count, width), 0),
            (shape(*head_rows), 0),
            (shape(*head_rows), 0),
            (shape(8, width, kind=jnp.float32), 1),
        ],
        "unmix",
        mix_flops,
    )
    flat = (KV_HEADS, GROUP * row_count, LANES)
    grad_heads, extra = grad_heads.reshape(flat), extra.reshape(flat)
    grad_heads, feed_sent = lax.optimization_barrier((grad_heads, feed_sent))
    feeds = feeds[0] + collect([feeds[0]] + feed_sent, "seq")[1:]
    filled = attention_backward(
        place, query_heads, grad_heads, extra, pairs[0], 0, (), ctx_count, sub_count, chunk, GROUP
    )
    filled, feeds = lax.optimization_barrier((filled, feeds))
    (block_low,) = row_call(
        functools.partial(block_kernel, len(feeds)),
        chunk,
        [(part, 0) for part in feeds] + [(hidden, 0)],
        [(shape(width, row_count), 0)],
        "block",
        0,
    )
    block_low, filled = lax.optimization_barrier((block_low, filled))
    block_home = back_home(block_low)
    query_grad, pair_grad = attention_backward(
        place,
        query_heads,
        grad_heads,
        extra,
        pairs[1],
        cuts[1].start,
        filled,
        ctx_count,
        sub_count,
        chunk,
        GROUP,
    )
    block_home, query_grad, pair_grad, hidden_low, ffn_out = lax.optimization_barrier(
        (block_home, query_grad, pair_grad, hidden_low, ffn_out)
    )
    pair_grad = lax.psum_scatter(pair_grad, ("ctx", "sub"), scatter_dimension=1, tiled=True)
    query_grad = query_grad.reshape(head_rows)
    half_cols, extra_rows = qkv_cols // 2, 16
    (proj_early,) = row_call(
        early_kernel,
        chunk,
        [(query_grad, 0), (cosine_table, 0), (sine_table, 0)],
        [(shape(row_count, -(-half_cols // LANES) * LANES), 0)],
        "early",
        0,
    )
    early_grad = jnp.concatenate(
        [
            matmul("rf,re->fe", attn_low, hidden_low).astype(jnp.bfloat16),
            matmul("rd,re->de", normed, proj_early).astype(jnp.bfloat16),
        ],
        axis=1,
    )
    early_grad = early_grad.reshape(seq_count, sub_count, tile_rows, early_grad.shape[1])
    early_grad = reduce_blocks(reduce_blocks(early_grad, "sub", 1), "seq", 0)
    out_out = owner_sums(early_grad[:, :width], out_cols, None)
    qkv_early = owner_sums(early_grad[:, width : width + half_cols], tile_cols, 0)
    block_out = deliver(block_home, jnp.bfloat16)
    pair_grad, out_out, qkv_early, block_out = lax.optimization_barrier(
        (pair_grad, out_out, qkv_early, block_out)
    )
    out_out = out_out.astype(jnp.float32)
    proj_grad, input_low, gain_one_grad = row_call(
        finish_kernel,
        chunk,
        [
            (query_grad, 0),
            (pair_grad, 0),
            (cosine_table, 0),
            (sine_table, 0),
            (qkv_all, 1),
            (rows_low, 0),
            (hidden_grad, 0),
            (gain_one, 1),
        ],
        [
            (shape(row_count, padded_cols), 0),
            (shape(width, row_count), 0),
            (shape(8, width, kind=jnp.float32), 1),
        ],
        "finish",
        qkv_flops,
    )
    input_grad = deliver(back_home(input_low), jnp.float32)

    late_cols = qkv_cols - half_cols
    qkv_grad = matmul("rd,re->de", normed, proj_grad[:, half_cols:qkv_cols]).astype(jnp.bfloat16)
    gains_grad = jnp.concatenate([gain_one_grad[:1], gain_two_grad[:1]]).astype(jnp.bfloat16)
    folded = -(-width // late_cols)
    gains_rows = jnp.pad(gains_grad, ((0, 0), (0, folded * late_cols - width)))
    gains_rows = jnp.pad(
        gains_rows.reshape(2 * folded, late_cols), ((0, extra_rows - 2 * folded), (0, 0))
    )
    last = jnp.concatenate(
        [
            qkv_grad.reshape(seq_count, sub_count, tile_rows, late_cols),
            jnp.broadcast_to(gains_rows, (seq_count, sub_count) + gains_rows.shape),
        ],
        axis=2,
    )
    last = reduce_blocks(reduce_blocks(last, "sub", 1), "seq", 0)
    gains_sum = last[tile_rows : tile_rows + 2 * folded].reshape(2, folded * late_cols)[:, :width]
    gains_out = reduce_blocks(
        reduce_blocks(
            jnp.transpose(gains_sum.reshape(2, owners, gain_part), (1, 0, 2)).reshape(
                owners // ctx_count, ctx_count, 2, gain_part
            ),
            "shard",
            0,
        ),
        "ctx",
        0,
    ).astype(jnp.float32)
    qkv_late = owner_sums(last[:tile_rows], tile_cols, owners // ctx_count // 2)
    is_early = lax.axis_index("shard") < owners // ctx_count // 2
    qkv_out = jnp.where(is_early, qkv_early, qkv_late).astype(jnp.float32)
    ffn_out = ffn_out.astype(jnp.float32)
    return (
        block_out,
        input_grad,
        gains_out,
        qkv_out,
        out_out,
        ffn_out[:, :hidden_part],
        ffn_out[:, hidden_part : 2 * hidden_part],
        ffn_out[:, 2 * hidden_part :].T,
    )


def solution(mesh):
    shard_count, ctx_count, tensor_count = (mesh.shape[axis] for axis in ("shard", "ctx", "tensor"))

    def run(tokens, *rest):
        seq_count = tokens.shape[0] // shard_count
        split = Mesh(
            mesh.devices.reshape(shard_count, ctx_count, seq_count, tensor_count // seq_count),
            ("shard", "ctx", "seq", "sub"),
        )
        rows = P("shard", "ctx", None)
        pool = ("shard", "ctx")
        team = ("seq", "sub")
        weights = (P(None, pool), P(team, pool), P(team, pool), P(pool, team), P(pool, team), P(team, pool))
        return jax.shard_map(
            shards,
            mesh=split,
            in_specs=(rows,) + weights + (rows,),
            out_specs=(rows, rows) + weights,
            check_vma=False,
        )(tokens, *rest)

    return run
```

```python
import functools

import jax
import jax.numpy as jnp
from jax import lax
from jax.experimental import pallas as pl
from jax.experimental.pallas import tpu as pltpu
from jax.sharding import Mesh
from jax.sharding import PartitionSpec as P

HEADS = 15
KV_HEADS = 5
HEAD_DIM = 64
GROUP = 3
LANES = 128
HALF = HEAD_DIM


epsilon = 1e-05
rope_base = 100000.0
masked_score = -1e30


def pair_place(pair, ctx_count, sub):
    turn = pair // (2 * sub)
    spot = pair % (2 * sub)
    low = spot < sub
    return jnp.where(low, turn * sub + spot, (ctx_count - 1 - turn) * sub + 2 * sub - 1 - spot)


def dot_nt(a, b):
    return lax.dot_general(a, b, (((1,), (1,)), ((), ())), preferred_element_type=jnp.float32)


def dot_nn(a, b):
    return lax.dot_general(a, b, (((1,), (0,)), ((), ())), preferred_element_type=jnp.float32)


def dot_tn(a, b):
    return lax.dot_general(a, b, (((0,), (0,)), ((), ())), preferred_element_type=jnp.float32)


def causal(rows, cols, chunk, key_axis):
    shape = (rows, cols)
    query_axis = 1 - key_axis
    query = lax.broadcasted_iota(jnp.int32, shape, query_axis)
    key = lax.broadcasted_iota(jnp.int32, shape, key_axis)
    return key <= lax.rem(query, chunk)


def forward_kernel(ctx_count, sub, chunk, group, pair_ref, q_ref, kv_ref, out_ref, top, total):
    pairs = ctx_count * sub
    own = pair_ref[0]
    part = group * chunk
    lanes = lambda rows: lax.broadcasted_iota(jnp.int32, (rows, LANES), 1)

    def load(place, slot, count):
        return kv_ref[0, pl.ds(pl.multiple_of(place * 2 * chunk + slot * chunk, chunk), count * chunk), :]

    def weighted(powers, kv):
        ones = jnp.where(lanes(kv.shape[0]) < HALF, jnp.ones_like(kv), kv)
        return dot_nn(powers, ones)

    def update(start, rows, kv, first, mask):
        scores = dot_nt(q_ref[0, start : start + rows, :], kv)
        if mask is not None:
            scores = jnp.where(mask, scores, masked_score)
        best = jnp.max(scores, axis=1, keepdims=True)
        spot = slice(start, start + rows)
        if first:
            top[spot, :] = jnp.broadcast_to(best, (rows, LANES))
            powers = jnp.exp(scores - best).astype(jnp.bfloat16)
            total[spot, :] = weighted(powers, kv)
        else:
            old = top[spot, :]
            new = jnp.maximum(old, best)
            powers = jnp.exp(scores - new[:, :1]).astype(jnp.bfloat16)
            total[spot, :] = total[spot, :] * jnp.exp(old - new) + weighted(powers, kv)
            top[spot, :] = new

    place = pair_place(own, ctx_count, sub)
    near = load(place, 0, 1)
    both = load(place, 0, 2)
    near_mask = causal(chunk, chunk, chunk, 1)
    columns = lax.broadcasted_iota(jnp.int32, (chunk, 2 * chunk), 1)
    queries = lax.broadcasted_iota(jnp.int32, (chunk, 2 * chunk), 0)
    both_mask = columns <= queries + chunk
    for head in range(group):
        update(head * chunk, chunk, near, True, near_mask)
        update(part + head * chunk, chunk, both, True, both_mask)

    def sweep(first, last, count, start, heads):
        def load_at(pair):
            return load(pair_place(pair, ctx_count, sub), 0, count)

        def absorb(kv):
            for head in range(heads):
                update(start + head * chunk, chunk, kv, False, None)

        twos = (last - first) // 2

        @pl.loop(0, twos)
        def _(step):
            pair = first + 2 * step
            absorb(jnp.concatenate([load_at(pair), load_at(pair + 1)], axis=0))

        @pl.when(first + 2 * twos < last)
        def _():
            absorb(load_at(last - 1))

    sweep(0, own, 1, 0, 2 * group)
    sweep(own + 1, pairs, 2, part, group)

    for head in range(2 * group):
        spot = slice(head * chunk, (head + 1) * chunk)
        sums = total[spot, :]
        count = sums[:, :1]
        out_ref[0, spot, :] = jnp.where(
            lanes(chunk) < HALF, top[spot, :] + jnp.log(count), sums / count
        )


def attention_forward(own_pair, queries, pairs_all, ctx_count, sub, chunk, group):
    rows = queries.shape[1]
    heads, length, _ = pairs_all.shape
    grid_spec = pltpu.PrefetchScalarGridSpec(
        num_scalar_prefetch=1,
        grid=(heads,),
        in_specs=[
            pl.BlockSpec((1, rows, LANES), lambda h, p: (h, 0, 0)),
            pl.BlockSpec((1, length, LANES), lambda h, p: (h, 0, 0)),
        ],
        out_specs=pl.BlockSpec((1, rows, LANES), lambda h, p: (h, 0, 0)),
        scratch_shapes=[
            pltpu.VMEM((rows, LANES), jnp.float32),
            pltpu.VMEM((rows, LANES), jnp.float32),
        ],
    )
    cost = heads * rows * length // 2
    return pl.pallas_call(
        functools.partial(forward_kernel, ctx_count, sub, chunk, group),
        out_shape=jax.ShapeDtypeStruct((heads, rows, LANES), jnp.float32),
        grid_spec=grid_spec,
        compiler_params=pltpu.CompilerParams(vmem_limit_bytes=48 * 2**20),
        cost_estimate=pl.CostEstimate(
            flops=cost * 4 * HALF, bytes_accessed=heads * LANES * (rows * 6 + length * 2), transcendentals=cost
        ),
        name="attention_forward",
    )(own_pair, queries, pairs_all)


def backward_kernel(
    ctx_count, sub, chunk, group, pair_ref, q_ref, cot_ref, extra_ref, kv_ref, dq_ref, dkv_ref
):
    pairs = ctx_count * sub
    own = pair_ref[0]
    part = group * chunk

    def minus(rows, low, high):
        lane = lax.broadcasted_iota(jnp.int32, (rows, LANES), 1)
        return jnp.where((lane >= low) & (lane < high), -1.0, 0.0).astype(jnp.bfloat16)

    def load(place, slot, count):
        base = pl.multiple_of(place * 2 * chunk + slot * chunk, chunk)
        return kv_ref[0, pl.ds(base, count * chunk), :]

    def step(start, rows, kv, first, mask):
        keys = kv.shape[0]
        key_side = jnp.concatenate([kv, minus(keys, 0, 3)], axis=1)
        value_side = jnp.concatenate([kv, minus(keys, 3, 6)], axis=1)
        pair_sum = None
        for at in range(start, start + rows, chunk):
            spot = slice(at, at + chunk)
            query = q_ref[0, spot, :]
            cot = cot_ref[0, spot, :]
            extra = extra_ref[0, spot, :]
            powers = jnp.exp(dot_nt(key_side, jnp.concatenate([query, extra], axis=1)))
            if mask is not None:
                powers = jnp.where(mask, powers, 0.0)
            slope = dot_nt(value_side, jnp.concatenate([cot, extra], axis=1))
            grads = (powers * slope).astype(jnp.bfloat16)
            powers = powers.astype(jnp.bfloat16)
            term = dot_nn(powers, cot) + dot_nn(grads, query)
            pair_sum = term if pair_sum is None else pair_sum + term
            moved = dot_tn(grads, kv)
            if first:
                dq_ref[0, spot, :] = moved
            else:
                dq_ref[0, spot, :] += moved
        return pair_sum

    def store(place, slot, count, value):
        base = pl.multiple_of(place * 2 * chunk + slot * chunk, chunk)
        dkv_ref[0, pl.ds(base, count * chunk), :] = value.astype(jnp.bfloat16)

    place = pair_place(own, ctx_count, sub)
    near_mask = causal(chunk, chunk, chunk, 0)
    keys = lax.broadcasted_iota(jnp.int32, (2 * chunk, chunk), 0)
    queries = lax.broadcasted_iota(jnp.int32, (2 * chunk, chunk), 1)
    far = step(part, part, load(place, 0, 2), True, keys <= queries + chunk)
    near = step(0, part, load(place, 0, 1), True, near_mask)
    store(place, 0, 1, far[:chunk] + near)
    store(place, 1, 1, far[chunk:])

    def sweep(first, last, count, start, rows):
        twos = (last - first) // 2

        def put(at, value):
            store(at, 0, count, value)
            if count == 1:
                store(at, 1, 1, jnp.zeros((chunk, LANES), jnp.float32))

        @pl.loop(0, twos)
        def _(turn):
            one = pair_place(first + 2 * turn, ctx_count, sub)
            two = pair_place(first + 2 * turn + 1, ctx_count, sub)
            kv = jnp.concatenate([load(one, 0, count), load(two, 0, count)], axis=0)
            sums = step(start, rows, kv, False, None)
            put(one, sums[: count * chunk])
            put(two, sums[count * chunk :])

        @pl.when(first + 2 * twos < last)
        def _():
            at = pair_place(last - 1, ctx_count, sub)
            put(at, step(start, rows, load(at, 0, count), False, None))

    sweep(0, own, 1, 0, 2 * part)
    sweep(own + 1, pairs, 2, part, part)


def attention_backward(
    own_pair, queries, cots, extra, pairs_all, base, stop, filled, ctx_count, sub, chunk, group
):
    total_heads, rows, _ = queries.shape
    heads, length = stop - base, pairs_all.shape[1]
    row_spec = pl.BlockSpec((1, rows, LANES), lambda h, p: (base + h, 0, 0))
    long_spec = pl.BlockSpec((1, length, LANES), lambda h, p: (base + h, 0, 0))
    cost = heads * rows * length // 2
    kernel = functools.partial(backward_kernel, ctx_count, sub, chunk, group)

    def filling(pair_ref, q_ref, cot_ref, extra_ref, kv_ref, old_dq_ref, old_dkv_ref, dq_ref, dkv_ref):
        kernel(pair_ref, q_ref, cot_ref, extra_ref, kv_ref, dq_ref, dkv_ref)

    return pl.pallas_call(
        filling if filled else kernel,
        out_shape=(
            jax.ShapeDtypeStruct((total_heads, rows, LANES), jnp.float32),
            jax.ShapeDtypeStruct((total_heads, length, LANES), jnp.bfloat16),
        ),
        grid_spec=pltpu.PrefetchScalarGridSpec(
            num_scalar_prefetch=1,
            grid=(heads,),
            in_specs=[row_spec, row_spec, row_spec, long_spec]
            + [pl.BlockSpec(memory_space=pl.ANY)] * len(filled),
            out_specs=(row_spec, long_spec),
        ),
        input_output_aliases={5 + at: at for at in range(len(filled))},
        compiler_params=pltpu.CompilerParams(vmem_limit_bytes=48 * 2**20),
        cost_estimate=pl.CostEstimate(
            flops=cost * 10 * HALF, bytes_accessed=heads * LANES * (rows * 10 + length * 4), transcendentals=cost
        ),
        name="attention_backward",
    )(own_pair, queries, cots, extra, pairs_all, *filled)


def three_parts(values):
    high = values.astype(jnp.bfloat16)
    rest = values - high.astype(jnp.float32)
    middle = rest.astype(jnp.bfloat16)
    low = (rest - middle.astype(jnp.float32)).astype(jnp.bfloat16)
    return [high, middle, low]


def lane_index(rows):
    return lax.broadcasted_iota(jnp.int32, (rows, LANES), 1)


def swap_halves(tile):
    lane = lane_index(tile.shape[0])
    quarter = HALF // 2
    return jnp.where(
        lax.rem(lane, HALF) < quarter,
        pltpu.roll(tile, LANES - quarter, 1),
        pltpu.roll(tile, quarter, 1),
    )


def normalise(values):
    inv_rms = lax.rsqrt(jnp.mean(values * values, axis=-1, keepdims=True) + epsilon)
    return values * inv_rms, inv_rms


def norm_back(upstream, values, gain_row):
    unit_rows, inv_rms = normalise(values)
    shaped = upstream * gain_row
    inner_mean = jnp.mean(shaped * unit_rows, axis=-1, keepdims=True)
    return inv_rms * (shaped - unit_rows * inner_mean), upstream * unit_rows


def assemble_kernel(rows, in_ref, out_ref):
    tiles = [in_ref[at, :rows, :] for at in range(in_ref.shape[0])]
    used = len(tiles) * tiles[0].shape[1]
    if used < out_ref.shape[1]:
        tiles.append(jnp.zeros((rows, out_ref.shape[1] - used), tiles[0].dtype))
    out_ref[...] = jnp.concatenate(tiles, axis=1)


def assemble(gathered, teams, rows, cols):
    count = gathered.shape[0] // teams
    return pl.pallas_call(
        functools.partial(assemble_kernel, rows),
        grid=(teams,),
        in_specs=[pl.BlockSpec((count,) + gathered.shape[1:], lambda t: (t, 0, 0))],
        out_specs=pl.BlockSpec((rows, cols), lambda t: (t, 0)),
        out_shape=jax.ShapeDtypeStruct((teams * rows, cols), gathered.dtype),
        compiler_params=pltpu.CompilerParams(vmem_limit_bytes=48 * 2**20),
        name="assemble",
    )(gathered)


def project_kernel(token_ref, gain_ref, weight_ref, cos_ref, sin_ref, q_ref, kv_ref, normed_ref):
    rows = token_ref.shape[0]
    unit_rows, _ = normalise(token_ref[...].astype(jnp.float32))
    normed = (unit_rows * gain_ref[...]).astype(jnp.bfloat16)
    normed_ref[...] = normed
    projected = dot_nn(normed, weight_ref[...])
    cos, sin = cos_ref[...], sin_ref[...]
    low = lane_index(rows) < HALF

    def tile(column):
        return projected[:, column // 2 * LANES : (column // 2 + 1) * LANES]

    def turned(column):
        raw = tile(column)
        out = raw * cos + swap_halves(raw) * sin
        return pltpu.roll(out, HALF, 1) if column % 2 else out

    for head in range(HEADS):
        query = jnp.where(low, turned(head) * HEAD_DIM ** (-0.5), 0.0)
        q_ref[head // GROUP, 0, head % GROUP] = query.astype(jnp.bfloat16)
    for head in range(KV_HEADS):
        key = turned(HEADS + head)
        column = HEADS + KV_HEADS + head
        value = tile(column) if column % 2 else pltpu.roll(tile(column), HALF, 1)
        kv_ref[head] = jnp.where(low, key, value).astype(jnp.bfloat16)


def whole(shape):
    return pl.BlockSpec(shape, lambda c: (0,) * len(shape))


def row_call(kernel, chunk, ins, outs, name, flops):
    def spec(array):
        shape = array.shape
        if len(shape) == 5:
            return pl.BlockSpec((shape[0], 1) + shape[2:], lambda c: (0, c, 0, 0, 0))
        if len(shape) == 3:
            return pl.BlockSpec((shape[0], chunk, shape[2]), lambda c: (0, c, 0))
        if shape[0] != 2 * chunk:
            return pl.BlockSpec((shape[0], chunk), lambda c: (0, c))
        return pl.BlockSpec((chunk, shape[1]), lambda c: (c, 0))

    moved = sum(a.size * a.dtype.itemsize for a, _ in ins) + sum(o.size * o.dtype.itemsize for o, _ in outs)
    return pl.pallas_call(
        kernel,
        grid=(2,),
        in_specs=[whole(a.shape) if fixed else spec(a) for a, fixed in ins],
        out_specs=[whole(o.shape) if fixed else spec(o) for o, fixed in outs],
        out_shape=[o for o, _ in outs],
        compiler_params=pltpu.CompilerParams(vmem_limit_bytes=56 * 2**20),
        cost_estimate=pl.CostEstimate(flops=flops, bytes_accessed=moved, transcendentals=0),
        name=name,
    )(*[a for a, _ in ins])


def pick(refs, head):
    group, at = head // GROUP, 0
    for ref in refs:
        if group < at + ref.shape[0]:
            return ref[group - at, 0, head % GROUP]
        at += ref.shape[0]


def pick_pair(refs, group):
    at = 0
    for ref in refs:
        if group < at + ref.shape[0]:
            return ref[group - at]
        at += ref.shape[0]


def mix_kernel(count, *refs):
    attended_refs = refs[:count]
    weight_ref, token_ref, gain_ref, hidden_ref, normed_ref, attn_ref = refs[count:]
    total = token_ref[...].astype(jnp.float32)
    first = lane_index(token_ref.shape[0]) < HALF
    for head in range(HEADS):
        rows = pick(attended_refs, head)
        low = rows.astype(jnp.bfloat16)
        if head % 2:
            both = jnp.concatenate([low_before, low], axis=1)
            total = total + dot_nn(both, weight_ref[head - 1 : head + 1].reshape(2 * LANES, -1))
        elif head == HEADS - 1:
            total = total + dot_nn(low, weight_ref[head])
        low_before = low
        base = head // 2 * LANES
        if head % 2:
            both = jnp.where(first, pltpu.roll(before, HALF, 1), rows)
            attn_ref[:, base : base + LANES] = both.astype(jnp.bfloat16)
        elif head == HEADS - 1:
            alone = pltpu.roll(rows, HALF, 1)[:, :HALF]
            attn_ref[:, base : base + HALF] = alone.astype(jnp.bfloat16)
        before = rows
    hidden_ref[...] = total
    unit_rows, _ = normalise(total)
    normed_ref[:, : total.shape[1]] = (unit_rows * gain_ref[...]).astype(jnp.bfloat16)


def accumulate(ref, rows):
    summed = jnp.broadcast_to(jnp.sum(rows, axis=0, keepdims=True), ref.shape)

    @pl.when(pl.program_id(0) == 0)
    def _():
        ref[...] = summed

    @pl.when(pl.program_id(0) != 0)
    def _():
        ref[...] += summed


def unmix_kernel(count, parts, *refs):
    ups = refs[:count]
    attended_refs, refs = refs[count : count + parts], refs[count + parts :]
    (hidden_ref, cot_ref, gain_ref, weight_ref, grad_ref, low_ref, heads_ref, extra_ref, gain_grad_ref) = refs
    width = hidden_ref.shape[1]
    upstream = ups[0][:, :width].astype(jnp.float32)
    for ref in ups[1:]:
        upstream = upstream + ref[:, :width].astype(jnp.float32)
    back, gain_rows = norm_back(upstream, hidden_ref[...], gain_ref[...])
    accumulate(gain_grad_ref, gain_rows)
    hidden_grad = cot_ref[...] + back
    grad_ref[...] = hidden_grad
    hidden_low = hidden_grad.astype(jnp.bfloat16)
    low_ref[...] = hidden_low
    lane = lane_index(hidden_low.shape[0])
    for head in range(HEADS):
        spot = (head // GROUP, 0, head % GROUP)
        if head % 2 == 0:
            many = weight_ref[head : head + 2].reshape(-1, weight_ref.shape[2])
            cots_two = dot_nt(hidden_low, many).astype(jnp.bfloat16)
        side = head % 2 * LANES
        cots = cots_two[:, side : side + LANES]
        heads_ref[spot] = cots
        attended = pick(attended_refs, head)
        delta = jnp.sum(cots.astype(jnp.float32) * attended, axis=1, keepdims=True)
        base = jnp.where(lane < 3, attended[:, :1], jnp.where(lane < 6, delta, 0.0))
        high, middle, low = three_parts(base)
        part = lax.rem(lane, 3)
        extra_ref[spot] = jnp.where(
            part == 0,
            high.astype(jnp.float32),
            jnp.where(part == 1, middle.astype(jnp.float32), low.astype(jnp.float32)),
        ).astype(jnp.bfloat16)


def turn_back(dq_ref, dkv_ref, cos_ref, sin_ref, proj_ref):
    rows = cos_ref.shape[0]
    cos, sin = cos_ref[...], sin_ref[...]
    low = lane_index(rows) < HALF

    def half(column):
        if column < HEADS:
            return dq_ref[column // GROUP, 0, column % GROUP] * HEAD_DIM ** (-0.5), 0
        if column < HEADS + KV_HEADS:
            return dkv_ref[column - HEADS].astype(jnp.float32), 0
        if column < HEADS + 2 * KV_HEADS:
            return dkv_ref[column - HEADS - KV_HEADS].astype(jnp.float32), 1
        return jnp.zeros((rows, LANES), jnp.float32), 0

    def placed(column):
        value, side = half(column)
        return value if side == column % 2 else pltpu.roll(value, HALF, 1)

    for at in range(proj_ref.shape[1] // LANES):
        raw = jnp.where(low, placed(2 * at), placed(2 * at + 1))
        if 2 * at < HEADS + KV_HEADS:
            raw = raw * cos - swap_halves(raw) * sin
        proj_ref[:, at * LANES : (at + 1) * LANES] = raw.astype(jnp.bfloat16)


def early_kernel(dq_ref, cos_ref, sin_ref, proj_ref):
    turn_back(dq_ref, None, cos_ref, sin_ref, proj_ref)


def block_kernel(count, *refs):
    hidden_ref, out_ref = refs[count], refs[count + 1]
    rows = hidden_ref[...]
    for ref in refs[:count]:
        rows = rows + ref[:, : rows.shape[1]].astype(jnp.float32)
    out_ref[...] = jnp.transpose(rows).astype(jnp.bfloat16)


def finish_kernel(
    dq_ref, dkv_ref, cos_ref, sin_ref, weight_ref, token_ref, grad_ref, gain_ref,
    proj_ref, input_ref, gain_grad_ref,
):
    turn_back(dq_ref, dkv_ref, cos_ref, sin_ref, proj_ref)
    upstream = dot_nt(proj_ref[...], weight_ref[...])
    back, gain_rows = norm_back(upstream, token_ref[...].astype(jnp.float32), gain_ref[...])
    accumulate(gain_grad_ref, gain_rows)
    input_ref[...] = jnp.transpose(grad_ref[...] + back).astype(jnp.bfloat16)


def feed_kernel(count, *refs):
    weight_ref = refs[2 * count]
    for at in range(count):
        outs = refs[2 * count + 1 + 4 * at : 2 * count + 5 + 4 * at]
        feed_rows(refs[2 * at], refs[2 * at + 1], weight_ref, *outs)


def feed_rows(rows_ref, cot_ref, weight_ref, back_ref, feed_ref, inner_ref, grad_ref):
    part = inner_ref.shape[1]
    width = weight_ref.shape[0]
    rows, cots = rows_ref[:, :width], cot_ref[:, :width]
    gate_up, down = weight_ref[:, : 2 * part], weight_ref[:, 2 * part :]
    both = dot_nn(rows, gate_up)
    inner_grad = dot_nn(cots, down)
    gate_value, up_value = both[:, :part], both[:, part:]
    gate_sigmoid = jax.nn.sigmoid(gate_value)
    swish = gate_value * gate_sigmoid
    inner = (swish * up_value).astype(jnp.bfloat16)
    inner_ref[...] = inner
    gate_grad = inner_grad * up_value * (gate_sigmoid * (1.0 + gate_value * (1.0 - gate_sigmoid)))
    grad_ref[:, :part] = gate_grad.astype(jnp.bfloat16)
    grad_ref[:, part:] = (inner_grad * swish).astype(jnp.bfloat16)
    back_ref[:, :width] = dot_nt(grad_ref[...], gate_up).astype(back_ref.dtype)
    feed_ref[:, :width] = dot_nt(inner, down).astype(feed_ref.dtype)


def weight_grad_kernel(count, *refs):
    rows, cots = refs[:count], refs[count : 2 * count]
    inners, grads = refs[2 * count : 3 * count], refs[3 * count : 4 * count]
    out_ref = refs[4 * count]
    width = out_ref.shape[0]
    step = pl.program_id(0)

    @pl.when(step < 2)
    def _():
        out_ref[...] = sum(dot_tn(a[:, :width], b[...]) for a, b in zip(rows, grads)).astype(jnp.bfloat16)

    @pl.when(step == 2)
    def _():
        out_ref[...] = sum(dot_tn(a[:, :width], b[...]) for a, b in zip(cots, inners)).astype(jnp.bfloat16)


def weight_grads(width, rows, cots, inners, grads):
    count, size, part = len(rows), rows[0].shape[0], inners[0].shape[1]
    once = [pl.BlockSpec((size, rows[0].shape[1]), lambda j: (0, 0))] * (2 * count)
    once += [pl.BlockSpec((size, part), lambda j: (0, 0))] * count
    turns = [pl.BlockSpec((size, part), lambda j: (0, jnp.minimum(j, 1)))] * count
    return pl.pallas_call(
        functools.partial(weight_grad_kernel, count),
        grid=(3,),
        in_specs=once + turns,
        out_specs=pl.BlockSpec((width, part), lambda j: (0, j)),
        out_shape=jax.ShapeDtypeStruct((width, 3 * part), jnp.bfloat16),
        compiler_params=pltpu.CompilerParams(vmem_limit_bytes=56 * 2**20),
        cost_estimate=pl.CostEstimate(
            flops=6 * count * size * width * part,
            bytes_accessed=count * size * (4 * width + 6 * part) + 6 * width * part,
            transcendentals=0,
        ),
        name="weight_grads",
    )(*rows, *cots, *inners, *grads)


def matmul(spec, left, right):
    return jnp.einsum(spec, left, right, preferred_element_type=jnp.float32)


def pull(values, axis, ahead):
    count = lax.axis_size(axis)
    return lax.ppermute(values, axis, [((i + ahead) % count, i) for i in range(count)])


def swap_ends(values):
    count = lax.axis_size("ctx")
    return lax.ppermute(values, "ctx", [(i, count - 1 - i) for i in range(count)])


def spread(values, axis):
    return [values] + [pull(values, axis, ahead) for ahead in range(1, lax.axis_size(axis))]


def gather(values, axis):
    count = lax.axis_size(axis)
    ahead = jnp.stack(spread(values, axis))
    return lax.dynamic_slice_in_dim(
        jnp.concatenate([ahead, ahead]), count - lax.axis_index(axis), count, 0
    )


def collect(parts, axis):
    received = [parts[0]]
    for ahead in range(1, len(parts)):
        received.append(pull(parts[ahead].astype(jnp.bfloat16), axis, len(parts) - ahead))
    return received


def total(parts):
    return sum(part.astype(jnp.float32) for part in parts)


def reduce_blocks(values, axis, dim):
    count = lax.axis_size(axis)
    at = lax.axis_index(axis)
    blocks = [
        lax.dynamic_index_in_dim(values, (at + ahead) % count, dim, keepdims=False)
        for ahead in range(count)
    ]
    return total(collect(blocks, axis)).astype(jnp.bfloat16)


def reduce_to(values, axis, base):
    count, at = lax.axis_size(axis), lax.axis_index(axis)
    size = values.shape[0]
    summed = 0.0
    for ahead in range(count):
        target = jnp.clip((at + ahead) % count - base, 0, size - 1)
        block = lax.dynamic_index_in_dim(values, target, 0, keepdims=False)
        if ahead:
            ways = [(i, (i + ahead) % count) for i in range(count)]
            block = lax.ppermute(block, axis, [w for w in ways if base <= w[1] < base + size])
        summed = summed + block.astype(jnp.float32)
    return summed.astype(jnp.bfloat16)


def place_kernel(seq_ref, chunk_ref, *refs):
    out_ref = refs[-1]
    for at, ref in enumerate(refs[:-1]):

        @pl.when(pl.program_id(0) == at)
        def _(ref=ref):
            out_ref[0] = ref[...].astype(out_ref.dtype)


def place_rows(pieces, seqs, chunks, seq_count, chunk_count, kind):
    width, chunk = pieces[0].shape
    return pl.pallas_call(
        place_kernel,
        out_shape=jax.ShapeDtypeStruct((seq_count, width, chunk_count * chunk), kind),
        grid_spec=pltpu.PrefetchScalarGridSpec(
            num_scalar_prefetch=2,
            grid=(len(pieces),),
            in_specs=[pl.BlockSpec((width, chunk), lambda i, s, c: (0, 0))] * len(pieces),
            out_specs=pl.BlockSpec((1, width, chunk), lambda i, s, c: (s[i], 0, c[i])),
        ),
        compiler_params=pltpu.CompilerParams(vmem_limit_bytes=32 * 2**20),
        name="place_rows",
    )(seqs, chunks, *pieces)


def shards(tokens, gains, qkv_weight, out_weight, gate_weight, up_weight, down_weight, cotangent):
    seq_count, span_len, width = tokens.shape
    ctx_count, sub_count = lax.axis_size("ctx"), lax.axis_size("sub")
    pair_count = ctx_count * sub_count
    chunk = span_len // (2 * sub_count)
    row_count = 2 * chunk
    owners = lax.axis_size(("shard", "ctx"))
    tensor_count = lax.axis_size(("seq", "sub"))
    everyone = ("seq", "sub", "shard", "ctx")
    own_seq, own_sub, own_ctx = lax.axis_index("seq"), lax.axis_index("sub"), lax.axis_index("ctx")
    is_low = own_ctx < ctx_count // 2
    own_pair = jnp.where(
        is_low,
        2 * sub_count * own_ctx + own_sub,
        2 * pair_count - 1 - 2 * sub_count * own_ctx - own_sub,
    ).astype(jnp.int32)

    def take_rows(values):
        span = lax.dynamic_index_in_dim(values, own_seq, 0, keepdims=False)
        kept = lax.dynamic_slice_in_dim(span, own_sub * chunk, chunk, 0)
        moved = lax.dynamic_slice_in_dim(span, (2 * sub_count - 1 - own_sub) * chunk, chunk, 0)
        return kept, moved

    def in_order(kept, moved):
        return jnp.where(is_low, jnp.concatenate([kept, moved]), jnp.concatenate([moved, kept]))

    def owner_sums(grad, cols, base):
        count = grad.shape[1] // cols
        grad = jnp.transpose(grad.reshape(grad.shape[0], count, cols), (1, 0, 2))
        grad = grad.reshape(count // ctx_count, ctx_count, -1, cols)
        return reduce_blocks(grad, "shard", 0) if base is None else reduce_to(grad, "shard", base)

    def exchange(home):
        far = [spread(rows, "seq") for rows in home]
        return [part for rows in far for seq_rows in rows for part in spread(seq_rows, "sub")]

    def deliver(pieces, kind):
        seqs, chunks = [], []
        for moved in range(2):
            for seq_ahead in range(seq_count):
                for sub_ahead in range(sub_count):
                    sub = (own_sub + sub_ahead) % sub_count
                    seqs.append((own_seq + seq_ahead) % seq_count)
                    chunks.append(2 * sub_count - 1 - sub if moved else sub)
        placed = place_rows(
            pieces,
            jnp.stack(seqs).astype(jnp.int32),
            jnp.stack(chunks).astype(jnp.int32),
            seq_count,
            2 * sub_count,
            kind,
        )
        return jnp.transpose(placed, (0, 2, 1))

    def back_home(columns):
        low, high = columns[:, :chunk], columns[:, chunk:]
        kept = jnp.where(is_low, low, high)
        moved = swap_ends(jnp.where(is_low, high, low))
        return [kept, moved]

    tile_rows, tile_cols = qkv_weight.shape
    gain_part = gains.shape[1]
    first_tile = jnp.concatenate(
        [qkv_weight, jnp.pad(gains, ((0, 0), (0, tile_cols - gain_part)))], axis=0
    )
    first_all = lax.all_gather(first_tile, everyone, axis=0, tiled=False)
    qkv_cols = owners * tile_cols
    padded_cols = -(-qkv_cols // LANES) * LANES
    qkv_all = assemble(first_all, tensor_count, tile_rows, padded_cols)
    gain_all = (
        jnp.transpose(first_all[:owners, tile_rows:, :gain_part], (1, 0, 2))
        .reshape(2, 1, width)
        .astype(jnp.float32)
    )
    gain_one, gain_two = gain_all[0], gain_all[1]
    out_rows, out_cols = out_weight.shape
    out_tiles = gather(gather(gather(gather(out_weight, "ctx"), "shard"), "seq"), "sub")
    out_heads = jnp.pad(
        jnp.transpose(out_tiles, (1, 0, 4, 2, 3, 5)).reshape(HEADS, HEAD_DIM, width),
        ((0, 0), (HEAD_DIM, 0), (0, 0)),
    )

    qkv_all, out_heads = lax.optimization_barrier((qkv_all, out_heads))

    kept_tokens, moved_tokens = take_rows(tokens)
    kept_cot, moved_cot = take_rows(cotangent)
    rows_low = in_order(kept_tokens, swap_ends(moved_tokens))
    cot = in_order(kept_cot, swap_ends(moved_cot.astype(jnp.bfloat16)).astype(jnp.float32))
    qkv_all, cot = lax.optimization_barrier((qkv_all, cot))
    wide = -(-width // LANES) * LANES
    far_cots = spread(jnp.pad(cot.astype(jnp.bfloat16), ((0, 0), (0, wide - width))), "seq")
    step = jnp.arange(chunk, dtype=jnp.int32)
    positions = jnp.concatenate([own_pair * chunk + step, (2 * pair_count - 1 - own_pair) * chunk + step])
    half_dim = HEAD_DIM // 2
    frequency = rope_base ** (-2.0 * jnp.arange(half_dim, dtype=jnp.float32) / HEAD_DIM)
    angles = positions.astype(jnp.float32)[:, None] * frequency[None, :]
    cosine, sine = jnp.cos(angles), jnp.sin(angles)
    cosine_table = jnp.concatenate([cosine] * 4, axis=1)
    sine_table = jnp.concatenate([-sine, sine] * 2, axis=1)

    def shape(*dims, kind=jnp.bfloat16):
        return jax.ShapeDtypeStruct(dims, kind)

    head_rows = (KV_HEADS, 2, GROUP, chunk, LANES)
    qkv_flops = 2 * row_count * width * padded_cols
    query_heads, pair_own, normed = row_call(
        project_kernel,
        chunk,
        [(rows_low, 0), (gain_one, 1), (qkv_all, 1), (cosine_table, 0), (sine_table, 0)],
        [(shape(*head_rows), 0), (shape(KV_HEADS, row_count, LANES), 0), (shape(row_count, width), 0)],
        "project",
        qkv_flops,
    )
    query_heads = query_heads.reshape(KV_HEADS, GROUP * row_count, LANES)
    pair_all = lax.all_gather(pair_own, ("ctx", "sub"), axis=1, tiled=True)
    ffn_tile = jnp.concatenate([gate_weight, up_weight, down_weight.T], axis=1)
    pair_all, far_cots, ffn_tile = lax.optimization_barrier((pair_all, far_cots, ffn_tile))
    ffn_all = lax.all_gather(ffn_tile, ("shard", "ctx"), axis=0, tiled=True)
    hidden_part = gate_weight.shape[1]
    place = own_pair[None]
    attended = attention_forward(place, query_heads, pair_all, ctx_count, sub_count, chunk, GROUP)
    attended = [attended.reshape(head_rows)]
    cot_low = [spread(seq_rows, "sub") for seq_rows in far_cots]
    mix_flops = 4 * row_count * width * width
    hidden, normed_own, attn_low = row_call(
        functools.partial(mix_kernel, len(attended)),
        chunk,
        [(rows, 0) for rows in attended]
        + [(out_heads, 1), (rows_low, 0), (gain_two, 1)],
        [
            (shape(row_count, width, kind=jnp.float32), 0),
            (shape(row_count, wide), 0),
            (shape(row_count, width), 0),
        ],
        "mix",
        mix_flops,
    )
    far_rows = spread(normed_own, "seq")
    feeds, backs, pieces = [], [], []
    for seq_ahead, near_rows in enumerate(far_rows):
        if seq_ahead:
            near_rows, backs[-1] = lax.optimization_barrier((near_rows, backs[-1]))
        near = list(zip(spread(near_rows, "sub"), cot_low[seq_ahead]))
        kinds = [jnp.bfloat16 if sub_ahead else jnp.float32 for sub_ahead in range(sub_count)]
        found = row_call(
            functools.partial(feed_kernel, sub_count),
            chunk,
            [(array, 0) for both in near for array in both] + [(ffn_all, 1)],
            [
                (out, 0)
                for kind in kinds
                for out in (
                    shape(row_count, wide, kind=kind),
                    shape(row_count, wide, kind=kind),
                    shape(row_count, hidden_part),
                    shape(row_count, 2 * hidden_part),
                )
            ],
            "feed",
            8 * sub_count * row_count * width * 2 * hidden_part,
        )
        seq_backs, seq_feeds = found[0::4], found[1::4]
        pieces += [both + tuple(rest) for both, *rest in zip(near, found[2::4], found[3::4])]
        backs.append(collect(seq_backs, "sub"))
        feeds.append(collect(seq_feeds, "sub"))
    backs = backs[0] + collect([backs[0]] + [total(parts) for parts in backs[1:]], "seq")[1:]
    feed_sent = [total(parts).astype(jnp.bfloat16) for parts in feeds[1:]]
    ffn_grad = weight_grads(width, *zip(*pieces))
    backs, ffn_grad = lax.optimization_barrier((backs, ffn_grad))
    ffn_out = lax.psum_scatter(ffn_grad, ("shard", "ctx"), scatter_dimension=0, tiled=True)
    hidden_grad, hidden_low, grad_heads, extra, gain_two_grad = row_call(
        functools.partial(unmix_kernel, len(backs), len(attended)),
        chunk,
        [(part, 0) for part in backs + attended]
        + [(hidden, 0), (cot, 0), (gain_two, 1), (out_heads, 1)],
        [
            (shape(row_count, width, kind=jnp.float32), 0),
            (shape(row_count, width), 0),
            (shape(*head_rows), 0),
            (shape(*head_rows), 0),
            (shape(8, width, kind=jnp.float32), 1),
        ],
        "unmix",
        mix_flops,
    )
    flat = (KV_HEADS, GROUP * row_count, LANES)
    grad_heads, extra = grad_heads.reshape(flat), extra.reshape(flat)
    grad_heads, feed_sent = lax.optimization_barrier((grad_heads, feed_sent))
    feeds = feeds[0] + collect([feeds[0]] + feed_sent, "seq")[1:]
    filled = attention_backward(
        place, query_heads, grad_heads, extra, pair_all, 0, 3, (), ctx_count, sub_count, chunk, GROUP
    )
    filled, feeds = lax.optimization_barrier((filled, feeds))
    (block_low,) = row_call(
        functools.partial(block_kernel, len(feeds)),
        chunk,
        [(part, 0) for part in feeds] + [(hidden, 0)],
        [(shape(width, row_count), 0)],
        "block",
        0,
    )
    block_low, filled = lax.optimization_barrier((block_low, filled))
    block_home = back_home(block_low)
    query_grad, pair_grad = attention_backward(
        place,
        query_heads,
        grad_heads,
        extra,
        pair_all,
        3,
        KV_HEADS,
        filled,
        ctx_count,
        sub_count,
        chunk,
        GROUP,
    )
    block_home, query_grad, pair_grad, hidden_low, ffn_out = lax.optimization_barrier(
        (block_home, query_grad, pair_grad, hidden_low, ffn_out)
    )
    pair_grad = lax.psum_scatter(pair_grad, ("ctx", "sub"), scatter_dimension=1, tiled=True)
    query_grad = query_grad.reshape(head_rows)
    half_cols, extra_rows = qkv_cols // 2, 16
    (proj_early,) = row_call(
        early_kernel,
        chunk,
        [(query_grad, 0), (cosine_table, 0), (sine_table, 0)],
        [(shape(row_count, -(-half_cols // LANES) * LANES), 0)],
        "early",
        0,
    )
    early_grad = jnp.concatenate(
        [
            matmul("rf,re->fe", attn_low, hidden_low).astype(jnp.bfloat16),
            matmul("rd,re->de", normed, proj_early).astype(jnp.bfloat16),
        ],
        axis=1,
    )
    early_grad = early_grad.reshape(seq_count, sub_count, tile_rows, early_grad.shape[1])
    early_grad = reduce_blocks(reduce_blocks(early_grad, "sub", 1), "seq", 0)
    out_sums = owner_sums(early_grad[:, :width], out_cols, None)
    qkv_early = owner_sums(early_grad[:, width : width + half_cols], tile_cols, 0)
    pair_grad, out_sums, qkv_early, block_pieces = lax.optimization_barrier(
        (pair_grad, out_sums, qkv_early, exchange(block_home))
    )
    block_out = deliver(block_pieces, jnp.bfloat16)
    proj_grad, input_low, gain_one_grad = row_call(
        finish_kernel,
        chunk,
        [
            (query_grad, 0),
            (pair_grad, 0),
            (cosine_table, 0),
            (sine_table, 0),
            (qkv_all, 1),
            (rows_low, 0),
            (hidden_grad, 0),
            (gain_one, 1),
        ],
        [
            (shape(row_count, padded_cols), 0),
            (shape(width, row_count), 0),
            (shape(8, width, kind=jnp.float32), 1),
        ],
        "finish",
        qkv_flops,
    )
    input_grad = deliver(exchange(back_home(input_low)), jnp.float32)

    late_cols = qkv_cols - half_cols
    qkv_grad = matmul("rd,re->de", normed, proj_grad[:, half_cols:qkv_cols]).astype(jnp.bfloat16)
    gains_grad = jnp.concatenate([gain_one_grad[:1], gain_two_grad[:1]]).astype(jnp.bfloat16)
    folded = -(-width // late_cols)
    gains_rows = jnp.pad(gains_grad, ((0, 0), (0, folded * late_cols - width)))
    gains_rows = jnp.pad(
        gains_rows.reshape(2 * folded, late_cols), ((0, extra_rows - 2 * folded), (0, 0))
    )
    last = jnp.concatenate(
        [
            qkv_grad.reshape(seq_count, sub_count, tile_rows, late_cols),
            jnp.broadcast_to(gains_rows, (seq_count, sub_count) + gains_rows.shape),
        ],
        axis=2,
    )
    last = reduce_blocks(reduce_blocks(last, "sub", 1), "seq", 0)
    gains_sum = last[tile_rows : tile_rows + 2 * folded].reshape(2, folded * late_cols)[:, :width]
    gains_tiles = jnp.transpose(gains_sum.reshape(2, owners, gain_part), (1, 0, 2))
    gains_tiles = reduce_blocks(
        gains_tiles.reshape(owners // ctx_count, ctx_count, 2, gain_part), "shard", 0
    )
    qkv_late = owner_sums(last[:tile_rows], tile_cols, owners // ctx_count // 2)
    is_early = lax.axis_index("shard") < owners // ctx_count // 2
    qkv_sums = jnp.where(is_early, qkv_early, qkv_late)
    final = jnp.concatenate(
        [
            jnp.concatenate(
                [out_sums, jnp.pad(gains_tiles, ((0, 0), (0, extra_rows - 2), (0, 0)))], axis=1
            ),
            jnp.pad(qkv_sums, ((0, 0), (0, extra_rows), (0, 0))),
        ],
        axis=2,
    )
    final = reduce_blocks(final, "ctx", 0).astype(jnp.float32)
    gains_out = final[tile_rows : tile_rows + 2, :gain_part]
    out_out, qkv_out = final[:tile_rows, :out_cols], final[:tile_rows, out_cols:]
    ffn_out = ffn_out.astype(jnp.float32)
    return (
        block_out,
        input_grad,
        gains_out,
        qkv_out,
        out_out,
        ffn_out[:, :hidden_part],
        ffn_out[:, hidden_part : 2 * hidden_part],
        ffn_out[:, 2 * hidden_part :].T,
    )


def solution(mesh):
    shard_count, ctx_count, tensor_count = (mesh.shape[axis] for axis in ("shard", "ctx", "tensor"))

    def run(tokens, *rest):
        seq_count = tokens.shape[0] // shard_count
        split = Mesh(
            mesh.devices.reshape(shard_count, ctx_count, seq_count, tensor_count // seq_count),
            ("shard", "ctx", "seq", "sub"),
        )
        rows = P("shard", "ctx", None)
        pool = ("shard", "ctx")
        team = ("seq", "sub")
        weights = (P(None, pool), P(team, pool), P(team, pool), P(pool, team), P(pool, team), P(team, pool))
        return jax.shard_map(
            shards,
            mesh=split,
            in_specs=(rows,) + weights + (rows,),
            out_specs=(rows, rows) + weights,
            check_vma=False,
        )(tokens, *rest)

    return run
```

```python
import functools

import jax
import jax.numpy as jnp
from jax import lax
from jax.experimental import pallas as pl
from jax.experimental.pallas import tpu as pltpu
from jax.sharding import Mesh
from jax.sharding import PartitionSpec as P

HEADS = 15
KV_HEADS = 5
HEAD_DIM = 64
GROUP = 3
LANES = 128
HALF = HEAD_DIM


epsilon = 1e-05
rope_base = 100000.0
masked_score = -1e30


def pair_place(pair, ctx_count, sub):
    turn = pair // (2 * sub)
    spot = pair % (2 * sub)
    low = spot < sub
    return jnp.where(low, turn * sub + spot, (ctx_count - 1 - turn) * sub + 2 * sub - 1 - spot)


def dot_nt(a, b):
    return lax.dot_general(a, b, (((1,), (1,)), ((), ())), preferred_element_type=jnp.float32)


def dot_nn(a, b):
    return lax.dot_general(a, b, (((1,), (0,)), ((), ())), preferred_element_type=jnp.float32)


def dot_tn(a, b):
    return lax.dot_general(a, b, (((0,), (0,)), ((), ())), preferred_element_type=jnp.float32)


def causal(rows, cols, chunk, key_axis):
    shape = (rows, cols)
    query_axis = 1 - key_axis
    query = lax.broadcasted_iota(jnp.int32, shape, query_axis)
    key = lax.broadcasted_iota(jnp.int32, shape, key_axis)
    return key <= lax.rem(query, chunk)


def forward_kernel(ctx_count, sub, chunk, group, pair_ref, q_ref, kv_ref, out_ref, top, total):
    pairs = ctx_count * sub
    own = pair_ref[0]
    part = group * chunk
    lanes = lambda rows: lax.broadcasted_iota(jnp.int32, (rows, LANES), 1)

    def load(place, slot, count):
        return kv_ref[0, pl.ds(pl.multiple_of(place * 2 * chunk + slot * chunk, chunk), count * chunk), :]

    def weighted(powers, kv):
        ones = jnp.where(lanes(kv.shape[0]) < HALF, jnp.ones_like(kv), kv)
        return dot_nn(powers, ones)

    def update(start, rows, kv, first, mask):
        scores = dot_nt(q_ref[0, start : start + rows, :], kv)
        if mask is not None:
            scores = jnp.where(mask, scores, masked_score)
        best = jnp.max(scores, axis=1, keepdims=True)
        spot = slice(start, start + rows)
        if first:
            top[spot, :] = jnp.broadcast_to(best, (rows, LANES))
            powers = jnp.exp(scores - best).astype(jnp.bfloat16)
            total[spot, :] = weighted(powers, kv)
        else:
            old = top[spot, :]
            new = jnp.maximum(old, best)
            powers = jnp.exp(scores - new[:, :1]).astype(jnp.bfloat16)
            total[spot, :] = total[spot, :] * jnp.exp(old - new) + weighted(powers, kv)
            top[spot, :] = new

    place = pair_place(own, ctx_count, sub)
    near = load(place, 0, 1)
    both = load(place, 0, 2)
    near_mask = causal(chunk, chunk, chunk, 1)
    columns = lax.broadcasted_iota(jnp.int32, (chunk, 2 * chunk), 1)
    queries = lax.broadcasted_iota(jnp.int32, (chunk, 2 * chunk), 0)
    both_mask = columns <= queries + chunk
    for head in range(group):
        update(head * chunk, chunk, near, True, near_mask)
        update(part + head * chunk, chunk, both, True, both_mask)

    def sweep(first, last, count, start, heads):
        def load_at(pair):
            return load(pair_place(pair, ctx_count, sub), 0, count)

        def absorb(kv):
            for head in range(heads):
                update(start + head * chunk, chunk, kv, False, None)

        for size in (4, 2, 1) if count == 1 else (2, 1):
            turns = (last - first) // size

            @pl.loop(0, turns)
            def _(step, first=first, size=size):
                pair = first + size * step
                found = [load_at(pair + at) for at in range(size)]
                absorb(found[0] if size == 1 else jnp.concatenate(found, axis=0))

            first = first + size * turns

    sweep(0, own, 1, 0, 2 * group)
    sweep(own + 1, pairs, 2, part, group)

    for head in range(2 * group):
        spot = slice(head * chunk, (head + 1) * chunk)
        sums = total[spot, :]
        count = sums[:, :1]
        out_ref[0, spot, :] = jnp.where(
            lanes(chunk) < HALF, top[spot, :] + jnp.log(count), sums / count
        )


def attention_forward(own_pair, queries, pairs_all, ctx_count, sub, chunk, group):
    rows = queries.shape[1]
    heads, length, _ = pairs_all.shape
    grid_spec = pltpu.PrefetchScalarGridSpec(
        num_scalar_prefetch=1,
        grid=(heads,),
        in_specs=[
            pl.BlockSpec((1, rows, LANES), lambda h, p: (h, 0, 0)),
            pl.BlockSpec((1, length, LANES), lambda h, p: (h, 0, 0)),
        ],
        out_specs=pl.BlockSpec((1, rows, LANES), lambda h, p: (h, 0, 0)),
        scratch_shapes=[
            pltpu.VMEM((rows, LANES), jnp.float32),
            pltpu.VMEM((rows, LANES), jnp.float32),
        ],
    )
    cost = heads * rows * length // 2
    return pl.pallas_call(
        functools.partial(forward_kernel, ctx_count, sub, chunk, group),
        out_shape=jax.ShapeDtypeStruct((heads, rows, LANES), jnp.float32),
        grid_spec=grid_spec,
        compiler_params=pltpu.CompilerParams(vmem_limit_bytes=48 * 2**20),
        cost_estimate=pl.CostEstimate(
            flops=cost * 4 * HALF, bytes_accessed=heads * LANES * (rows * 6 + length * 2), transcendentals=cost
        ),
        name="attention_forward",
    )(own_pair, queries, pairs_all)


def backward_kernel(
    ctx_count, sub, chunk, group, pair_ref, q_ref, cot_ref, extra_ref, kv_ref, dq_ref, dkv_ref
):
    pairs = ctx_count * sub
    own = pair_ref[0]
    part = group * chunk

    def minus(rows, low, high):
        lane = lax.broadcasted_iota(jnp.int32, (rows, LANES), 1)
        return jnp.where((lane >= low) & (lane < high), -1.0, 0.0).astype(jnp.bfloat16)

    def load(place, slot, count):
        base = pl.multiple_of(place * 2 * chunk + slot * chunk, chunk)
        return kv_ref[0, pl.ds(base, count * chunk), :]

    def step(start, rows, kv, first, mask):
        keys = kv.shape[0]
        key_side = jnp.concatenate([kv, minus(keys, 0, 3)], axis=1)
        value_side = jnp.concatenate([kv, minus(keys, 3, 6)], axis=1)
        pair_sum = None
        for at in range(start, start + rows, chunk):
            spot = slice(at, at + chunk)
            query = q_ref[0, spot, :]
            cot = cot_ref[0, spot, :]
            extra = extra_ref[0, spot, :]
            powers = jnp.exp(dot_nt(key_side, jnp.concatenate([query, extra], axis=1)))
            if mask is not None:
                powers = jnp.where(mask, powers, 0.0)
            slope = dot_nt(value_side, jnp.concatenate([cot, extra], axis=1))
            grads = (powers * slope).astype(jnp.bfloat16)
            powers = powers.astype(jnp.bfloat16)
            term = dot_nn(powers, cot) + dot_nn(grads, query)
            pair_sum = term if pair_sum is None else pair_sum + term
            moved = dot_tn(grads, kv)
            if first:
                dq_ref[0, spot, :] = moved
            else:
                dq_ref[0, spot, :] += moved
        return pair_sum

    def store(place, slot, count, value):
        base = pl.multiple_of(place * 2 * chunk + slot * chunk, chunk)
        dkv_ref[0, pl.ds(base, count * chunk), :] = value.astype(jnp.bfloat16)

    place = pair_place(own, ctx_count, sub)
    near_mask = causal(chunk, chunk, chunk, 0)
    keys = lax.broadcasted_iota(jnp.int32, (2 * chunk, chunk), 0)
    queries = lax.broadcasted_iota(jnp.int32, (2 * chunk, chunk), 1)
    far = step(part, part, load(place, 0, 2), True, keys <= queries + chunk)
    near = step(0, part, load(place, 0, 1), True, near_mask)
    store(place, 0, 1, far[:chunk] + near)
    store(place, 1, 1, far[chunk:])

    def sweep(first, last, count, start, rows):
        def put(at, value):
            store(at, 0, count, value)
            if count == 1:
                store(at, 1, 1, jnp.zeros((chunk, LANES), jnp.float32))

        for size in (4, 2, 1) if count == 1 else (2, 1):
            turns = (last - first) // size

            @pl.loop(0, turns)
            def _(turn, first=first, size=size):
                places = [pair_place(first + size * turn + at, ctx_count, sub) for at in range(size)]
                found = [load(at, 0, count) for at in places]
                kv = found[0] if size == 1 else jnp.concatenate(found, axis=0)
                sums = step(start, rows, kv, False, None)
                for at, spot in enumerate(places):
                    put(spot, sums[at * count * chunk : (at + 1) * count * chunk])

            first = first + size * turns

    sweep(0, own, 1, 0, 2 * part)
    sweep(own + 1, pairs, 2, part, part)


def attention_backward(
    own_pair, queries, cots, extra, pairs_all, base, stop, filled, ctx_count, sub, chunk, group
):
    total_heads, rows, _ = queries.shape
    heads, length = stop - base, pairs_all.shape[1]
    row_spec = pl.BlockSpec((1, rows, LANES), lambda h, p: (base + h, 0, 0))
    long_spec = pl.BlockSpec((1, length, LANES), lambda h, p: (base + h, 0, 0))
    cost = heads * rows * length // 2
    kernel = functools.partial(backward_kernel, ctx_count, sub, chunk, group)

    def filling(pair_ref, q_ref, cot_ref, extra_ref, kv_ref, old_dq_ref, old_dkv_ref, dq_ref, dkv_ref):
        kernel(pair_ref, q_ref, cot_ref, extra_ref, kv_ref, dq_ref, dkv_ref)

    return pl.pallas_call(
        filling if filled else kernel,
        out_shape=(
            jax.ShapeDtypeStruct((total_heads, rows, LANES), jnp.float32),
            jax.ShapeDtypeStruct((total_heads, length, LANES), jnp.bfloat16),
        ),
        grid_spec=pltpu.PrefetchScalarGridSpec(
            num_scalar_prefetch=1,
            grid=(heads,),
            in_specs=[row_spec, row_spec, row_spec, long_spec]
            + [pl.BlockSpec(memory_space=pl.ANY)] * len(filled),
            out_specs=(row_spec, long_spec),
        ),
        input_output_aliases={5 + at: at for at in range(len(filled))},
        compiler_params=pltpu.CompilerParams(vmem_limit_bytes=48 * 2**20),
        cost_estimate=pl.CostEstimate(
            flops=cost * 10 * HALF, bytes_accessed=heads * LANES * (rows * 10 + length * 4), transcendentals=cost
        ),
        name="attention_backward",
    )(own_pair, queries, cots, extra, pairs_all, *filled)


def three_parts(values):
    high = values.astype(jnp.bfloat16)
    rest = values - high.astype(jnp.float32)
    middle = rest.astype(jnp.bfloat16)
    low = (rest - middle.astype(jnp.float32)).astype(jnp.bfloat16)
    return [high, middle, low]


def lane_index(rows):
    return lax.broadcasted_iota(jnp.int32, (rows, LANES), 1)


def swap_halves(tile):
    lane = lane_index(tile.shape[0])
    quarter = HALF // 2
    return jnp.where(
        lax.rem(lane, HALF) < quarter,
        pltpu.roll(tile, LANES - quarter, 1),
        pltpu.roll(tile, quarter, 1),
    )


def normalise(values):
    inv_rms = lax.rsqrt(jnp.mean(values * values, axis=-1, keepdims=True) + epsilon)
    return values * inv_rms, inv_rms


def norm_back(upstream, values, gain_row):
    unit_rows, inv_rms = normalise(values)
    shaped = upstream * gain_row
    inner_mean = jnp.mean(shaped * unit_rows, axis=-1, keepdims=True)
    return inv_rms * (shaped - unit_rows * inner_mean), upstream * unit_rows


def assemble_kernel(rows, in_ref, out_ref):
    tiles = [in_ref[at, :rows, :] for at in range(in_ref.shape[0])]
    used = len(tiles) * tiles[0].shape[1]
    if used < out_ref.shape[1]:
        tiles.append(jnp.zeros((rows, out_ref.shape[1] - used), tiles[0].dtype))
    out_ref[...] = jnp.concatenate(tiles, axis=1)


def assemble(gathered, teams, rows, cols):
    count = gathered.shape[0] // teams
    return pl.pallas_call(
        functools.partial(assemble_kernel, rows),
        grid=(teams,),
        in_specs=[pl.BlockSpec((count,) + gathered.shape[1:], lambda t: (t, 0, 0))],
        out_specs=pl.BlockSpec((rows, cols), lambda t: (t, 0)),
        out_shape=jax.ShapeDtypeStruct((teams * rows, cols), gathered.dtype),
        compiler_params=pltpu.CompilerParams(vmem_limit_bytes=48 * 2**20),
        name="assemble",
    )(gathered)


def project_kernel(token_ref, gain_ref, weight_ref, cos_ref, sin_ref, q_ref, kv_ref, normed_ref):
    rows = token_ref.shape[0]
    unit_rows, _ = normalise(token_ref[...].astype(jnp.float32))
    normed = (unit_rows * gain_ref[...]).astype(jnp.bfloat16)
    normed_ref[...] = normed
    projected = dot_nn(normed, weight_ref[...])
    cos, sin = cos_ref[...], sin_ref[...]
    low = lane_index(rows) < HALF

    def tile(column):
        return projected[:, column // 2 * LANES : (column // 2 + 1) * LANES]

    def turned(column):
        raw = tile(column)
        out = raw * cos + swap_halves(raw) * sin
        return pltpu.roll(out, HALF, 1) if column % 2 else out

    for head in range(HEADS):
        query = jnp.where(low, turned(head) * HEAD_DIM ** (-0.5), 0.0)
        q_ref[head // GROUP, 0, head % GROUP] = query.astype(jnp.bfloat16)
    for head in range(KV_HEADS):
        key = turned(HEADS + head)
        column = HEADS + KV_HEADS + head
        value = tile(column) if column % 2 else pltpu.roll(tile(column), HALF, 1)
        kv_ref[head] = jnp.where(low, key, value).astype(jnp.bfloat16)


def whole(shape):
    return pl.BlockSpec(shape, lambda c: (0,) * len(shape))


def row_call(kernel, chunk, ins, outs, name, flops):
    def spec(array):
        shape = array.shape
        if len(shape) == 5:
            return pl.BlockSpec((shape[0], 1) + shape[2:], lambda c: (0, c, 0, 0, 0))
        if len(shape) == 3:
            return pl.BlockSpec((shape[0], chunk, shape[2]), lambda c: (0, c, 0))
        if shape[0] != 2 * chunk:
            return pl.BlockSpec((shape[0], chunk), lambda c: (0, c))
        return pl.BlockSpec((chunk, shape[1]), lambda c: (c, 0))

    moved = sum(a.size * a.dtype.itemsize for a, _ in ins) + sum(o.size * o.dtype.itemsize for o, _ in outs)
    return pl.pallas_call(
        kernel,
        grid=(2,),
        in_specs=[whole(a.shape) if fixed else spec(a) for a, fixed in ins],
        out_specs=[whole(o.shape) if fixed else spec(o) for o, fixed in outs],
        out_shape=[o for o, _ in outs],
        compiler_params=pltpu.CompilerParams(vmem_limit_bytes=56 * 2**20),
        cost_estimate=pl.CostEstimate(flops=flops, bytes_accessed=moved, transcendentals=0),
        name=name,
    )(*[a for a, _ in ins])


def pick(refs, head):
    group, at = head // GROUP, 0
    for ref in refs:
        if group < at + ref.shape[0]:
            return ref[group - at, 0, head % GROUP]
        at += ref.shape[0]


def pick_pair(refs, group):
    at = 0
    for ref in refs:
        if group < at + ref.shape[0]:
            return ref[group - at]
        at += ref.shape[0]


def mix_kernel(count, *refs):
    attended_refs = refs[:count]
    weight_ref, token_ref, gain_ref, hidden_ref, normed_ref, attn_ref = refs[count:]
    total = token_ref[...].astype(jnp.float32)
    first = lane_index(token_ref.shape[0]) < HALF
    for head in range(HEADS):
        rows = pick(attended_refs, head)
        low = rows.astype(jnp.bfloat16)
        if head % 2:
            both = jnp.concatenate([low_before, low], axis=1)
            total = total + dot_nn(both, weight_ref[head - 1 : head + 1].reshape(2 * LANES, -1))
        elif head == HEADS - 1:
            total = total + dot_nn(low, weight_ref[head])
        low_before = low
        base = head // 2 * LANES
        if head % 2:
            both = jnp.where(first, pltpu.roll(before, HALF, 1), rows)
            attn_ref[:, base : base + LANES] = both.astype(jnp.bfloat16)
        elif head == HEADS - 1:
            alone = pltpu.roll(rows, HALF, 1)[:, :HALF]
            attn_ref[:, base : base + HALF] = alone.astype(jnp.bfloat16)
        before = rows
    hidden_ref[...] = total
    unit_rows, _ = normalise(total)
    normed_ref[:, : total.shape[1]] = (unit_rows * gain_ref[...]).astype(jnp.bfloat16)


def accumulate(ref, rows):
    summed = jnp.broadcast_to(jnp.sum(rows, axis=0, keepdims=True), ref.shape)

    @pl.when(pl.program_id(0) == 0)
    def _():
        ref[...] = summed

    @pl.when(pl.program_id(0) != 0)
    def _():
        ref[...] += summed


def unmix_kernel(count, parts, *refs):
    ups = refs[:count]
    attended_refs, refs = refs[count : count + parts], refs[count + parts :]
    (hidden_ref, cot_ref, gain_ref, weight_ref, grad_ref, low_ref, heads_ref, extra_ref, gain_grad_ref) = refs
    width = hidden_ref.shape[1]
    upstream = ups[0][:, :width].astype(jnp.float32)
    for ref in ups[1:]:
        upstream = upstream + ref[:, :width].astype(jnp.float32)
    back, gain_rows = norm_back(upstream, hidden_ref[...], gain_ref[...])
    accumulate(gain_grad_ref, gain_rows)
    hidden_grad = cot_ref[...] + back
    grad_ref[...] = hidden_grad
    hidden_low = hidden_grad.astype(jnp.bfloat16)
    low_ref[...] = hidden_low
    lane = lane_index(hidden_low.shape[0])
    for head in range(HEADS):
        spot = (head // GROUP, 0, head % GROUP)
        if head % 2 == 0:
            many = weight_ref[head : head + 2].reshape(-1, weight_ref.shape[2])
            cots_two = dot_nt(hidden_low, many).astype(jnp.bfloat16)
        side = head % 2 * LANES
        cots = cots_two[:, side : side + LANES]
        heads_ref[spot] = cots
        attended = pick(attended_refs, head)
        delta = jnp.sum(cots.astype(jnp.float32) * attended, axis=1, keepdims=True)
        base = jnp.where(lane < 3, attended[:, :1], jnp.where(lane < 6, delta, 0.0))
        high, middle, low = three_parts(base)
        part = lax.rem(lane, 3)
        extra_ref[spot] = jnp.where(
            part == 0,
            high.astype(jnp.float32),
            jnp.where(part == 1, middle.astype(jnp.float32), low.astype(jnp.float32)),
        ).astype(jnp.bfloat16)


def turn_back(dq_ref, dkv_ref, cos_ref, sin_ref, proj_ref):
    rows = cos_ref.shape[0]
    cos, sin = cos_ref[...], sin_ref[...]
    low = lane_index(rows) < HALF

    def half(column):
        if column < HEADS:
            return dq_ref[column // GROUP, 0, column % GROUP] * HEAD_DIM ** (-0.5), 0
        if column < HEADS + KV_HEADS:
            return dkv_ref[column - HEADS].astype(jnp.float32), 0
        if column < HEADS + 2 * KV_HEADS:
            return dkv_ref[column - HEADS - KV_HEADS].astype(jnp.float32), 1
        return jnp.zeros((rows, LANES), jnp.float32), 0

    def placed(column):
        value, side = half(column)
        return value if side == column % 2 else pltpu.roll(value, HALF, 1)

    for at in range(proj_ref.shape[1] // LANES):
        raw = jnp.where(low, placed(2 * at), placed(2 * at + 1))
        if 2 * at < HEADS + KV_HEADS:
            raw = raw * cos - swap_halves(raw) * sin
        proj_ref[:, at * LANES : (at + 1) * LANES] = raw.astype(jnp.bfloat16)


def early_kernel(dq_ref, cos_ref, sin_ref, proj_ref):
    turn_back(dq_ref, None, cos_ref, sin_ref, proj_ref)


def block_kernel(count, *refs):
    hidden_ref, out_ref = refs[count], refs[count + 1]
    rows = hidden_ref[...]
    for ref in refs[:count]:
        rows = rows + ref[:, : rows.shape[1]].astype(jnp.float32)
    out_ref[...] = jnp.transpose(rows).astype(jnp.bfloat16)


def finish_kernel(
    dq_ref, dkv_ref, cos_ref, sin_ref, weight_ref, token_ref, grad_ref, gain_ref,
    proj_ref, input_ref, gain_grad_ref,
):
    turn_back(dq_ref, dkv_ref, cos_ref, sin_ref, proj_ref)
    upstream = dot_nt(proj_ref[...], weight_ref[...])
    back, gain_rows = norm_back(upstream, token_ref[...].astype(jnp.float32), gain_ref[...])
    accumulate(gain_grad_ref, gain_rows)
    input_ref[...] = jnp.transpose(grad_ref[...] + back).astype(jnp.bfloat16)


def feed_kernel(count, *refs):
    weight_ref = refs[2 * count]
    for at in range(count):
        outs = refs[2 * count + 1 + 4 * at : 2 * count + 5 + 4 * at]
        feed_rows(refs[2 * at], refs[2 * at + 1], weight_ref, *outs)


def feed_rows(rows_ref, cot_ref, weight_ref, back_ref, feed_ref, inner_ref, grad_ref):
    part = inner_ref.shape[1]
    width = weight_ref.shape[0]
    rows, cots = rows_ref[:, :width], cot_ref[:, :width]
    gate_up, down = weight_ref[:, : 2 * part], weight_ref[:, 2 * part :]
    both = dot_nn(rows, gate_up)
    inner_grad = dot_nn(cots, down)
    gate_value, up_value = both[:, :part], both[:, part:]
    gate_sigmoid = jax.nn.sigmoid(gate_value)
    swish = gate_value * gate_sigmoid
    inner = (swish * up_value).astype(jnp.bfloat16)
    inner_ref[...] = inner
    gate_grad = inner_grad * up_value * (gate_sigmoid * (1.0 + gate_value * (1.0 - gate_sigmoid)))
    grad_ref[:, :part] = gate_grad.astype(jnp.bfloat16)
    grad_ref[:, part:] = (inner_grad * swish).astype(jnp.bfloat16)
    back_ref[:, :width] = dot_nt(grad_ref[...], gate_up).astype(back_ref.dtype)
    feed_ref[:, :width] = dot_nt(inner, down).astype(feed_ref.dtype)


def weight_grad_kernel(count, *refs):
    rows, cots = refs[:count], refs[count : 2 * count]
    inners, grads = refs[2 * count : 3 * count], refs[3 * count : 4 * count]
    out_ref = refs[4 * count]
    width = out_ref.shape[0]
    step = pl.program_id(0)

    @pl.when(step < 2)
    def _():
        out_ref[...] = sum(dot_tn(a[:, :width], b[...]) for a, b in zip(rows, grads)).astype(jnp.bfloat16)

    @pl.when(step == 2)
    def _():
        out_ref[...] = sum(dot_tn(a[:, :width], b[...]) for a, b in zip(cots, inners)).astype(jnp.bfloat16)


def weight_grads(width, rows, cots, inners, grads):
    count, size, part = len(rows), rows[0].shape[0], inners[0].shape[1]
    once = [pl.BlockSpec((size, rows[0].shape[1]), lambda j: (0, 0))] * (2 * count)
    once += [pl.BlockSpec((size, part), lambda j: (0, 0))] * count
    turns = [pl.BlockSpec((size, part), lambda j: (0, jnp.minimum(j, 1)))] * count
    return pl.pallas_call(
        functools.partial(weight_grad_kernel, count),
        grid=(3,),
        in_specs=once + turns,
        out_specs=pl.BlockSpec((width, part), lambda j: (0, j)),
        out_shape=jax.ShapeDtypeStruct((width, 3 * part), jnp.bfloat16),
        compiler_params=pltpu.CompilerParams(vmem_limit_bytes=56 * 2**20),
        cost_estimate=pl.CostEstimate(
            flops=6 * count * size * width * part,
            bytes_accessed=count * size * (4 * width + 6 * part) + 6 * width * part,
            transcendentals=0,
        ),
        name="weight_grads",
    )(*rows, *cots, *inners, *grads)


def matmul(spec, left, right):
    return jnp.einsum(spec, left, right, preferred_element_type=jnp.float32)


def pull(values, axis, ahead):
    count = lax.axis_size(axis)
    return lax.ppermute(values, axis, [((i + ahead) % count, i) for i in range(count)])


def swap_ends(values):
    count = lax.axis_size("ctx")
    return lax.ppermute(values, "ctx", [(i, count - 1 - i) for i in range(count)])


def spread(values, axis):
    return [values] + [pull(values, axis, ahead) for ahead in range(1, lax.axis_size(axis))]


def gather(values, axis):
    count = lax.axis_size(axis)
    ahead = jnp.stack(spread(values, axis))
    return lax.dynamic_slice_in_dim(
        jnp.concatenate([ahead, ahead]), count - lax.axis_index(axis), count, 0
    )


def collect(parts, axis):
    received = [parts[0]]
    for ahead in range(1, len(parts)):
        received.append(pull(parts[ahead].astype(jnp.bfloat16), axis, len(parts) - ahead))
    return received


def total(parts):
    return sum(part.astype(jnp.float32) for part in parts)


def reduce_blocks(values, axis, dim):
    count = lax.axis_size(axis)
    at = lax.axis_index(axis)
    blocks = [
        lax.dynamic_index_in_dim(values, (at + ahead) % count, dim, keepdims=False)
        for ahead in range(count)
    ]
    return total(collect(blocks, axis)).astype(jnp.bfloat16)


def reduce_to(values, axis, base):
    count, at = lax.axis_size(axis), lax.axis_index(axis)
    size = values.shape[0]
    summed = 0.0
    for ahead in range(count):
        target = jnp.clip((at + ahead) % count - base, 0, size - 1)
        block = lax.dynamic_index_in_dim(values, target, 0, keepdims=False)
        if ahead:
            ways = [(i, (i + ahead) % count) for i in range(count)]
            block = lax.ppermute(block, axis, [w for w in ways if base <= w[1] < base + size])
        summed = summed + block.astype(jnp.float32)
    return summed.astype(jnp.bfloat16)


def place_kernel(seq_ref, chunk_ref, *refs):
    out_ref = refs[-1]
    for at, ref in enumerate(refs[:-1]):

        @pl.when(pl.program_id(0) == at)
        def _(ref=ref):
            out_ref[0] = ref[...].astype(out_ref.dtype)


def place_rows(pieces, seqs, chunks, seq_count, chunk_count, kind):
    width, chunk = pieces[0].shape
    return pl.pallas_call(
        place_kernel,
        out_shape=jax.ShapeDtypeStruct((seq_count, width, chunk_count * chunk), kind),
        grid_spec=pltpu.PrefetchScalarGridSpec(
            num_scalar_prefetch=2,
            grid=(len(pieces),),
            in_specs=[pl.BlockSpec((width, chunk), lambda i, s, c: (0, 0))] * len(pieces),
            out_specs=pl.BlockSpec((1, width, chunk), lambda i, s, c: (s[i], 0, c[i])),
        ),
        compiler_params=pltpu.CompilerParams(vmem_limit_bytes=32 * 2**20),
        name="place_rows",
    )(seqs, chunks, *pieces)


def shards(tokens, gains, qkv_weight, out_weight, gate_weight, up_weight, down_weight, cotangent):
    seq_count, span_len, width = tokens.shape
    ctx_count, sub_count = lax.axis_size("ctx"), lax.axis_size("sub")
    pair_count = ctx_count * sub_count
    chunk = span_len // (2 * sub_count)
    row_count = 2 * chunk
    owners = lax.axis_size(("shard", "ctx"))
    tensor_count = lax.axis_size(("seq", "sub"))
    everyone = ("seq", "sub", "shard", "ctx")
    own_seq, own_sub, own_ctx = lax.axis_index("seq"), lax.axis_index("sub"), lax.axis_index("ctx")
    is_low = own_ctx < ctx_count // 2
    own_pair = jnp.where(
        is_low,
        2 * sub_count * own_ctx + own_sub,
        2 * pair_count - 1 - 2 * sub_count * own_ctx - own_sub,
    ).astype(jnp.int32)

    def take_rows(values):
        span = lax.dynamic_index_in_dim(values, own_seq, 0, keepdims=False)
        kept = lax.dynamic_slice_in_dim(span, own_sub * chunk, chunk, 0)
        moved = lax.dynamic_slice_in_dim(span, (2 * sub_count - 1 - own_sub) * chunk, chunk, 0)
        return kept, moved

    def in_order(kept, moved):
        return jnp.where(is_low, jnp.concatenate([kept, moved]), jnp.concatenate([moved, kept]))

    def owner_sums(grad, cols, base):
        count = grad.shape[1] // cols
        grad = jnp.transpose(grad.reshape(grad.shape[0], count, cols), (1, 0, 2))
        grad = grad.reshape(count // ctx_count, ctx_count, -1, cols)
        return reduce_blocks(grad, "shard", 0) if base is None else reduce_to(grad, "shard", base)

    def exchange(home):
        far = [spread(rows, "seq") for rows in home]
        return [part for rows in far for seq_rows in rows for part in spread(seq_rows, "sub")]

    def deliver(pieces, kind):
        seqs, chunks = [], []
        for moved in range(2):
            for seq_ahead in range(seq_count):
                for sub_ahead in range(sub_count):
                    sub = (own_sub + sub_ahead) % sub_count
                    seqs.append((own_seq + seq_ahead) % seq_count)
                    chunks.append(2 * sub_count - 1 - sub if moved else sub)
        placed = place_rows(
            pieces,
            jnp.stack(seqs).astype(jnp.int32),
            jnp.stack(chunks).astype(jnp.int32),
            seq_count,
            2 * sub_count,
            kind,
        )
        return jnp.transpose(placed, (0, 2, 1))

    def to_send(columns):
        low, high = columns[:, :chunk], columns[:, chunk:]
        return jnp.where(is_low, low, high), jnp.where(is_low, high, low)

    tile_rows, tile_cols = qkv_weight.shape
    gain_part = gains.shape[1]
    first_tile = jnp.concatenate(
        [qkv_weight, jnp.pad(gains, ((0, 0), (0, tile_cols - gain_part)))], axis=0
    )
    first_all = lax.all_gather(first_tile, everyone, axis=0, tiled=False)
    qkv_cols = owners * tile_cols
    padded_cols = -(-qkv_cols // LANES) * LANES
    qkv_all = assemble(first_all, tensor_count, tile_rows, padded_cols)
    gain_all = (
        jnp.transpose(first_all[:owners, tile_rows:, :gain_part], (1, 0, 2))
        .reshape(2, 1, width)
        .astype(jnp.float32)
    )
    gain_one, gain_two = gain_all[0], gain_all[1]
    out_rows, out_cols = out_weight.shape
    out_tiles = gather(gather(gather(gather(out_weight, "ctx"), "shard"), "seq"), "sub")
    out_heads = jnp.pad(
        jnp.transpose(out_tiles, (1, 0, 4, 2, 3, 5)).reshape(HEADS, HEAD_DIM, width),
        ((0, 0), (HEAD_DIM, 0), (0, 0)),
    )

    qkv_all, out_heads = lax.optimization_barrier((qkv_all, out_heads))

    kept_tokens, moved_tokens = take_rows(tokens)
    kept_cot, moved_cot = take_rows(cotangent)
    rows_low = in_order(kept_tokens, swap_ends(moved_tokens))
    cot = in_order(kept_cot, swap_ends(moved_cot.astype(jnp.bfloat16)).astype(jnp.float32))
    qkv_all, cot = lax.optimization_barrier((qkv_all, cot))
    wide = -(-width // LANES) * LANES
    far_cots = spread(jnp.pad(cot.astype(jnp.bfloat16), ((0, 0), (0, wide - width))), "seq")
    step = jnp.arange(chunk, dtype=jnp.int32)
    positions = jnp.concatenate([own_pair * chunk + step, (2 * pair_count - 1 - own_pair) * chunk + step])
    half_dim = HEAD_DIM // 2
    frequency = rope_base ** (-2.0 * jnp.arange(half_dim, dtype=jnp.float32) / HEAD_DIM)
    angles = positions.astype(jnp.float32)[:, None] * frequency[None, :]
    cosine, sine = jnp.cos(angles), jnp.sin(angles)
    cosine_table = jnp.concatenate([cosine] * 4, axis=1)
    sine_table = jnp.concatenate([-sine, sine] * 2, axis=1)

    def shape(*dims, kind=jnp.bfloat16):
        return jax.ShapeDtypeStruct(dims, kind)

    head_rows = (KV_HEADS, 2, GROUP, chunk, LANES)
    qkv_flops = 2 * row_count * width * padded_cols
    query_heads, pair_own, normed = row_call(
        project_kernel,
        chunk,
        [(rows_low, 0), (gain_one, 1), (qkv_all, 1), (cosine_table, 0), (sine_table, 0)],
        [(shape(*head_rows), 0), (shape(KV_HEADS, row_count, LANES), 0), (shape(row_count, width), 0)],
        "project",
        qkv_flops,
    )
    query_heads = query_heads.reshape(KV_HEADS, GROUP * row_count, LANES)
    pair_all = lax.all_gather(pair_own, ("ctx", "sub"), axis=1, tiled=True)
    ffn_tile = jnp.concatenate([gate_weight, up_weight, down_weight.T], axis=1)
    pair_all, far_cots, ffn_tile = lax.optimization_barrier((pair_all, far_cots, ffn_tile))
    ffn_all = lax.all_gather(ffn_tile, ("shard", "ctx"), axis=0, tiled=True)
    hidden_part = gate_weight.shape[1]
    place = own_pair[None]
    attended = attention_forward(place, query_heads, pair_all, ctx_count, sub_count, chunk, GROUP)
    attended = [attended.reshape(head_rows)]
    cot_low = [spread(seq_rows, "sub") for seq_rows in far_cots]
    mix_flops = 4 * row_count * width * width
    hidden, normed_own, attn_low = row_call(
        functools.partial(mix_kernel, len(attended)),
        chunk,
        [(rows, 0) for rows in attended]
        + [(out_heads, 1), (rows_low, 0), (gain_two, 1)],
        [
            (shape(row_count, width, kind=jnp.float32), 0),
            (shape(row_count, wide), 0),
            (shape(row_count, width), 0),
        ],
        "mix",
        mix_flops,
    )
    far_rows = spread(normed_own, "seq")
    feeds, backs, pieces = [], [], []
    for seq_ahead, near_rows in enumerate(far_rows):
        if seq_ahead:
            near_rows, backs[-1] = lax.optimization_barrier((near_rows, backs[-1]))
        near = list(zip(spread(near_rows, "sub"), cot_low[seq_ahead]))
        kinds = [jnp.bfloat16 if sub_ahead else jnp.float32 for sub_ahead in range(sub_count)]
        found = row_call(
            functools.partial(feed_kernel, sub_count),
            chunk,
            [(array, 0) for both in near for array in both] + [(ffn_all, 1)],
            [
                (out, 0)
                for kind in kinds
                for out in (
                    shape(row_count, wide, kind=kind),
                    shape(row_count, wide, kind=kind),
                    shape(row_count, hidden_part),
                    shape(row_count, 2 * hidden_part),
                )
            ],
            "feed",
            8 * sub_count * row_count * width * 2 * hidden_part,
        )
        seq_backs, seq_feeds = found[0::4], found[1::4]
        pieces += [both + tuple(rest) for both, *rest in zip(near, found[2::4], found[3::4])]
        backs.append(collect(seq_backs, "sub"))
        feeds.append(collect(seq_feeds, "sub"))
    backs = backs[0] + collect([backs[0]] + [total(parts) for parts in backs[1:]], "seq")[1:]
    feed_sent = [total(parts).astype(jnp.bfloat16) for parts in feeds[1:]]
    ffn_grad = weight_grads(width, *zip(*pieces))
    backs, ffn_grad = lax.optimization_barrier((backs, ffn_grad))
    ffn_out = lax.psum_scatter(ffn_grad, ("shard", "ctx"), scatter_dimension=0, tiled=True)
    hidden_grad, hidden_low, grad_heads, extra, gain_two_grad = row_call(
        functools.partial(unmix_kernel, len(backs), len(attended)),
        chunk,
        [(part, 0) for part in backs + attended]
        + [(hidden, 0), (cot, 0), (gain_two, 1), (out_heads, 1)],
        [
            (shape(row_count, width, kind=jnp.float32), 0),
            (shape(row_count, width), 0),
            (shape(*head_rows), 0),
            (shape(*head_rows), 0),
            (shape(8, width, kind=jnp.float32), 1),
        ],
        "unmix",
        mix_flops,
    )
    flat = (KV_HEADS, GROUP * row_count, LANES)
    grad_heads, extra = grad_heads.reshape(flat), extra.reshape(flat)
    grad_heads, feed_sent = lax.optimization_barrier((grad_heads, feed_sent))
    feeds = feeds[0] + collect([feeds[0]] + feed_sent, "seq")[1:]
    filled = attention_backward(
        place, query_heads, grad_heads, extra, pair_all, 0, 3, (), ctx_count, sub_count, chunk, GROUP
    )
    filled, feeds = lax.optimization_barrier((filled, feeds))
    (block_low,) = row_call(
        functools.partial(block_kernel, len(feeds)),
        chunk,
        [(part, 0) for part in feeds] + [(hidden, 0)],
        [(shape(width, row_count), 0)],
        "block",
        0,
    )
    block_low, filled = lax.optimization_barrier((block_low, filled))
    block_kept, block_moved = to_send(block_low)
    block_home = [block_kept, swap_ends(block_moved)]
    query_grad, pair_grad = attention_backward(
        place,
        query_heads,
        grad_heads,
        extra,
        pair_all,
        3,
        KV_HEADS,
        filled,
        ctx_count,
        sub_count,
        chunk,
        GROUP,
    )
    block_home, query_grad, pair_grad, hidden_low, ffn_out = lax.optimization_barrier(
        (block_home, query_grad, pair_grad, hidden_low, ffn_out)
    )
    pair_grad = lax.psum_scatter(pair_grad, ("ctx", "sub"), scatter_dimension=1, tiled=True)
    query_grad = query_grad.reshape(head_rows)
    half_cols, extra_rows = qkv_cols // 2, 16
    (proj_early,) = row_call(
        early_kernel,
        chunk,
        [(query_grad, 0), (cosine_table, 0), (sine_table, 0)],
        [(shape(row_count, -(-half_cols // LANES) * LANES), 0)],
        "early",
        0,
    )
    early_grad = jnp.concatenate(
        [
            matmul("rf,re->fe", attn_low, hidden_low).astype(jnp.bfloat16),
            matmul("rd,re->de", normed, proj_early).astype(jnp.bfloat16),
        ],
        axis=1,
    )
    early_grad = early_grad.reshape(seq_count, sub_count, tile_rows, early_grad.shape[1])
    early_grad = reduce_blocks(reduce_blocks(early_grad, "sub", 1), "seq", 0)
    out_sums = owner_sums(early_grad[:, :width], out_cols, None)
    qkv_early = owner_sums(early_grad[:, width : width + half_cols], tile_cols, 0)
    pair_grad, out_sums, qkv_early, block_pieces = lax.optimization_barrier(
        (pair_grad, out_sums, qkv_early, exchange(block_home))
    )
    block_out = deliver(block_pieces, jnp.bfloat16)
    proj_grad, input_low, gain_one_grad = row_call(
        finish_kernel,
        chunk,
        [
            (query_grad, 0),
            (pair_grad, 0),
            (cosine_table, 0),
            (sine_table, 0),
            (qkv_all, 1),
            (rows_low, 0),
            (hidden_grad, 0),
            (gain_one, 1),
        ],
        [
            (shape(row_count, padded_cols), 0),
            (shape(width, row_count), 0),
            (shape(8, width, kind=jnp.float32), 1),
        ],
        "finish",
        qkv_flops,
    )
    input_kept, input_moved = to_send(input_low)
    input_kept, input_moved, proj_grad = lax.optimization_barrier((input_kept, input_moved, proj_grad))
    input_moved, block_out = lax.optimization_barrier((swap_ends(input_moved), block_out))
    input_grad = deliver(exchange([input_kept, input_moved]), jnp.float32)

    late_cols = qkv_cols - half_cols
    qkv_grad = matmul("rd,re->de", normed, proj_grad[:, half_cols:qkv_cols]).astype(jnp.bfloat16)
    gains_grad = jnp.concatenate([gain_one_grad[:1], gain_two_grad[:1]]).astype(jnp.bfloat16)
    gains_rows = jnp.pad(gains_grad, ((0, extra_rows - 2), (0, wide - width)))
    for axis in ("sub", "seq"):
        gains_rows = total(spread(gains_rows, axis)).astype(jnp.bfloat16)
    gains_sum = gains_rows[:2, :width]
    last = qkv_grad.reshape(seq_count, sub_count, tile_rows, late_cols)
    last = reduce_blocks(reduce_blocks(last, "sub", 1), "seq", 0)
    gains_tiles = jnp.transpose(gains_sum.reshape(2, owners, gain_part), (1, 0, 2))
    gains_tiles = reduce_blocks(
        gains_tiles.reshape(owners // ctx_count, ctx_count, 2, gain_part), "shard", 0
    )
    qkv_late = owner_sums(last, tile_cols, owners // ctx_count // 2)
    is_early = lax.axis_index("shard") < owners // ctx_count // 2
    qkv_sums = jnp.where(is_early, qkv_early, qkv_late)
    final = jnp.concatenate(
        [
            jnp.concatenate(
                [out_sums, jnp.pad(gains_tiles, ((0, 0), (0, extra_rows - 2), (0, 0)))], axis=1
            ),
            jnp.pad(qkv_sums, ((0, 0), (0, extra_rows), (0, 0))),
        ],
        axis=2,
    )
    final = reduce_blocks(final, "ctx", 0).astype(jnp.float32)
    gains_out = final[tile_rows : tile_rows + 2, :gain_part]
    out_out, qkv_out = final[:tile_rows, :out_cols], final[:tile_rows, out_cols:]
    ffn_out = ffn_out.astype(jnp.float32)
    return (
        block_out,
        input_grad,
        gains_out,
        qkv_out,
        out_out,
        ffn_out[:, :hidden_part],
        ffn_out[:, hidden_part : 2 * hidden_part],
        ffn_out[:, 2 * hidden_part :].T,
    )


def solution(mesh):
    shard_count, ctx_count, tensor_count = (mesh.shape[axis] for axis in ("shard", "ctx", "tensor"))

    def run(tokens, *rest):
        seq_count = tokens.shape[0] // shard_count
        split = Mesh(
            mesh.devices.reshape(shard_count, ctx_count, seq_count, tensor_count // seq_count),
            ("shard", "ctx", "seq", "sub"),
        )
        rows = P("shard", "ctx", None)
        pool = ("shard", "ctx")
        team = ("seq", "sub")
        weights = (P(None, pool), P(team, pool), P(team, pool), P(pool, team), P(pool, team), P(team, pool))
        return jax.shard_map(
            shards,
            mesh=split,
            in_specs=(rows,) + weights + (rows,),
            out_specs=(rows, rows) + weights,
            check_vma=False,
        )(tokens, *rest)

    return run
```

```python
import functools

import jax
import jax.numpy as jnp
from jax import lax
from jax.experimental import pallas as pl
from jax.experimental.pallas import tpu as pltpu
from jax.sharding import Mesh
from jax.sharding import PartitionSpec as P

HEADS = 15
KV_HEADS = 5
HEAD_DIM = 64
GROUP = 3
LANES = 128
HALF = HEAD_DIM


epsilon = 1e-05
rope_base = 100000.0
masked_score = -1e30


def pair_place(pair, ctx_count, sub):
    turn = pair // (2 * sub)
    spot = pair % (2 * sub)
    low = spot < sub
    return jnp.where(low, turn * sub + spot, (ctx_count - 1 - turn) * sub + 2 * sub - 1 - spot)


def dot_nt(a, b):
    return lax.dot_general(a, b, (((1,), (1,)), ((), ())), preferred_element_type=jnp.float32)


def dot_nn(a, b):
    return lax.dot_general(a, b, (((1,), (0,)), ((), ())), preferred_element_type=jnp.float32)


def dot_tn(a, b):
    return lax.dot_general(a, b, (((0,), (0,)), ((), ())), preferred_element_type=jnp.float32)


def causal(rows, cols, chunk, key_axis):
    shape = (rows, cols)
    query_axis = 1 - key_axis
    query = lax.broadcasted_iota(jnp.int32, shape, query_axis)
    key = lax.broadcasted_iota(jnp.int32, shape, key_axis)
    return key <= lax.rem(query, chunk)


def forward_kernel(ctx_count, sub, chunk, group, pair_ref, q_ref, kv_ref, out_ref, top, total):
    pairs = ctx_count * sub
    own = pair_ref[0]
    part = group * chunk
    lanes = lambda rows: lax.broadcasted_iota(jnp.int32, (rows, LANES), 1)

    def load(place, slot, count):
        return kv_ref[0, pl.ds(pl.multiple_of(place * 2 * chunk + slot * chunk, chunk), count * chunk), :]

    def weighted(powers, kv):
        ones = jnp.where(lanes(kv.shape[0]) < HALF, jnp.ones_like(kv), kv)
        return dot_nn(powers, ones)

    def update(start, rows, kv, first, mask):
        scores = dot_nt(q_ref[0, start : start + rows, :], kv)
        if mask is not None:
            scores = jnp.where(mask, scores, masked_score)
        best = jnp.max(scores, axis=1, keepdims=True)
        spot = slice(start, start + rows)
        if first:
            top[spot, :] = jnp.broadcast_to(best, (rows, LANES))
            powers = jnp.exp(scores - best).astype(jnp.bfloat16)
            total[spot, :] = weighted(powers, kv)
        else:
            old = top[spot, :]
            new = jnp.maximum(old, best)
            powers = jnp.exp(scores - new[:, :1]).astype(jnp.bfloat16)
            total[spot, :] = total[spot, :] * jnp.exp(old - new) + weighted(powers, kv)
            top[spot, :] = new

    place = pair_place(own, ctx_count, sub)
    near = load(place, 0, 1)
    both = load(place, 0, 2)
    near_mask = causal(chunk, chunk, chunk, 1)
    columns = lax.broadcasted_iota(jnp.int32, (chunk, 2 * chunk), 1)
    queries = lax.broadcasted_iota(jnp.int32, (chunk, 2 * chunk), 0)
    both_mask = columns <= queries + chunk
    for head in range(group):
        update(head * chunk, chunk, near, True, near_mask)
        update(part + head * chunk, chunk, both, True, both_mask)

    def sweep(first, last, count, start, heads):
        def load_at(pair):
            return load(pair_place(pair, ctx_count, sub), 0, count)

        def absorb(kv):
            for head in range(heads):
                update(start + head * chunk, chunk, kv, False, None)

        twos = (last - first) // 2

        @pl.loop(0, twos)
        def _(step):
            pair = first + 2 * step
            absorb(jnp.concatenate([load_at(pair), load_at(pair + 1)], axis=0))

        @pl.when(first + 2 * twos < last)
        def _():
            absorb(load_at(last - 1))

    sweep(0, own, 1, 0, 2 * group)
    sweep(own + 1, pairs, 2, part, group)

    for head in range(2 * group):
        spot = slice(head * chunk, (head + 1) * chunk)
        sums = total[spot, :]
        count = sums[:, :1]
        out_ref[0, spot, :] = jnp.where(
            lanes(chunk) < HALF, top[spot, :] + jnp.log(count), sums / count
        )


def attention_forward(own_pair, queries, pairs_all, ctx_count, sub, chunk, group):
    rows = queries.shape[1]
    heads, length, _ = pairs_all.shape
    grid_spec = pltpu.PrefetchScalarGridSpec(
        num_scalar_prefetch=1,
        grid=(heads,),
        in_specs=[
            pl.BlockSpec((1, rows, LANES), lambda h, p: (h, 0, 0)),
            pl.BlockSpec((1, length, LANES), lambda h, p: (h, 0, 0)),
        ],
        out_specs=pl.BlockSpec((1, rows, LANES), lambda h, p: (h, 0, 0)),
        scratch_shapes=[
            pltpu.VMEM((rows, LANES), jnp.float32),
            pltpu.VMEM((rows, LANES), jnp.float32),
        ],
    )
    cost = heads * rows * length // 2
    return pl.pallas_call(
        functools.partial(forward_kernel, ctx_count, sub, chunk, group),
        out_shape=jax.ShapeDtypeStruct((heads, rows, LANES), jnp.float32),
        grid_spec=grid_spec,
        compiler_params=pltpu.CompilerParams(vmem_limit_bytes=48 * 2**20),
        cost_estimate=pl.CostEstimate(
            flops=cost * 4 * HALF, bytes_accessed=heads * LANES * (rows * 6 + length * 2), transcendentals=cost
        ),
        name="attention_forward",
    )(own_pair, queries, pairs_all)


def backward_kernel(
    ctx_count, sub, chunk, group, pair_ref, q_ref, cot_ref, extra_ref, kv_ref, dq_ref, dkv_ref
):
    pairs = ctx_count * sub
    own = pair_ref[0]
    part = group * chunk

    def minus(rows, low, high):
        lane = lax.broadcasted_iota(jnp.int32, (rows, LANES), 1)
        return jnp.where((lane >= low) & (lane < high), -1.0, 0.0).astype(jnp.bfloat16)

    def load(place, slot, count):
        base = pl.multiple_of(place * 2 * chunk + slot * chunk, chunk)
        return kv_ref[0, pl.ds(base, count * chunk), :]

    def step(start, rows, kv, first, mask):
        keys = kv.shape[0]
        key_side = jnp.concatenate([kv, minus(keys, 0, 3)], axis=1)
        value_side = jnp.concatenate([kv, minus(keys, 3, 6)], axis=1)
        pair_sum = None
        for at in range(start, start + rows, chunk):
            spot = slice(at, at + chunk)
            query = q_ref[0, spot, :]
            cot = cot_ref[0, spot, :]
            extra = extra_ref[0, spot, :]
            powers = jnp.exp(dot_nt(key_side, jnp.concatenate([query, extra], axis=1)))
            if mask is not None:
                powers = jnp.where(mask, powers, 0.0)
            slope = dot_nt(value_side, jnp.concatenate([cot, extra], axis=1))
            grads = (powers * slope).astype(jnp.bfloat16)
            powers = powers.astype(jnp.bfloat16)
            term = dot_nn(powers, cot) + dot_nn(grads, query)
            pair_sum = term if pair_sum is None else pair_sum + term
            moved = dot_tn(grads, kv)
            if first:
                dq_ref[0, spot, :] = moved
            else:
                dq_ref[0, spot, :] += moved
        return pair_sum

    def store(place, slot, count, value):
        base = pl.multiple_of(place * 2 * chunk + slot * chunk, chunk)
        dkv_ref[0, pl.ds(base, count * chunk), :] = value.astype(jnp.bfloat16)

    place = pair_place(own, ctx_count, sub)
    near_mask = causal(chunk, chunk, chunk, 0)
    keys = lax.broadcasted_iota(jnp.int32, (2 * chunk, chunk), 0)
    queries = lax.broadcasted_iota(jnp.int32, (2 * chunk, chunk), 1)
    far = step(part, part, load(place, 0, 2), True, keys <= queries + chunk)
    near = step(0, part, load(place, 0, 1), True, near_mask)
    store(place, 0, 1, far[:chunk] + near)
    store(place, 1, 1, far[chunk:])

    def sweep(first, last, count, start, rows):
        twos = (last - first) // 2

        def put(at, value):
            store(at, 0, count, value)
            if count == 1:
                store(at, 1, 1, jnp.zeros((chunk, LANES), jnp.float32))

        @pl.loop(0, twos)
        def _(turn):
            one = pair_place(first + 2 * turn, ctx_count, sub)
            two = pair_place(first + 2 * turn + 1, ctx_count, sub)
            kv = jnp.concatenate([load(one, 0, count), load(two, 0, count)], axis=0)
            sums = step(start, rows, kv, False, None)
            put(one, sums[: count * chunk])
            put(two, sums[count * chunk :])

        @pl.when(first + 2 * twos < last)
        def _():
            at = pair_place(last - 1, ctx_count, sub)
            put(at, step(start, rows, load(at, 0, count), False, None))

    sweep(0, own, 1, 0, 2 * part)
    sweep(own + 1, pairs, 2, part, part)


def attention_backward(
    own_pair, queries, cots, extra, pairs_all, base, stop, filled, ctx_count, sub, chunk, group
):
    total_heads, rows, _ = queries.shape
    heads, length = stop - base, pairs_all.shape[1]
    row_spec = pl.BlockSpec((1, rows, LANES), lambda h, p: (base + h, 0, 0))
    long_spec = pl.BlockSpec((1, length, LANES), lambda h, p: (base + h, 0, 0))
    cost = heads * rows * length // 2
    kernel = functools.partial(backward_kernel, ctx_count, sub, chunk, group)

    def filling(pair_ref, q_ref, cot_ref, extra_ref, kv_ref, old_dq_ref, old_dkv_ref, dq_ref, dkv_ref):
        kernel(pair_ref, q_ref, cot_ref, extra_ref, kv_ref, dq_ref, dkv_ref)

    return pl.pallas_call(
        filling if filled else kernel,
        out_shape=(
            jax.ShapeDtypeStruct((total_heads, rows, LANES), jnp.float32),
            jax.ShapeDtypeStruct((total_heads, length, LANES), jnp.bfloat16),
        ),
        grid_spec=pltpu.PrefetchScalarGridSpec(
            num_scalar_prefetch=1,
            grid=(heads,),
            in_specs=[row_spec, row_spec, row_spec, long_spec]
            + [pl.BlockSpec(memory_space=pl.ANY)] * len(filled),
            out_specs=(row_spec, long_spec),
        ),
        input_output_aliases={5 + at: at for at in range(len(filled))},
        compiler_params=pltpu.CompilerParams(vmem_limit_bytes=48 * 2**20),
        cost_estimate=pl.CostEstimate(
            flops=cost * 10 * HALF, bytes_accessed=heads * LANES * (rows * 10 + length * 4), transcendentals=cost
        ),
        name="attention_backward",
    )(own_pair, queries, cots, extra, pairs_all, *filled)


def three_parts(values):
    high = values.astype(jnp.bfloat16)
    rest = values - high.astype(jnp.float32)
    middle = rest.astype(jnp.bfloat16)
    low = (rest - middle.astype(jnp.float32)).astype(jnp.bfloat16)
    return [high, middle, low]


def lane_index(rows):
    return lax.broadcasted_iota(jnp.int32, (rows, LANES), 1)


def swap_halves(tile):
    lane = lane_index(tile.shape[0])
    quarter = HALF // 2
    return jnp.where(
        lax.rem(lane, HALF) < quarter,
        pltpu.roll(tile, LANES - quarter, 1),
        pltpu.roll(tile, quarter, 1),
    )


def normalise(values):
    inv_rms = lax.rsqrt(jnp.mean(values * values, axis=-1, keepdims=True) + epsilon)
    return values * inv_rms, inv_rms


def norm_back(upstream, values, gain_row):
    unit_rows, inv_rms = normalise(values)
    shaped = upstream * gain_row
    inner_mean = jnp.mean(shaped * unit_rows, axis=-1, keepdims=True)
    return inv_rms * (shaped - unit_rows * inner_mean), upstream * unit_rows


def assemble_kernel(rows, in_ref, out_ref):
    tiles = [in_ref[at, :rows, :] for at in range(in_ref.shape[0])]
    used = len(tiles) * tiles[0].shape[1]
    if used < out_ref.shape[1]:
        tiles.append(jnp.zeros((rows, out_ref.shape[1] - used), tiles[0].dtype))
    out_ref[...] = jnp.concatenate(tiles, axis=1)


def assemble(gathered, teams, rows, cols):
    count = gathered.shape[0] // teams
    return pl.pallas_call(
        functools.partial(assemble_kernel, rows),
        grid=(teams,),
        in_specs=[pl.BlockSpec((count,) + gathered.shape[1:], lambda t: (t, 0, 0))],
        out_specs=pl.BlockSpec((rows, cols), lambda t: (t, 0)),
        out_shape=jax.ShapeDtypeStruct((teams * rows, cols), gathered.dtype),
        compiler_params=pltpu.CompilerParams(vmem_limit_bytes=48 * 2**20),
        name="assemble",
    )(gathered)


def project_kernel(token_ref, gain_ref, weight_ref, cos_ref, sin_ref, q_ref, kv_ref, normed_ref):
    rows = token_ref.shape[0]
    unit_rows, _ = normalise(token_ref[...].astype(jnp.float32))
    normed = (unit_rows * gain_ref[...]).astype(jnp.bfloat16)
    normed_ref[...] = normed
    projected = dot_nn(normed, weight_ref[...])
    cos, sin = cos_ref[...], sin_ref[...]
    low = lane_index(rows) < HALF

    def tile(column):
        return projected[:, column // 2 * LANES : (column // 2 + 1) * LANES]

    def turned(column):
        raw = tile(column)
        out = raw * cos + swap_halves(raw) * sin
        return pltpu.roll(out, HALF, 1) if column % 2 else out

    for head in range(HEADS):
        query = jnp.where(low, turned(head) * HEAD_DIM ** (-0.5), 0.0)
        q_ref[head // GROUP, 0, head % GROUP] = query.astype(jnp.bfloat16)
    for head in range(KV_HEADS):
        key = turned(HEADS + head)
        column = HEADS + KV_HEADS + head
        value = tile(column) if column % 2 else pltpu.roll(tile(column), HALF, 1)
        kv_ref[head] = jnp.where(low, key, value).astype(jnp.bfloat16)


def whole(shape):
    return pl.BlockSpec(shape, lambda c: (0,) * len(shape))


def row_call(kernel, chunk, ins, outs, name, flops):
    def spec(array):
        shape = array.shape
        if len(shape) == 5:
            return pl.BlockSpec((shape[0], 1) + shape[2:], lambda c: (0, c, 0, 0, 0))
        if len(shape) == 3:
            return pl.BlockSpec((shape[0], chunk, shape[2]), lambda c: (0, c, 0))
        if shape[0] != 2 * chunk:
            return pl.BlockSpec((shape[0], chunk), lambda c: (0, c))
        return pl.BlockSpec((chunk, shape[1]), lambda c: (c, 0))

    moved = sum(a.size * a.dtype.itemsize for a, _ in ins) + sum(o.size * o.dtype.itemsize for o, _ in outs)
    return pl.pallas_call(
        kernel,
        grid=(2,),
        in_specs=[whole(a.shape) if fixed else spec(a) for a, fixed in ins],
        out_specs=[whole(o.shape) if fixed else spec(o) for o, fixed in outs],
        out_shape=[o for o, _ in outs],
        compiler_params=pltpu.CompilerParams(vmem_limit_bytes=56 * 2**20),
        cost_estimate=pl.CostEstimate(flops=flops, bytes_accessed=moved, transcendentals=0),
        name=name,
    )(*[a for a, _ in ins])


def pick(refs, head):
    group, at = head // GROUP, 0
    for ref in refs:
        if group < at + ref.shape[0]:
            return ref[group - at, 0, head % GROUP]
        at += ref.shape[0]


def pick_pair(refs, group):
    at = 0
    for ref in refs:
        if group < at + ref.shape[0]:
            return ref[group - at]
        at += ref.shape[0]


def mix_kernel(count, *refs):
    attended_refs = refs[:count]
    weight_ref, token_ref, gain_ref, hidden_ref, normed_ref, attn_ref = refs[count:]
    total = token_ref[...].astype(jnp.float32)
    first = lane_index(token_ref.shape[0]) < HALF
    for head in range(HEADS):
        rows = pick(attended_refs, head)
        low = rows.astype(jnp.bfloat16)
        if head % 2:
            both = jnp.concatenate([low_before, low], axis=1)
            total = total + dot_nn(both, weight_ref[head - 1 : head + 1].reshape(2 * LANES, -1))
        elif head == HEADS - 1:
            total = total + dot_nn(low, weight_ref[head])
        low_before = low
        base = head // 2 * LANES
        if head % 2:
            both = jnp.where(first, pltpu.roll(before, HALF, 1), rows)
            attn_ref[:, base : base + LANES] = both.astype(jnp.bfloat16)
        elif head == HEADS - 1:
            alone = pltpu.roll(rows, HALF, 1)[:, :HALF]
            attn_ref[:, base : base + HALF] = alone.astype(jnp.bfloat16)
        before = rows
    hidden_ref[...] = total
    unit_rows, _ = normalise(total)
    normed_ref[:, : total.shape[1]] = (unit_rows * gain_ref[...]).astype(jnp.bfloat16)


def accumulate(ref, rows):
    summed = jnp.broadcast_to(jnp.sum(rows, axis=0, keepdims=True), ref.shape)

    @pl.when(pl.program_id(0) == 0)
    def _():
        ref[...] = summed

    @pl.when(pl.program_id(0) != 0)
    def _():
        ref[...] += summed


def unmix_kernel(count, parts, *refs):
    ups = refs[:count]
    attended_refs, refs = refs[count : count + parts], refs[count + parts :]
    (hidden_ref, cot_ref, gain_ref, weight_ref, grad_ref, low_ref, heads_ref, extra_ref, gain_grad_ref) = refs
    width = hidden_ref.shape[1]
    upstream = ups[0][:, :width].astype(jnp.float32)
    for ref in ups[1:]:
        upstream = upstream + ref[:, :width].astype(jnp.float32)
    back, gain_rows = norm_back(upstream, hidden_ref[...], gain_ref[...])
    accumulate(gain_grad_ref, gain_rows)
    hidden_grad = cot_ref[...] + back
    grad_ref[...] = hidden_grad
    hidden_low = hidden_grad.astype(jnp.bfloat16)
    low_ref[...] = hidden_low
    lane = lane_index(hidden_low.shape[0])
    for head in range(HEADS):
        spot = (head // GROUP, 0, head % GROUP)
        if head % 2 == 0:
            many = weight_ref[head : head + 2].reshape(-1, weight_ref.shape[2])
            cots_two = dot_nt(hidden_low, many).astype(jnp.bfloat16)
        side = head % 2 * LANES
        cots = cots_two[:, side : side + LANES]
        heads_ref[spot] = cots
        attended = pick(attended_refs, head)
        delta = jnp.sum(cots.astype(jnp.float32) * attended, axis=1, keepdims=True)
        base = jnp.where(lane < 3, attended[:, :1], jnp.where(lane < 6, delta, 0.0))
        high, middle, low = three_parts(base)
        part = lax.rem(lane, 3)
        extra_ref[spot] = jnp.where(
            part == 0,
            high.astype(jnp.float32),
            jnp.where(part == 1, middle.astype(jnp.float32), low.astype(jnp.float32)),
        ).astype(jnp.bfloat16)


def turn_back(dq_ref, dkv_ref, cos_ref, sin_ref, proj_ref):
    rows = cos_ref.shape[0]
    cos, sin = cos_ref[...], sin_ref[...]
    low = lane_index(rows) < HALF

    def half(column):
        if column < HEADS:
            return dq_ref[column // GROUP, 0, column % GROUP] * HEAD_DIM ** (-0.5), 0
        if column < HEADS + KV_HEADS:
            return dkv_ref[column - HEADS].astype(jnp.float32), 0
        if column < HEADS + 2 * KV_HEADS:
            return dkv_ref[column - HEADS - KV_HEADS].astype(jnp.float32), 1
        return jnp.zeros((rows, LANES), jnp.float32), 0

    def placed(column):
        value, side = half(column)
        return value if side == column % 2 else pltpu.roll(value, HALF, 1)

    for at in range(proj_ref.shape[1] // LANES):
        raw = jnp.where(low, placed(2 * at), placed(2 * at + 1))
        if 2 * at < HEADS + KV_HEADS:
            raw = raw * cos - swap_halves(raw) * sin
        proj_ref[:, at * LANES : (at + 1) * LANES] = raw.astype(jnp.bfloat16)


def early_kernel(dq_ref, cos_ref, sin_ref, proj_ref):
    turn_back(dq_ref, None, cos_ref, sin_ref, proj_ref)


def block_kernel(count, *refs):
    hidden_ref, out_ref = refs[count], refs[count + 1]
    rows = hidden_ref[...]
    for ref in refs[:count]:
        rows = rows + ref[:, : rows.shape[1]].astype(jnp.float32)
    out_ref[...] = jnp.transpose(rows).astype(jnp.bfloat16)


def finish_kernel(
    dq_ref, dkv_ref, cos_ref, sin_ref, weight_ref, token_ref, grad_ref, gain_ref,
    proj_ref, input_ref, gain_grad_ref,
):
    turn_back(dq_ref, dkv_ref, cos_ref, sin_ref, proj_ref)
    upstream = dot_nt(proj_ref[...], weight_ref[...])
    back, gain_rows = norm_back(upstream, token_ref[...].astype(jnp.float32), gain_ref[...])
    accumulate(gain_grad_ref, gain_rows)
    input_ref[...] = jnp.transpose(grad_ref[...] + back).astype(jnp.bfloat16)


def feed_kernel(count, *refs):
    weight_ref = refs[2 * count]
    for at in range(count):
        outs = refs[2 * count + 1 + 4 * at : 2 * count + 5 + 4 * at]
        feed_rows(refs[2 * at], refs[2 * at + 1], weight_ref, *outs)


def feed_rows(rows_ref, cot_ref, weight_ref, back_ref, feed_ref, inner_ref, grad_ref):
    part = inner_ref.shape[1]
    width = weight_ref.shape[0]
    rows, cots = rows_ref[:, :width], cot_ref[:, :width]
    gate_up, down = weight_ref[:, : 2 * part], weight_ref[:, 2 * part :]
    both = dot_nn(rows, gate_up)
    inner_grad = dot_nn(cots, down)
    gate_value, up_value = both[:, :part], both[:, part:]
    gate_sigmoid = jax.nn.sigmoid(gate_value)
    swish = gate_value * gate_sigmoid
    inner = (swish * up_value).astype(jnp.bfloat16)
    inner_ref[...] = inner
    gate_grad = inner_grad * up_value * (gate_sigmoid * (1.0 + gate_value * (1.0 - gate_sigmoid)))
    grad_ref[:, :part] = gate_grad.astype(jnp.bfloat16)
    grad_ref[:, part:] = (inner_grad * swish).astype(jnp.bfloat16)
    back_ref[:, :width] = dot_nt(grad_ref[...], gate_up).astype(back_ref.dtype)
    feed_ref[:, :width] = dot_nt(inner, down).astype(feed_ref.dtype)


def weight_grad_kernel(count, *refs):
    rows, cots = refs[:count], refs[count : 2 * count]
    inners, grads = refs[2 * count : 3 * count], refs[3 * count : 4 * count]
    out_ref = refs[4 * count]
    width = out_ref.shape[0]
    step = pl.program_id(0)

    @pl.when(step < 2)
    def _():
        out_ref[...] = sum(dot_tn(a[:, :width], b[...]) for a, b in zip(rows, grads)).astype(jnp.bfloat16)

    @pl.when(step == 2)
    def _():
        out_ref[...] = sum(dot_tn(a[:, :width], b[...]) for a, b in zip(cots, inners)).astype(jnp.bfloat16)


def weight_grads(width, rows, cots, inners, grads):
    count, size, part = len(rows), rows[0].shape[0], inners[0].shape[1]
    once = [pl.BlockSpec((size, rows[0].shape[1]), lambda j: (0, 0))] * (2 * count)
    once += [pl.BlockSpec((size, part), lambda j: (0, 0))] * count
    turns = [pl.BlockSpec((size, part), lambda j: (0, jnp.minimum(j, 1)))] * count
    return pl.pallas_call(
        functools.partial(weight_grad_kernel, count),
        grid=(3,),
        in_specs=once + turns,
        out_specs=pl.BlockSpec((width, part), lambda j: (0, j)),
        out_shape=jax.ShapeDtypeStruct((width, 3 * part), jnp.bfloat16),
        compiler_params=pltpu.CompilerParams(vmem_limit_bytes=56 * 2**20),
        cost_estimate=pl.CostEstimate(
            flops=6 * count * size * width * part,
            bytes_accessed=count * size * (4 * width + 6 * part) + 6 * width * part,
            transcendentals=0,
        ),
        name="weight_grads",
    )(*rows, *cots, *inners, *grads)


def matmul(spec, left, right):
    return jnp.einsum(spec, left, right, preferred_element_type=jnp.float32)


def pull(values, axis, ahead):
    count = lax.axis_size(axis)
    return lax.ppermute(values, axis, [((i + ahead) % count, i) for i in range(count)])


def swap_ends(values):
    count = lax.axis_size("ctx")
    return lax.ppermute(values, "ctx", [(i, count - 1 - i) for i in range(count)])


def spread(values, axis):
    return [values] + [pull(values, axis, ahead) for ahead in range(1, lax.axis_size(axis))]


def gather(values, axis):
    count = lax.axis_size(axis)
    ahead = jnp.stack(spread(values, axis))
    return lax.dynamic_slice_in_dim(
        jnp.concatenate([ahead, ahead]), count - lax.axis_index(axis), count, 0
    )


def collect(parts, axis):
    received = [parts[0]]
    for ahead in range(1, len(parts)):
        received.append(pull(parts[ahead].astype(jnp.bfloat16), axis, len(parts) - ahead))
    return received


def total(parts):
    return sum(part.astype(jnp.float32) for part in parts)


def reduce_blocks(values, axis, dim):
    count = lax.axis_size(axis)
    at = lax.axis_index(axis)
    blocks = [
        lax.dynamic_index_in_dim(values, (at + ahead) % count, dim, keepdims=False)
        for ahead in range(count)
    ]
    return total(collect(blocks, axis)).astype(jnp.bfloat16)


def reduce_to(values, axis, base):
    count, at = lax.axis_size(axis), lax.axis_index(axis)
    size = values.shape[0]
    summed = 0.0
    for ahead in range(count):
        target = jnp.clip((at + ahead) % count - base, 0, size - 1)
        block = lax.dynamic_index_in_dim(values, target, 0, keepdims=False)
        if ahead:
            ways = [(i, (i + ahead) % count) for i in range(count)]
            block = lax.ppermute(block, axis, [w for w in ways if base <= w[1] < base + size])
        summed = summed + block.astype(jnp.float32)
    return summed.astype(jnp.bfloat16)


def place_kernel(seq_ref, chunk_ref, *refs):
    out_ref = refs[-1]
    for at, ref in enumerate(refs[:-1]):

        @pl.when(pl.program_id(0) == at)
        def _(ref=ref):
            out_ref[0] = ref[...].astype(out_ref.dtype)


def place_rows(pieces, seqs, chunks, seq_count, chunk_count, kind):
    width, chunk = pieces[0].shape
    return pl.pallas_call(
        place_kernel,
        out_shape=jax.ShapeDtypeStruct((seq_count, width, chunk_count * chunk), kind),
        grid_spec=pltpu.PrefetchScalarGridSpec(
            num_scalar_prefetch=2,
            grid=(len(pieces),),
            in_specs=[pl.BlockSpec((width, chunk), lambda i, s, c: (0, 0))] * len(pieces),
            out_specs=pl.BlockSpec((1, width, chunk), lambda i, s, c: (s[i], 0, c[i])),
        ),
        compiler_params=pltpu.CompilerParams(vmem_limit_bytes=32 * 2**20),
        name="place_rows",
    )(seqs, chunks, *pieces)


def shards(tokens, gains, qkv_weight, out_weight, gate_weight, up_weight, down_weight, cotangent):
    seq_count, span_len, width = tokens.shape
    ctx_count, sub_count = lax.axis_size("ctx"), lax.axis_size("sub")
    pair_count = ctx_count * sub_count
    chunk = span_len // (2 * sub_count)
    row_count = 2 * chunk
    owners = lax.axis_size(("shard", "ctx"))
    tensor_count = lax.axis_size(("seq", "sub"))
    everyone = ("seq", "sub", "shard", "ctx")
    own_seq, own_sub, own_ctx = lax.axis_index("seq"), lax.axis_index("sub"), lax.axis_index("ctx")
    is_low = own_ctx < ctx_count // 2
    own_pair = jnp.where(
        is_low,
        2 * sub_count * own_ctx + own_sub,
        2 * pair_count - 1 - 2 * sub_count * own_ctx - own_sub,
    ).astype(jnp.int32)

    def take_rows(values):
        span = lax.dynamic_index_in_dim(values, own_seq, 0, keepdims=False)
        kept = lax.dynamic_slice_in_dim(span, own_sub * chunk, chunk, 0)
        moved = lax.dynamic_slice_in_dim(span, (2 * sub_count - 1 - own_sub) * chunk, chunk, 0)
        return kept, moved

    def in_order(kept, moved):
        return jnp.where(is_low, jnp.concatenate([kept, moved]), jnp.concatenate([moved, kept]))

    def owner_sums(grad, cols, base):
        count = grad.shape[1] // cols
        grad = jnp.transpose(grad.reshape(grad.shape[0], count, cols), (1, 0, 2))
        grad = grad.reshape(count // ctx_count, ctx_count, -1, cols)
        return reduce_blocks(grad, "shard", 0) if base is None else reduce_to(grad, "shard", base)

    def exchange(home):
        far = [spread(rows, "seq") for rows in home]
        return [part for rows in far for seq_rows in rows for part in spread(seq_rows, "sub")]

    def deliver(pieces, kind):
        seqs, chunks = [], []
        for moved in range(2):
            for seq_ahead in range(seq_count):
                for sub_ahead in range(sub_count):
                    sub = (own_sub + sub_ahead) % sub_count
                    seqs.append((own_seq + seq_ahead) % seq_count)
                    chunks.append(2 * sub_count - 1 - sub if moved else sub)
        placed = place_rows(
            pieces,
            jnp.stack(seqs).astype(jnp.int32),
            jnp.stack(chunks).astype(jnp.int32),
            seq_count,
            2 * sub_count,
            kind,
        )
        return jnp.transpose(placed, (0, 2, 1))

    def to_send(columns):
        low, high = columns[:, :chunk], columns[:, chunk:]
        return jnp.where(is_low, low, high), jnp.where(is_low, high, low)

    tile_rows, tile_cols = qkv_weight.shape
    gain_part = gains.shape[1]
    first_tile = jnp.concatenate(
        [qkv_weight, jnp.pad(gains, ((0, 0), (0, tile_cols - gain_part)))], axis=0
    )
    first_all = lax.all_gather(first_tile, everyone, axis=0, tiled=False)
    qkv_cols = owners * tile_cols
    padded_cols = -(-qkv_cols // LANES) * LANES
    qkv_all = assemble(first_all, tensor_count, tile_rows, padded_cols)
    gain_all = (
        jnp.transpose(first_all[:owners, tile_rows:, :gain_part], (1, 0, 2))
        .reshape(2, 1, width)
        .astype(jnp.float32)
    )
    gain_one, gain_two = gain_all[0], gain_all[1]
    out_rows, out_cols = out_weight.shape
    out_tiles = gather(gather(gather(gather(out_weight, "ctx"), "shard"), "seq"), "sub")
    out_heads = jnp.pad(
        jnp.transpose(out_tiles, (1, 0, 4, 2, 3, 5)).reshape(HEADS, HEAD_DIM, width),
        ((0, 0), (HEAD_DIM, 0), (0, 0)),
    )

    qkv_all, out_heads = lax.optimization_barrier((qkv_all, out_heads))

    kept_tokens, moved_tokens = take_rows(tokens)
    kept_cot, moved_cot = take_rows(cotangent)
    rows_low = in_order(kept_tokens, swap_ends(moved_tokens))
    cot = in_order(kept_cot, swap_ends(moved_cot.astype(jnp.bfloat16)).astype(jnp.float32))
    qkv_all, cot = lax.optimization_barrier((qkv_all, cot))
    wide = -(-width // LANES) * LANES
    far_cots = spread(jnp.pad(cot.astype(jnp.bfloat16), ((0, 0), (0, wide - width))), "seq")
    step = jnp.arange(chunk, dtype=jnp.int32)
    positions = jnp.concatenate([own_pair * chunk + step, (2 * pair_count - 1 - own_pair) * chunk + step])
    half_dim = HEAD_DIM // 2
    frequency = rope_base ** (-2.0 * jnp.arange(half_dim, dtype=jnp.float32) / HEAD_DIM)
    angles = positions.astype(jnp.float32)[:, None] * frequency[None, :]
    cosine, sine = jnp.cos(angles), jnp.sin(angles)
    cosine_table = jnp.concatenate([cosine] * 4, axis=1)
    sine_table = jnp.concatenate([-sine, sine] * 2, axis=1)

    def shape(*dims, kind=jnp.bfloat16):
        return jax.ShapeDtypeStruct(dims, kind)

    head_rows = (KV_HEADS, 2, GROUP, chunk, LANES)
    qkv_flops = 2 * row_count * width * padded_cols
    query_heads, pair_own, normed = row_call(
        project_kernel,
        chunk,
        [(rows_low, 0), (gain_one, 1), (qkv_all, 1), (cosine_table, 0), (sine_table, 0)],
        [(shape(*head_rows), 0), (shape(KV_HEADS, row_count, LANES), 0), (shape(row_count, width), 0)],
        "project",
        qkv_flops,
    )
    query_heads = query_heads.reshape(KV_HEADS, GROUP * row_count, LANES)
    pair_all = lax.all_gather(pair_own, ("ctx", "sub"), axis=1, tiled=True)
    ffn_tile = jnp.concatenate([gate_weight, up_weight, down_weight.T], axis=1)
    pair_all, far_cots, ffn_tile = lax.optimization_barrier((pair_all, far_cots, ffn_tile))
    ffn_all = lax.all_gather(ffn_tile, ("shard", "ctx"), axis=0, tiled=True)
    hidden_part = gate_weight.shape[1]
    place = own_pair[None]
    attended = attention_forward(place, query_heads, pair_all, ctx_count, sub_count, chunk, GROUP)
    attended = [attended.reshape(head_rows)]
    cot_low = [spread(seq_rows, "sub") for seq_rows in far_cots]
    mix_flops = 4 * row_count * width * width
    hidden, normed_own, attn_low = row_call(
        functools.partial(mix_kernel, len(attended)),
        chunk,
        [(rows, 0) for rows in attended]
        + [(out_heads, 1), (rows_low, 0), (gain_two, 1)],
        [
            (shape(row_count, width, kind=jnp.float32), 0),
            (shape(row_count, wide), 0),
            (shape(row_count, width), 0),
        ],
        "mix",
        mix_flops,
    )
    far_rows = spread(normed_own, "seq")
    feeds, backs, pieces = [], [], []
    for seq_ahead, near_rows in enumerate(far_rows):
        if seq_ahead:
            near_rows, backs[-1] = lax.optimization_barrier((near_rows, backs[-1]))
        near = list(zip(spread(near_rows, "sub"), cot_low[seq_ahead]))
        kinds = [jnp.bfloat16 if sub_ahead else jnp.float32 for sub_ahead in range(sub_count)]
        found = row_call(
            functools.partial(feed_kernel, sub_count),
            chunk,
            [(array, 0) for both in near for array in both] + [(ffn_all, 1)],
            [
                (out, 0)
                for kind in kinds
                for out in (
                    shape(row_count, wide, kind=kind),
                    shape(row_count, wide, kind=kind),
                    shape(row_count, hidden_part),
                    shape(row_count, 2 * hidden_part),
                )
            ],
            "feed",
            8 * sub_count * row_count * width * 2 * hidden_part,
        )
        seq_backs, seq_feeds = found[0::4], found[1::4]
        pieces += [both + tuple(rest) for both, *rest in zip(near, found[2::4], found[3::4])]
        backs.append(collect(seq_backs, "sub"))
        feeds.append(collect(seq_feeds, "sub"))
    backs = backs[0] + collect([backs[0]] + [total(parts) for parts in backs[1:]], "seq")[1:]
    feed_sent = [total(parts).astype(jnp.bfloat16) for parts in feeds[1:]]
    ffn_grad = weight_grads(width, *zip(*pieces))
    backs, ffn_grad = lax.optimization_barrier((backs, ffn_grad))
    ffn_out = lax.psum_scatter(ffn_grad, ("shard", "ctx"), scatter_dimension=0, tiled=True)
    hidden_grad, hidden_low, grad_heads, extra, gain_two_grad = row_call(
        functools.partial(unmix_kernel, len(backs), len(attended)),
        chunk,
        [(part, 0) for part in backs + attended]
        + [(hidden, 0), (cot, 0), (gain_two, 1), (out_heads, 1)],
        [
            (shape(row_count, width, kind=jnp.float32), 0),
            (shape(row_count, width), 0),
            (shape(*head_rows), 0),
            (shape(*head_rows), 0),
            (shape(8, width, kind=jnp.float32), 1),
        ],
        "unmix",
        mix_flops,
    )
    flat = (KV_HEADS, GROUP * row_count, LANES)
    grad_heads, extra = grad_heads.reshape(flat), extra.reshape(flat)
    grad_heads, feed_sent = lax.optimization_barrier((grad_heads, feed_sent))
    feeds = feeds[0] + collect([feeds[0]] + feed_sent, "seq")[1:]
    filled = attention_backward(
        place, query_heads, grad_heads, extra, pair_all, 0, 3, (), ctx_count, sub_count, chunk, GROUP
    )
    filled, feeds = lax.optimization_barrier((filled, feeds))
    (block_low,) = row_call(
        functools.partial(block_kernel, len(feeds)),
        chunk,
        [(part, 0) for part in feeds] + [(hidden, 0)],
        [(shape(width, row_count), 0)],
        "block",
        0,
    )
    block_low, filled = lax.optimization_barrier((block_low, filled))
    block_kept, block_moved = to_send(block_low)
    block_home = [block_kept, swap_ends(block_moved)]
    query_grad, pair_grad = attention_backward(
        place,
        query_heads,
        grad_heads,
        extra,
        pair_all,
        3,
        KV_HEADS,
        filled,
        ctx_count,
        sub_count,
        chunk,
        GROUP,
    )
    block_home, query_grad, pair_grad, hidden_low, ffn_out = lax.optimization_barrier(
        (block_home, query_grad, pair_grad, hidden_low, ffn_out)
    )
    pair_grad = lax.psum_scatter(pair_grad, ("ctx", "sub"), scatter_dimension=1, tiled=True)
    query_grad = query_grad.reshape(head_rows)
    half_cols, extra_rows = qkv_cols // 2, 16
    (proj_early,) = row_call(
        early_kernel,
        chunk,
        [(query_grad, 0), (cosine_table, 0), (sine_table, 0)],
        [(shape(row_count, -(-half_cols // LANES) * LANES), 0)],
        "early",
        0,
    )
    early_grad = jnp.concatenate(
        [
            matmul("rf,re->fe", attn_low, hidden_low).astype(jnp.bfloat16),
            matmul("rd,re->de", normed, proj_early).astype(jnp.bfloat16),
        ],
        axis=1,
    )
    early_grad = early_grad.reshape(seq_count, sub_count, tile_rows, early_grad.shape[1])
    early_grad = reduce_blocks(reduce_blocks(early_grad, "sub", 1), "seq", 0)
    out_sums = owner_sums(early_grad[:, :width], out_cols, None)
    qkv_early = owner_sums(early_grad[:, width : width + half_cols], tile_cols, 0)
    pair_grad, out_sums, qkv_early, block_pieces = lax.optimization_barrier(
        (pair_grad, out_sums, qkv_early, exchange(block_home))
    )
    block_out = deliver(block_pieces, jnp.bfloat16)
    proj_grad, input_low, gain_one_grad = row_call(
        finish_kernel,
        chunk,
        [
            (query_grad, 0),
            (pair_grad, 0),
            (cosine_table, 0),
            (sine_table, 0),
            (qkv_all, 1),
            (rows_low, 0),
            (hidden_grad, 0),
            (gain_one, 1),
        ],
        [
            (shape(row_count, padded_cols), 0),
            (shape(width, row_count), 0),
            (shape(8, width, kind=jnp.float32), 1),
        ],
        "finish",
        qkv_flops,
    )
    input_kept, input_moved = to_send(input_low)
    input_kept, input_moved, proj_grad = lax.optimization_barrier((input_kept, input_moved, proj_grad))
    input_moved, block_out = lax.optimization_barrier((swap_ends(input_moved), block_out))
    input_grad = deliver(exchange([input_kept, input_moved]), jnp.float32)

    late_cols = qkv_cols - half_cols
    qkv_grad = matmul("rd,re->de", normed, proj_grad[:, half_cols:qkv_cols]).astype(jnp.bfloat16)
    gains_grad = jnp.concatenate([gain_one_grad[:1], gain_two_grad[:1]]).astype(jnp.bfloat16)
    gains_rows = jnp.pad(gains_grad, ((0, extra_rows - 2), (0, wide - width)))
    for axis in ("sub", "seq"):
        gains_rows = total(spread(gains_rows, axis)).astype(jnp.bfloat16)
    gains_sum = gains_rows[:2, :width]
    last = qkv_grad.reshape(seq_count, sub_count, tile_rows, late_cols)
    last = reduce_blocks(reduce_blocks(last, "sub", 1), "seq", 0)
    gains_tiles = jnp.transpose(gains_sum.reshape(2, owners, gain_part), (1, 0, 2))
    gains_tiles = reduce_blocks(
        gains_tiles.reshape(owners // ctx_count, ctx_count, 2, gain_part), "shard", 0
    )
    qkv_late = owner_sums(last, tile_cols, owners // ctx_count // 2)
    is_early = lax.axis_index("shard") < owners // ctx_count // 2
    qkv_sums = jnp.where(is_early, qkv_early, qkv_late)
    final = jnp.concatenate(
        [
            jnp.concatenate(
                [out_sums, jnp.pad(gains_tiles, ((0, 0), (0, extra_rows - 2), (0, 0)))], axis=1
            ),
            jnp.pad(qkv_sums, ((0, 0), (0, extra_rows), (0, 0))),
        ],
        axis=2,
    )
    final = reduce_blocks(final, "ctx", 0).astype(jnp.float32)
    gains_out = final[tile_rows : tile_rows + 2, :gain_part]
    out_out, qkv_out = final[:tile_rows, :out_cols], final[:tile_rows, out_cols:]
    ffn_out = ffn_out.astype(jnp.float32)
    return (
        block_out,
        input_grad,
        gains_out,
        qkv_out,
        out_out,
        ffn_out[:, :hidden_part],
        ffn_out[:, hidden_part : 2 * hidden_part],
        ffn_out[:, 2 * hidden_part :].T,
    )


def solution(mesh):
    shard_count, ctx_count, tensor_count = (mesh.shape[axis] for axis in ("shard", "ctx", "tensor"))

    def run(tokens, *rest):
        seq_count = tokens.shape[0] // shard_count
        split = Mesh(
            mesh.devices.reshape(shard_count, ctx_count, seq_count, tensor_count // seq_count),
            ("shard", "ctx", "seq", "sub"),
        )
        rows = P("shard", "ctx", None)
        pool = ("shard", "ctx")
        team = ("seq", "sub")
        weights = (P(None, pool), P(team, pool), P(team, pool), P(pool, team), P(pool, team), P(team, pool))
        return jax.shard_map(
            shards,
            mesh=split,
            in_specs=(rows,) + weights + (rows,),
            out_specs=(rows, rows) + weights,
            check_vma=False,
        )(tokens, *rest)

    return run
```
